32 devices in a mesh: grp: 2 (over x), layer: 8 (over z, y), ex: 2 (over core).
Axes of the slice: x: 2, y: 2, z: 4, core: 2. Of those that a mesh axis runs over, the one named last changes fastest.
Arguments:
- store: bfloat16 [8, 4096, 4096], P('layer', ('grp', 'ex')), parts along dimension 1, may hold values from -0.03125 to 0.03125
- queries: bfloat16 [8, 1024, 4096], P('layer', ('grp', 'ex')), parts along dimension 1, may hold values from -6 to 6
- left_inv: bfloat16 [8, 32, 32], P('layer')
- right_inv: bfloat16 [8, 128, 128], P('layer')
- query_prompt: int32 [1024], P('grp'), parts along dimension 0, may hold values from 0 to 127, as said below
- winner: int32 [256], P('grp'), parts along dimension 0, may hold values from 0 to 511, as said below
Outputs:
- scores: bfloat16 [512, 4096], P(None, ('grp', 'ex')), parts along dimension 1
- advantage: bfloat16 [128, 4096], P(None, ('grp', 'ex')), parts along dimension 1
The draws below stay inside these ranges and needn't reach their ends.
There are 2 independent parts, one for each index of `grp`. The reference program is written for one: setup_inputs(seed, part) draws one part's arguments, and reference() takes and returns one part's arrays. A program takes and returns all parts, laid end to end along the dimension named above; an argument that names none is the same for every part. Nothing has to cross between parts.
Inputs may be any that keep to these rules, and one draw needn't show every extreme that they name: `query_prompt`: each prompt id appears for exactly 4 responses. winner[p] is a response whose query_prompt is p.
All inputs are finite; a program needn't handle non-finite values.
Results may differ from the reference program's by a relative error of at most 0.0067.
Values may be sent and summed in bfloat16 or wider, within the bound.
No kernel may reach another device: no remote copies, remote signals or barrier semaphores. Data moves between devices by JAX's collectives and lax.ppermute only.
A program may use at most 64 MiB of HBM per device.

```python
import jax
import jax.numpy as jnp
from jax import lax

KIN = 32
KOUT = 128
BEST = 4
NPR = 128
PDIM = 4096
NQ = 512
LAYERS = 8
EXAMPLES = 2048


def factor_inverse(key, width):
    noise = jax.random.normal(key, (LAYERS, width, width), jnp.float32)
    spread = 0.3 * (noise + jnp.swapaxes(noise, 1, 2)) / (2.0 * width) ** 0.5
    logs = jax.random.uniform(jax.random.fold_in(key, 5), (LAYERS, width, 1), jnp.float32, -0.693, 0.693)
    return spread + jnp.eye(width, dtype=jnp.float32)[None, :, :] * jnp.exp(logs)


def draw_left_inv(key, part):
    key = jax.random.fold_in(key, 1)
    return factor_inverse(key, KIN).astype(jnp.bfloat16)


def draw_right_inv(key, part):
    key = jax.random.fold_in(key, 2)
    return factor_inverse(key, KOUT).astype(jnp.bfloat16)


def grouping(key):
    ranks = jax.random.permutation(jax.random.fold_in(key, 7), NQ).astype(jnp.int32)
    positions = jnp.arange(NQ, dtype=jnp.int32)
    clash = ranks[0] // BEST == ranks[NQ - 1] // BEST
    other_rank = (ranks[0] + BEST) % NQ
    other_pos = jnp.sum(jnp.where(ranks == other_rank, positions, 0)).astype(jnp.int32)
    last_rank = ranks[NQ - 1]
    swapped = jnp.where(positions == NQ - 1, other_rank, jnp.where(positions == other_pos, last_rank, ranks))
    ranks = jnp.where(clash, swapped, ranks).astype(jnp.int32)
    picked = jax.random.randint(jax.random.fold_in(key, 9), (NPR,), 0, BEST).astype(jnp.int32)
    prompt_all = jnp.arange(NPR, dtype=jnp.int32)
    picked = jnp.where(prompt_all == ranks[0] // BEST, ranks[0] % BEST, picked)
    picked = jnp.where(prompt_all == ranks[NQ - 1] // BEST, ranks[NQ - 1] % BEST, picked).astype(jnp.int32)
    inverse = jnp.argsort(ranks, stable=True).astype(jnp.int32)
    target = prompt_all * BEST + picked
    return (ranks // BEST, inverse[target])


def draw_query_prompt(key, part):
    prompt_ids, chosen = grouping(key)
    return prompt_ids


def draw_winner(key, part):
    prompt_ids, chosen = grouping(key)
    return chosen


def steps_of(rng, shape, shards, smallest, largest):
    gain = 1.0
    for position, parts in shards:
        heights = jax.random.uniform(jax.random.fold_in(jax.random.fold_in(rng, 6), position), (parts,), jnp.float32, smallest / len(shards), largest / len(shards))
        gain = gain * jnp.repeat(jnp.exp(heights), shape[position] // parts).reshape((-1,) + (1,) * (len(shape) - 1 - position))
    return gain


def scatter_about(stream_key, extent, scale, most, cuts=(), held_as=jnp.bfloat16):
    values = scale * jax.random.normal(stream_key, extent, jnp.float32)
    if cuts:
        values = values * steps_of(stream_key, extent, cuts, -0.22, 0.18)
    return jnp.clip(values, -most, most).astype(held_as)


def setup_inputs(seed: int = 0, part: int = 0) -> dict:
    splits = jax.random.split(jax.random.key(seed), 7)
    part_keys = jax.random.split(jax.random.fold_in(splits[6], part), 7)
    store = scatter_about(part_keys[0], (LAYERS, EXAMPLES, PDIM), (LAYERS * PDIM) ** -0.5, 0.03125, ((0, 8), (1, 2)))
    queries = scatter_about(part_keys[1], (LAYERS, NQ, PDIM), 1.0, 6.0, ((0, 8), (1, 2)))
    left_inv = draw_left_inv(jax.random.fold_in(splits[6], 71), part)
    right_inv = draw_right_inv(jax.random.fold_in(splits[6], 71), part)
    query_prompt = draw_query_prompt(jax.random.fold_in(jax.random.fold_in(splits[6], part), 71), part)
    winner = draw_winner(jax.random.fold_in(jax.random.fold_in(splits[6], part), 71), part)
    return {"store": store, "queries": queries, "left_inv": left_inv, "right_inv": right_inv, "query_prompt": query_prompt, "winner": winner}


def layer_term(rows, store_layer, left, right):
    count = rows.shape[0]
    blocks = rows.reshape(count, KIN, KOUT).astype(jnp.float32)
    half = jnp.einsum('qik,km->qim', blocks, right.astype(jnp.float32)).astype(jnp.bfloat16)
    pre = jnp.einsum('ij,qjm->qim', left.astype(jnp.float32), half.astype(jnp.float32)).astype(jnp.bfloat16)
    pre = pre.reshape(count, KIN * KOUT)
    return jnp.dot(pre, store_layer.T, preferred_element_type=jnp.float32)


def reference(store, queries, left_inv, right_inv, query_prompt, winner):
    def step(total, items):
        store_layer, rows, left, right = items
        return total + layer_term(rows, store_layer, left, right), None

    start = jnp.zeros((queries.shape[1], store.shape[1]), jnp.float32)
    total, unused = lax.scan(step, start, (store, queries, left_inv, right_inv))
    scores = total.astype(jnp.bfloat16)
    ids = jnp.arange(queries.shape[1], dtype=jnp.int32)
    prompts = jnp.arange(winner.shape[0], dtype=jnp.int32)
    picks = (winner[:, None] == ids[None, :]).astype(jnp.float32)
    member = (query_prompt[None, :] == prompts[:, None]).astype(jnp.float32)
    weights = picks - member / BEST
    advantage = jnp.dot(weights, scores.astype(jnp.float32), precision=lax.Precision.HIGHEST)
    return scores, advantage.astype(jnp.bfloat16)
```

```python
import jax
import jax.numpy as jnp
from jax import lax
from jax.sharding import PartitionSpec as P

KIN = 32
KOUT = 128
BEST = 4
LANES = 128


def precondition(block, left_inv, right_inv):
    layers = block.shape[0]
    count = block.shape[1]
    blocks = block.reshape(layers, count, KIN, KOUT)
    half = jnp.einsum(
        "lqik,lkm->lqim", blocks, right_inv, preferred_element_type=jnp.float32
    ).astype(jnp.bfloat16)
    pre = jnp.einsum("lij,lqjm->lqim", left_inv, half, preferred_element_type=jnp.float32).astype(
        jnp.bfloat16
    )
    return pre.reshape(layers, count, KIN * KOUT)


def score_block(ready, store):
    return jnp.einsum("lqp,lep->qe", ready, store, preferred_element_type=jnp.float32)


class Grid:
    def __init__(self):
        self.count = lax.axis_size("layer")
        self.y_count = 2 if self.count % 2 == 0 else 1
        self.z_count = self.count // self.y_count
        index = lax.axis_index("layer")
        self.y = index % self.y_count
        self.z = index // self.y_count

    def along_y(self, block):
        route = [(i, i ^ 1) for i in range(self.count)]
        return lax.ppermute(block, "layer", route)

    def along_z(self, block, distance):
        step = distance * self.y_count
        route = [(i, (i + step) % self.count) for i in range(self.count)]
        return lax.ppermute(block, "layer", route)


def z_slots(grid, shape):
    columns = min(grid.z_count, shape[1] // LANES)
    return grid.z_count // columns, columns


def z_slot(grid, block, slot):
    row_blocks, column_blocks = z_slots(grid, block.shape)
    rows, columns = block.shape[0] // row_blocks, block.shape[1] // column_blocks
    return lax.dynamic_slice(
        block, ((slot // column_blocks) * rows, (slot % column_blocks) * columns), (rows, columns)
    )


def scatter_z(grid, block):
    narrow = block.astype(jnp.bfloat16)
    total = z_slot(grid, block, grid.z)
    for d in range(1, grid.z_count):
        sent = z_slot(grid, narrow, (grid.z + d) % grid.z_count)
        total = total + grid.along_z(sent, d).astype(jnp.float32)
    return total


def gather_z(grid, mine, shape):
    row_blocks, column_blocks = z_slots(grid, shape)
    rows, columns = mine.shape
    out = jnp.zeros(shape, mine.dtype)
    for d in range(grid.z_count):
        piece = grid.along_z(mine, d) if d else mine
        slot = (grid.z - d) % grid.z_count
        out = lax.dynamic_update_slice(
            out, piece, ((slot // column_blocks) * rows, (slot % column_blocks) * columns)
        )
    return out


def scatter_y(grid, block):
    if grid.y_count == 1:
        return block
    rows = block.shape[0] // 2
    mine = lax.dynamic_slice_in_dim(block, grid.y * rows, rows, 0)
    sent = lax.dynamic_slice_in_dim(block, (1 - grid.y) * rows, rows, 0).astype(jnp.bfloat16)
    return mine + grid.along_y(sent).astype(jnp.float32)


def gather_y(grid, mine):
    if grid.y_count == 1:
        return mine
    other = grid.along_y(mine)
    first = jnp.where(grid.y == 0, mine, other)
    second = jnp.where(grid.y == 0, other, mine)
    return jnp.concatenate([first, second], 0)


def sum_y_first(grid, block):
    half = scatter_y(grid, block)
    piece = scatter_z(grid, half).astype(jnp.bfloat16)
    return gather_y(grid, gather_z(grid, piece, half.shape))


def sum_z_first(grid, block):
    slot = scatter_z(grid, block)
    piece = scatter_y(grid, slot).astype(jnp.bfloat16)
    return gather_z(grid, gather_y(grid, piece), block.shape)


def shards(store, queries, left_inv, right_inv, query_prompt, winner):
    block_rows = queries.shape[1]
    columns = store.shape[1]
    grid = Grid()
    ex_count = lax.axis_size("ex")
    position = lax.axis_index("ex")
    mine = precondition(queries, left_inv, right_inv)
    scores = jnp.zeros((block_rows * ex_count, columns), jnp.bfloat16)
    current = mine
    for step in range(ex_count):
        if step > 0:
            route = [((i - 1) % ex_count, i) for i in range(ex_count)]
            current = lax.ppermute(current, "ex", route)
        source = (position - step) % ex_count
        tile = score_block(current, store)
        if step == 0:
            first = sum_z_first(grid, tile[:, : columns // 2])
            second = sum_y_first(grid, tile[:, columns // 2 :])
            done = jnp.concatenate([first, second], 1)
        else:
            done = sum_y_first(grid, tile)
        scores = lax.dynamic_update_slice_in_dim(scores, done, source * block_rows, 0)
    ids = jnp.arange(scores.shape[0], dtype=jnp.int32)
    prompts = jnp.arange(winner.shape[0], dtype=jnp.int32)
    picks = (winner[:, None] == ids[None, :]).astype(jnp.float32)
    member = (query_prompt[None, :] == prompts[:, None]).astype(jnp.float32)
    weights = (picks - member / BEST).astype(jnp.bfloat16)
    advantage = jnp.dot(weights, scores, preferred_element_type=jnp.float32)
    return (scores, advantage.astype(jnp.bfloat16))


def solution(mesh):
    return jax.shard_map(
        shards,
        mesh=mesh,
        in_specs=(
            P("layer", ("grp", "ex"), None),
            P("layer", ("grp", "ex"), None),
            P("layer", None, None),
            P("layer", None, None),
            P("grp"),
            P("grp"),
        ),
        out_specs=(P(None, ("grp", "ex")), P(None, ("grp", "ex"))),
        check_vma=False,
    )
```

```python
import jax
import jax.numpy as jnp
from jax import lax
from jax.sharding import PartitionSpec as P

KIN = 32
KOUT = 128
BEST = 4


def passed_along(block, axis, distance):
    devices = range(lax.axis_size(axis))
    route = [((i - distance) % len(devices), i) for i in devices]
    return lax.ppermute(block, axis, route)


def precondition(block, left_inv, right_inv):
    layers = block.shape[0]
    count = block.shape[1]
    blocks = block.reshape(layers, count, KIN, KOUT)
    half = jnp.einsum(
        "lqik,lkm->lqim", blocks, right_inv, preferred_element_type=jnp.float32
    ).astype(jnp.bfloat16)
    pre = jnp.einsum("lij,lqjm->lqim", left_inv, half, preferred_element_type=jnp.float32).astype(
        jnp.bfloat16
    )
    return pre.reshape(layers, count, KIN * KOUT)


def score_block(ready, store):
    return jnp.einsum("lqp,lep->qe", ready, store, preferred_element_type=jnp.float32)


def shards(store, queries, left_inv, right_inv, query_prompt, winner):
    block_rows = queries.shape[1]
    mine = precondition(queries, left_inv, right_inv)
    ex_count = lax.axis_size("ex")
    position = lax.axis_index("ex")
    scores = jnp.zeros((block_rows * ex_count, store.shape[1]), jnp.bfloat16)
    current = mine
    for step in range(ex_count):
        if step > 0:
            current = passed_along(current, "ex", 1)
        source = (position - step) % ex_count
        tile = score_block(current, store)
        done = lax.psum(tile.astype(jnp.bfloat16), "layer")
        scores = lax.dynamic_update_slice_in_dim(scores, done, source * block_rows, 0)
    ids = jnp.arange(scores.shape[0], dtype=jnp.int32)
    prompts = jnp.arange(winner.shape[0], dtype=jnp.int32)
    picks = (winner[:, None] == ids[None, :]).astype(jnp.float32)
    member = (query_prompt[None, :] == prompts[:, None]).astype(jnp.float32)
    weights = (picks - member / BEST).astype(jnp.bfloat16)
    advantage = jnp.dot(weights, scores, preferred_element_type=jnp.float32)
    return (scores, advantage.astype(jnp.bfloat16))


def solution(mesh):
    return jax.shard_map(
        shards,
        mesh=mesh,
        in_specs=(
            P("layer", ("grp", "ex"), None),
            P("layer", ("grp", "ex"), None),
            P("layer", None, None),
            P("layer", None, None),
            P("grp"),
            P("grp"),
        ),
        out_specs=(P(None, ("grp", "ex")), P(None, ("grp", "ex"))),
        check_vma=False,
    )
```

```python
import functools

import jax
import jax.numpy as jnp
from jax import lax
from jax.experimental import pallas as pl
from jax.experimental.pallas import tpu as pltpu
from jax.sharding import PartitionSpec as P

KIN = 32
KOUT = 128
BEST = 4
TILE = 16
PAIR = 2 * KOUT
BLOCK = 256
VMEM_LIMIT = 40 * 1024 * 1024


def block_rows_of(count):
    return min(BLOCK, count)


def left_matrix(left):
    wide = KIN * TILE
    row = lax.broadcasted_iota(jnp.int32, (wide, KIN), 0)
    column = lax.broadcasted_iota(jnp.int32, (wide, KIN), 1)
    spread = jnp.where((row >> 4) == column, 1.0, 0.0).astype(jnp.bfloat16)
    tall = jnp.dot(spread, left, preferred_element_type=jnp.float32).astype(jnp.bfloat16)
    full = lax.dot_general(
        tall, spread, (((1,), (1,)), ((), ())), preferred_element_type=jnp.float32
    )
    row = lax.broadcasted_iota(jnp.int32, (wide, wide), 0)
    column = lax.broadcasted_iota(jnp.int32, (wide, wide), 1)
    return jnp.where((row & (TILE - 1)) == (column & (TILE - 1)), full, 0.0).astype(jnp.bfloat16)


def right_matrix(right):
    zero = jnp.zeros_like(right)
    return jnp.concatenate(
        [jnp.concatenate([right, zero], 1), jnp.concatenate([zero, right], 1)], 0
    )


def precondition(rows_ref, left, right, half_ref, pre_ref):
    count = rows_ref.shape[0]
    both = right_matrix(right)
    for pair in range(KIN // 2):
        block = rows_ref[:, pair * PAIR : (pair + 1) * PAIR]
        half = jnp.dot(block, both, preferred_element_type=jnp.float32).astype(jnp.bfloat16)
        half_ref[2 * pair] = half[:, :KOUT]
        half_ref[2 * pair + 1] = half[:, KOUT:]
    mixer = left_matrix(left)

    def groups(index, carry):
        at = [pl.multiple_of(index * 2 * TILE + k * TILE, TILE) for k in range(2)]
        stacked = jnp.concatenate(
            [half_ref[:, pl.ds(a, TILE), :].reshape(KIN * TILE, KOUT) for a in at], 1
        )
        mixed = jnp.dot(mixer, stacked, preferred_element_type=jnp.float32).astype(jnp.bfloat16)
        for k in range(2):
            for i in range(KIN):
                pre_ref[pl.ds(at[k], TILE), i * KOUT : (i + 1) * KOUT] = mixed[
                    i * TILE : (i + 1) * TILE, k * KOUT : (k + 1) * KOUT
                ]
        return carry

    lax.fori_loop(0, count // (2 * TILE), groups, 0)


def store_copies(store_ref, store_vmem, sems, first):
    size = store_vmem.shape[1]
    return [
        pltpu.make_async_copy(
            store_ref.at[0, pl.ds(first + b * size, size)], store_vmem.at[b], sems.at[b]
        )
        for b in range(store_vmem.shape[0])
    ]


def dots(pre_ref, store_vmem, copies, out_ref):
    size = store_vmem.shape[1]
    for b, copy in enumerate(copies):
        copy.wait()
        out_ref[:, b * size : (b + 1) * size] = lax.dot_general(
            pre_ref[...],
            store_vmem[b],
            (((1,), (1,)), ((), ())),
            preferred_element_type=jnp.float32,
        )


def first_kernel(
    first, rows_ref, left_ref, right_ref, store_ref, pre_ref, out_ref,
    rows_vmem, half_ref, store_vmem, rows_sem, sems,
):
    rows_copy = pltpu.make_async_copy(rows_ref.at[0], rows_vmem, rows_sem)
    rows_copy.start()
    copies = store_copies(store_ref, store_vmem, sems, first)
    for copy in copies:
        copy.start()
    rows_copy.wait()
    precondition(rows_vmem, left_ref[0], right_ref[0], half_ref, pre_ref)
    dots(pre_ref, store_vmem, copies, out_ref)


def dot_kernel(first, pre_ref, store_ref, out_ref, store_vmem, sems):
    copies = store_copies(store_ref, store_vmem, sems, first)
    for copy in copies:
        copy.start()
    dots(pre_ref, store_vmem, copies, out_ref)


def store_scratch(columns, depth):
    size = block_rows_of(columns)
    return [
        pltpu.VMEM((columns // size, size, depth), jnp.bfloat16),
        pltpu.SemaphoreType.DMA((columns // size,)),
    ]


def precondition_and_score(queries, left_inv, right_inv, store, first, columns):
    count, depth = queries.shape[1:]
    store_vmem, sems = store_scratch(columns, depth)
    vmem = pl.BlockSpec(memory_space=pltpu.VMEM)
    anywhere = pl.BlockSpec(memory_space=pl.ANY)
    return pl.pallas_call(
        functools.partial(first_kernel, first),
        out_shape=(
            jax.ShapeDtypeStruct((count, depth), jnp.bfloat16),
            jax.ShapeDtypeStruct((count, columns), jnp.float32),
        ),
        in_specs=[anywhere, vmem, vmem, anywhere],
        out_specs=(vmem, vmem),
        scratch_shapes=[
            pltpu.VMEM((count, depth), jnp.bfloat16),
            pltpu.VMEM((KIN, count, KOUT), jnp.bfloat16),
            store_vmem,
            pltpu.SemaphoreType.DMA(()),
            sems,
        ],
        compiler_params=pltpu.CompilerParams(vmem_limit_bytes=VMEM_LIMIT),
        cost_estimate=pl.CostEstimate(
            flops=2 * count * depth * (columns + 1024),
            bytes_accessed=2 * depth * (2 * count + columns),
            transcendentals=0,
        ),
    )(queries, left_inv, right_inv, store)


def score(pre, store, first, columns):
    count, depth = pre.shape
    vmem = pl.BlockSpec(memory_space=pltpu.VMEM)
    anywhere = pl.BlockSpec(memory_space=pl.ANY)
    return pl.pallas_call(
        functools.partial(dot_kernel, first),
        out_shape=jax.ShapeDtypeStruct((count, columns), jnp.float32),
        in_specs=[vmem, anywhere],
        out_specs=vmem,
        scratch_shapes=store_scratch(columns, depth),
        compiler_params=pltpu.CompilerParams(vmem_limit_bytes=VMEM_LIMIT),
        cost_estimate=pl.CostEstimate(
            flops=2 * count * depth * columns,
            bytes_accessed=2 * depth * (count + columns),
            transcendentals=0,
        ),
    )(pre, store)


def swap(block, bit):
    route = [(i, i ^ bit) for i in range(lax.axis_size("layer"))]
    return lax.ppermute(block, "layer", route)


def sum_layers(block):
    count = lax.axis_size("layer")
    if count & (count - 1):
        return lax.psum(block, "layer").astype(jnp.bfloat16)
    index = lax.axis_index("layer")
    bits = [1 << k for k in range(count.bit_length() - 1)]
    for bit in bits:
        rows = block.shape[0] // 2
        upper = (index & bit) // bit
        kept = lax.dynamic_slice_in_dim(block, upper * rows, rows, 0)
        sent = lax.dynamic_slice_in_dim(block, (1 - upper) * rows, rows, 0)
        block = kept + swap(sent.astype(jnp.bfloat16), bit).astype(jnp.float32)
    block = block.astype(jnp.bfloat16)
    for bit in reversed(bits):
        other = swap(block, bit)
        low = (index & bit) == 0
        block = jnp.concatenate(
            [jnp.where(low, block, other), jnp.where(low, other, block)], 0
        )
    return block


def shards(store, queries, left_inv, right_inv, query_prompt, winner):
    rows = queries.shape[1]
    columns = store.shape[1]
    half = columns // 2
    ex_count = lax.axis_size("ex")
    position = lax.axis_index("ex")
    pre, left_part = precondition_and_score(queries, left_inv, right_inv, store, 0, half)
    scores = jnp.zeros((rows * ex_count, columns), jnp.bfloat16)
    current = pre
    for step in range(ex_count):
        source = (position - step) % ex_count
        if step == 0:
            parts = [(0, left_part), (half, score(pre, store, half, columns - half))]
        else:
            route = [((i - 1) % ex_count, i) for i in range(ex_count)]
            current = lax.ppermute(current, "ex", route)
            parts = [(0, score(current, store, 0, columns))]
        for first, part in parts:
            scores = lax.dynamic_update_slice(
                scores, sum_layers(part), (source * rows, jnp.int32(first))
            )
    ids = jnp.arange(scores.shape[0], dtype=jnp.int32)
    prompts = jnp.arange(winner.shape[0], dtype=jnp.int32)
    picks = (winner[:, None] == ids[None, :]).astype(jnp.float32)
    member = (query_prompt[None, :] == prompts[:, None]).astype(jnp.float32)
    weights = (picks - member / BEST).astype(jnp.bfloat16)
    advantage = jnp.dot(weights, scores, preferred_element_type=jnp.float32)
    return (scores, advantage.astype(jnp.bfloat16))


def solution(mesh):
    return jax.shard_map(
        shards,
        mesh=mesh,
        in_specs=(
            P("layer", ("grp", "ex"), None),
            P("layer", ("grp", "ex"), None),
            P("layer", None, None),
            P("layer", None, None),
            P("grp"),
            P("grp"),
        ),
        out_specs=(P(None, ("grp", "ex")), P(None, ("grp", "ex"))),
        check_vma=False,
    )
```

```python
import functools

import jax
import jax.numpy as jnp
from jax import lax
from jax.experimental import pallas as pl
from jax.experimental.pallas import tpu as pltpu
from jax.sharding import PartitionSpec as P

KIN = 32
KOUT = 128
BEST = 4
TILE = 16
PAIR = 2 * KOUT
BLOCK = 256
VMEM_LIMIT = 40 * 1024 * 1024


def block_rows_of(count):
    return min(BLOCK, count)


def left_matrix(left):
    wide = KIN * TILE
    row = lax.broadcasted_iota(jnp.int32, (wide, KIN), 0)
    column = lax.broadcasted_iota(jnp.int32, (wide, KIN), 1)
    spread = jnp.where((row >> 4) == column, 1.0, 0.0).astype(jnp.bfloat16)
    tall = jnp.dot(spread, left, preferred_element_type=jnp.float32).astype(jnp.bfloat16)
    full = lax.dot_general(
        tall, spread, (((1,), (1,)), ((), ())), preferred_element_type=jnp.float32
    )
    row = lax.broadcasted_iota(jnp.int32, (wide, wide), 0)
    column = lax.broadcasted_iota(jnp.int32, (wide, wide), 1)
    return jnp.where((row & (TILE - 1)) == (column & (TILE - 1)), full, 0.0).astype(jnp.bfloat16)


def right_matrix(right):
    zero = jnp.zeros_like(right)
    return jnp.concatenate(
        [jnp.concatenate([right, zero], 1), jnp.concatenate([zero, right], 1)], 0
    )


def precondition(rows_ref, left, right, half_ref, pre_ref):
    count = rows_ref.shape[0]
    both = right_matrix(right)
    for pair in range(KIN // 2):
        block = rows_ref[:, pair * PAIR : (pair + 1) * PAIR]
        half = jnp.dot(block, both, preferred_element_type=jnp.float32).astype(jnp.bfloat16)
        half_ref[2 * pair] = half[:, :KOUT]
        half_ref[2 * pair + 1] = half[:, KOUT:]
    mixer = left_matrix(left)

    def groups(index, carry):
        at = [pl.multiple_of(index * 2 * TILE + k * TILE, TILE) for k in range(2)]
        stacked = jnp.concatenate(
            [half_ref[:, pl.ds(a, TILE), :].reshape(KIN * TILE, KOUT) for a in at], 1
        )
        mixed = jnp.dot(mixer, stacked, preferred_element_type=jnp.float32).astype(jnp.bfloat16)
        for k in range(2):
            for i in range(KIN):
                pre_ref[pl.ds(at[k], TILE), i * KOUT : (i + 1) * KOUT] = mixed[
                    i * TILE : (i + 1) * TILE, k * KOUT : (k + 1) * KOUT
                ]
        return carry

    lax.fori_loop(0, count // (2 * TILE), groups, 0)


def store_copies(store_ref, store_vmem, sems, first):
    size = store_vmem.shape[1]
    return [
        pltpu.make_async_copy(
            store_ref.at[0, pl.ds(first + b * size, size)], store_vmem.at[b], sems.at[b]
        )
        for b in range(store_vmem.shape[0])
    ]


def dots(pre_ref, store_vmem, copies, out_ref):
    size = store_vmem.shape[1]
    for b, copy in enumerate(copies):
        copy.wait()
        out_ref[:, b * size : (b + 1) * size] = lax.dot_general(
            pre_ref[...],
            store_vmem[b],
            (((1,), (1,)), ((), ())),
            preferred_element_type=jnp.float32,
        )


def first_kernel(
    first, rows_ref, left_ref, right_ref, store_ref, pre_ref, out_ref,
    left_vmem, right_vmem, rows_vmem, half_ref, store_vmem, head_sems, sems,
):
    heads = [
        pltpu.make_async_copy(source.at[0], target, head_sems.at[k])
        for k, (source, target) in enumerate(
            ((right_ref, right_vmem), (left_ref, left_vmem), (rows_ref, rows_vmem))
        )
    ]
    for copy in heads:
        copy.start()
    copies = store_copies(store_ref, store_vmem, sems, first)
    for copy in copies:
        copy.start()
    for copy in heads:
        copy.wait()
    precondition(rows_vmem, left_vmem[...], right_vmem[...], half_ref, pre_ref)
    dots(pre_ref, store_vmem, copies, out_ref)


def dot_kernel(first, pre_ref, store_ref, out_ref, store_vmem, sems):
    copies = store_copies(store_ref, store_vmem, sems, first)
    for copy in copies:
        copy.start()
    dots(pre_ref, store_vmem, copies, out_ref)


def in_hbm(array):
    return pltpu.with_memory_space_constraint(array, pltpu.HBM)


def store_scratch(columns, depth):
    size = block_rows_of(columns)
    return [
        pltpu.VMEM((columns // size, size, depth), jnp.bfloat16),
        pltpu.SemaphoreType.DMA((columns // size,)),
    ]


def precondition_and_score(queries, left_inv, right_inv, store, first, columns):
    count, depth = queries.shape[1:]
    store_vmem, sems = store_scratch(columns, depth)
    vmem = pl.BlockSpec(memory_space=pltpu.VMEM)
    hbm = pl.BlockSpec(memory_space=pltpu.HBM)
    return pl.pallas_call(
        functools.partial(first_kernel, first),
        out_shape=(
            jax.ShapeDtypeStruct((count, depth), jnp.bfloat16),
            jax.ShapeDtypeStruct((count, columns), jnp.float32),
        ),
        in_specs=[hbm] * 4,
        out_specs=(vmem, vmem),
        scratch_shapes=[
            pltpu.VMEM((KIN, KIN), jnp.bfloat16),
            pltpu.VMEM((KOUT, KOUT), jnp.bfloat16),
            pltpu.VMEM((count, depth), jnp.bfloat16),
            pltpu.VMEM((KIN, count, KOUT), jnp.bfloat16),
            store_vmem,
            pltpu.SemaphoreType.DMA((3,)),
            sems,
        ],
        compiler_params=pltpu.CompilerParams(vmem_limit_bytes=VMEM_LIMIT),
        cost_estimate=pl.CostEstimate(
            flops=2 * count * depth * (columns + 1024),
            bytes_accessed=2 * depth * (2 * count + columns),
            transcendentals=0,
        ),
    )(*map(in_hbm, (queries, left_inv, right_inv, store)))


def score(pre, store, first, columns):
    count, depth = pre.shape
    vmem = pl.BlockSpec(memory_space=pltpu.VMEM)
    hbm = pl.BlockSpec(memory_space=pltpu.HBM)
    return pl.pallas_call(
        functools.partial(dot_kernel, first),
        out_shape=jax.ShapeDtypeStruct((count, columns), jnp.float32),
        in_specs=[vmem, hbm],
        out_specs=vmem,
        scratch_shapes=store_scratch(columns, depth),
        compiler_params=pltpu.CompilerParams(vmem_limit_bytes=VMEM_LIMIT),
        cost_estimate=pl.CostEstimate(
            flops=2 * count * depth * columns,
            bytes_accessed=2 * depth * (count + columns),
            transcendentals=0,
        ),
    )(pre, in_hbm(store))


def swap(block, bit):
    route = [(i, i ^ bit) for i in range(lax.axis_size("layer"))]
    return lax.ppermute(block, "layer", route)


def halves(block, upper):
    rows = block.shape[0] // 2
    kept = lax.dynamic_slice_in_dim(block, upper * rows, rows, 0)
    sent = lax.dynamic_slice_in_dim(block, (1 - upper) * rows, rows, 0)
    return kept, sent.astype(jnp.bfloat16)


class LayerSum:
    def __init__(self):
        self.count = lax.axis_size("layer")
        self.index = lax.axis_index("layer")
        self.bits = [1 << k for k in range(self.count.bit_length() - 1)]

    def begin(self, block):
        if not self.bits:
            return block, None
        kept, sent = halves(block, (self.index & self.bits[0]) // self.bits[0])
        return kept, swap(sent, self.bits[0])

    def finish(self, kept, received):
        if received is None:
            return kept.astype(jnp.bfloat16)
        block = kept + received.astype(jnp.float32)
        for bit in self.bits[1:]:
            kept, sent = halves(block, (self.index & bit) // bit)
            block = kept + swap(sent, bit).astype(jnp.float32)
        block = block.astype(jnp.bfloat16)
        for bit in reversed(self.bits):
            other = swap(block, bit)
            low = (self.index & bit) == 0
            block = jnp.concatenate(
                [jnp.where(low, block, other), jnp.where(low, other, block)], 0
            )
        return block


def shards(store, queries, left_inv, right_inv, query_prompt, winner):
    rows = queries.shape[1]
    columns = store.shape[1]
    half = columns // 2
    ex_count = lax.axis_size("ex")
    position = lax.axis_index("ex")
    pre, left_part = precondition_and_score(queries, left_inv, right_inv, store, 0, half)
    scores = jnp.zeros((rows * ex_count, columns), jnp.bfloat16)
    layers = LayerSum()
    parts = [(position, 0, left_part), (position, half, score(pre, store, half, columns - half))]
    current = pre
    for step in range(1, ex_count):
        route = [((i - 1) % ex_count, i) for i in range(ex_count)]
        current = lax.ppermute(current, "ex", route)
        parts.append(((position - step) % ex_count, 0, score(current, store, 0, columns)))
    last = parts[-1][2]
    begun = [layers.begin(part) for _, _, part in parts]
    for (source, first, _), (kept, received) in zip(parts, begun):
        if kept.shape != begun[-1][0].shape:
            received, _ = lax.optimization_barrier((received, last))
        done = layers.finish(kept, received)
        scores = lax.dynamic_update_slice(scores, done, (source * rows, jnp.int32(first)))
    ids = jnp.arange(scores.shape[0], dtype=jnp.int32)
    prompts = jnp.arange(winner.shape[0], dtype=jnp.int32)
    picks = (winner[:, None] == ids[None, :]).astype(jnp.float32)
    member = (query_prompt[None, :] == prompts[:, None]).astype(jnp.float32)
    weights = (picks - member / BEST).astype(jnp.bfloat16)
    advantage = jnp.dot(weights, scores, preferred_element_type=jnp.float32)
    return (scores, advantage.astype(jnp.bfloat16))


def solution(mesh):
    return jax.shard_map(
        shards,
        mesh=mesh,
        in_specs=(
            P("layer", ("grp", "ex"), None),
            P("layer", ("grp", "ex"), None),
            P("layer", None, None),
            P("layer", None, None),
            P("grp"),
            P("grp"),
        ),
        out_specs=(P(None, ("grp", "ex")), P(None, ("grp", "ex"))),
        check_vma=False,
    )
```

```python
import functools

import jax
import jax.numpy as jnp
from jax import lax
from jax.experimental import pallas as pl
from jax.experimental.pallas import tpu as pltpu
from jax.sharding import PartitionSpec as P

KIN = 32
KOUT = 128
BEST = 4
ROWS = 8
WIDE = KIN * ROWS
PAIR = 2 * KOUT
DEPTH_BLOCK = 512
AHEAD = 3
VMEM_LIMIT = 40 * 1024 * 1024
NT = (((1,), (1,)), ((), ()))


def left_matrix(left):
    row = lax.broadcasted_iota(jnp.int32, (WIDE, KIN), 0)
    column = lax.broadcasted_iota(jnp.int32, (WIDE, KIN), 1)
    spread = jnp.where((row >> 3) == column, 1.0, 0.0).astype(jnp.bfloat16)
    tall = jnp.dot(spread, left, preferred_element_type=jnp.float32).astype(jnp.bfloat16)
    full = lax.dot_general(tall, spread, NT, preferred_element_type=jnp.float32)
    row = lax.broadcasted_iota(jnp.int32, (WIDE, WIDE), 0)
    column = lax.broadcasted_iota(jnp.int32, (WIDE, WIDE), 1)
    return jnp.where((row & (ROWS - 1)) == (column & (ROWS - 1)), full, 0.0).astype(jnp.bfloat16)


def right_matrix(right):
    zero = jnp.zeros_like(right)
    return jnp.concatenate(
        [jnp.concatenate([right, zero], 1), jnp.concatenate([zero, right], 1)], 0
    )


def side_by_side_to_stacked(block):
    tiles = block.reshape(block.shape[0] // ROWS, ROWS, PAIR)
    return jnp.concatenate([tiles[:, :, :KOUT], tiles[:, :, KOUT:]], 1)


def precondition(rows_ref, left, right, half_ref, pre_ref):
    count = rows_ref.shape[0]
    both = right_matrix(right)
    together = 4
    for start in range(0, KIN // 2, together):
        block = jnp.concatenate(
            [rows_ref[:, p * PAIR : (p + 1) * PAIR] for p in range(start, start + together)], 0
        )
        half = jnp.dot(block, both, preferred_element_type=jnp.float32)
        for k in range(together):
            at = 2 * ROWS * (start + k)
            half_ref[:, at : at + 2 * ROWS, :] = side_by_side_to_stacked(
                half[k * count : (k + 1) * count]
            ).astype(jnp.bfloat16)
    mixer = left_matrix(left)

    def groups(index, carry):
        stacked = jnp.concatenate([half_ref[2 * index], half_ref[2 * index + 1]], 1)
        mixed = side_by_side_to_stacked(
            jnp.dot(mixer, stacked, preferred_element_type=jnp.float32)
        ).astype(jnp.bfloat16)
        at = pl.ds(pl.multiple_of(index * 2 * ROWS, 2 * ROWS), 2 * ROWS)
        for i in range(KIN):
            pre_ref[at, i * KOUT : (i + 1) * KOUT] = mixed[i]
        return carry

    lax.fori_loop(0, count // (2 * ROWS), groups, 0, unroll=4)


def store_copies(store_ref, store_vmem, sems, first):
    blocks, columns, depth = store_vmem.shape
    return [
        pltpu.make_async_copy(
            store_ref.at[0, pl.ds(first, columns), pl.ds(b * depth, depth)],
            store_vmem.at[b],
            sems.at[b],
        )
        for b in range(blocks)
    ]


def dots(pre_ref, store_vmem, copies, total_ref, out_ref):
    depth = store_vmem.shape[2]
    for b, copy in enumerate(copies):
        copy.wait()
        if b + AHEAD < len(copies):
            copies[b + AHEAD].start()
        term = lax.dot_general(
            store_vmem[b],
            pre_ref[:, b * depth : (b + 1) * depth],
            NT,
            preferred_element_type=jnp.float32,
        )
        if b == 0:
            total_ref[...] = term
        elif b + 1 < len(copies):
            total_ref[...] += term
        else:
            out_ref[...] = (total_ref[...] + term).T


def first_kernel(
    first, rows_ref, left_ref, right_ref, store_ref, pre_ref, out_ref,
    left_vmem, right_vmem, rows_vmem, half_ref, store_vmem, total_ref, head_sems, sems,
):
    heads = [
        pltpu.make_async_copy(source.at[0], target, head_sems.at[k])
        for k, (source, target) in enumerate(
            ((right_ref, right_vmem), (left_ref, left_vmem), (rows_ref, rows_vmem))
        )
    ]
    for copy in heads:
        copy.start()
    copies = store_copies(store_ref, store_vmem, sems, first)
    for copy in copies[:AHEAD]:
        copy.start()
    for copy in heads:
        copy.wait()
    precondition(rows_vmem, left_vmem[...], right_vmem[...], half_ref, pre_ref)
    dots(pre_ref, store_vmem, copies, total_ref, out_ref)


def dot_kernel(first, pre_ref, store_ref, out_ref, store_vmem, total_ref, sems):
    copies = store_copies(store_ref, store_vmem, sems, first)
    for copy in copies[:AHEAD]:
        copy.start()
    dots(pre_ref, store_vmem, copies, total_ref, out_ref)


def in_hbm(array):
    return pltpu.with_memory_space_constraint(array, pltpu.HBM)


def scratch(count, columns, depth):
    blocks = depth // DEPTH_BLOCK
    return (
        pltpu.VMEM((blocks, columns, DEPTH_BLOCK), jnp.bfloat16),
        pltpu.VMEM((columns, count), jnp.float32),
        pltpu.SemaphoreType.DMA((blocks,)),
    )


def precondition_and_score(queries, left_inv, right_inv, store, first, columns):
    count, depth = queries.shape[1:]
    store_vmem, total, sems = scratch(count, columns, depth)
    vmem = pl.BlockSpec(memory_space=pltpu.VMEM)
    hbm = pl.BlockSpec(memory_space=pltpu.HBM)
    return pl.pallas_call(
        functools.partial(first_kernel, first),
        out_shape=(
            jax.ShapeDtypeStruct((count, depth), jnp.bfloat16),
            jax.ShapeDtypeStruct((count, columns), jnp.float32),
        ),
        in_specs=[hbm] * 4,
        out_specs=(vmem, vmem),
        scratch_shapes=[
            pltpu.VMEM((KIN, KIN), jnp.bfloat16),
            pltpu.VMEM((KOUT, KOUT), jnp.bfloat16),
            pltpu.VMEM((count, depth), jnp.bfloat16),
            pltpu.VMEM((count // ROWS, WIDE, KOUT), jnp.bfloat16),
            store_vmem,
            total,
            pltpu.SemaphoreType.DMA((3,)),
            sems,
        ],
        compiler_params=pltpu.CompilerParams(vmem_limit_bytes=VMEM_LIMIT),
        cost_estimate=pl.CostEstimate(
            flops=2 * count * depth * (columns + 1024),
            bytes_accessed=2 * depth * (2 * count + columns),
            transcendentals=0,
        ),
    )(*map(in_hbm, (queries, left_inv, right_inv, store)))


def score(pre, store, first, columns):
    count, depth = pre.shape
    vmem = pl.BlockSpec(memory_space=pltpu.VMEM)
    hbm = pl.BlockSpec(memory_space=pltpu.HBM)
    return pl.pallas_call(
        functools.partial(dot_kernel, first),
        out_shape=jax.ShapeDtypeStruct((count, columns), jnp.float32),
        in_specs=[vmem, hbm],
        out_specs=vmem,
        scratch_shapes=scratch(count, columns, depth),
        compiler_params=pltpu.CompilerParams(vmem_limit_bytes=VMEM_LIMIT),
        cost_estimate=pl.CostEstimate(
            flops=2 * count * depth * columns,
            bytes_accessed=2 * depth * (count + columns),
            transcendentals=0,
        ),
    )(pre, in_hbm(store))


def swap(block, bit):
    route = [(i, i ^ bit) for i in range(lax.axis_size("layer"))]
    return lax.ppermute(block, "layer", route)


class LayerSum:
    def __init__(self, block, bits, index):
        self.block, self.index = block, index
        self.moves = [(bit, True) for bit in bits] + [(bit, False) for bit in reversed(bits)]
        self.steps = len(self.moves)
        if not bits:
            self.block = block.astype(jnp.bfloat16)

    def sizes(self):
        size = self.block.size
        for _, halving in self.moves:
            size = size // 2 if halving else size
            yield 2 * size
            size = size if halving else size * 2

    def send(self, order):
        bit, halving = self.moves[0]
        if halving:
            rows = self.block.shape[0] // 2
            upper = (self.index & bit) // bit
            sent = lax.dynamic_slice_in_dim(self.block, (1 - upper) * rows, rows, 0)
            sent = sent.astype(jnp.bfloat16)
            self.block = lax.dynamic_slice_in_dim(self.block, upper * rows, rows, 0)
        else:
            sent = self.block
        self.received = swap(order.after(sent), bit)

    def take(self, order):
        bit, halving = self.moves.pop(0)
        received = order.mark(self.received)
        if halving:
            self.block = self.block + received.astype(jnp.float32)
            if not (self.moves and self.moves[0][1]):
                self.block = self.block.astype(jnp.bfloat16)
        else:
            low = (self.index & bit) == 0
            mine = self.block
            self.block = jnp.concatenate(
                [jnp.where(low, mine, received), jnp.where(low, received, mine)], 0
            )


class Order:
    def __init__(self):
        self.last = jnp.zeros((), jnp.float32)

    def after(self, value):
        value, _ = lax.optimization_barrier((value, self.last))
        return value

    def mark(self, value):
        value, self.last = lax.optimization_barrier((value, self.last))
        return value


STEP_US = 1.5
BYTES_PER_US = 50000


def sum_layers(chunks):
    order = Order()
    events = []
    for number, (start, chunk) in enumerate(chunks):
        chunk.send(order)
        at = start
        for size in chunk.sizes():
            at += STEP_US + size / BYTES_PER_US
            events.append((at, number))
    order.mark(chunks[-1][1].block)
    for _, number in sorted(events):
        chunk = chunks[number][1]
        chunk.take(order)
        if chunk.moves:
            chunk.send(order)
    return [chunk.block for _, chunk in chunks]


def shards(store, queries, left_inv, right_inv, query_prompt, winner):
    rows = queries.shape[1]
    columns = store.shape[1]
    half = columns // 2
    ex_count = lax.axis_size("ex")
    position = lax.axis_index("ex")
    pre, left_part = precondition_and_score(queries, left_inv, right_inv, store, 0, half)
    parts = [(position, 0, left_part), (position, half, score(pre, store, half, columns - half))]
    current = pre
    for step in range(1, ex_count):
        route = [((i - 1) % ex_count, i) for i in range(ex_count)]
        current = lax.ppermute(current, "ex", route)
        parts.append(((position - step) % ex_count, 0, score(current, store, 0, columns)))
    count = lax.axis_size("layer")
    index = lax.axis_index("layer")
    bits = [1 << k for k in range(count.bit_length() - 1)]
    done = sum_layers(
        [(2 * k, LayerSum(part, bits, index)) for k, (_, _, part) in enumerate(parts)]
    )
    scores = jnp.zeros((rows * ex_count, columns), jnp.bfloat16)
    for (source, first, _), block in zip(parts, done):
        scores = lax.dynamic_update_slice(scores, block, (source * rows, jnp.int32(first)))
    ids = jnp.arange(scores.shape[0], dtype=jnp.int32)
    prompts = jnp.arange(winner.shape[0], dtype=jnp.int32)
    picks = (winner[:, None] == ids[None, :]).astype(jnp.float32)
    member = (query_prompt[None, :] == prompts[:, None]).astype(jnp.float32)
    weights = (picks - member / BEST).astype(jnp.bfloat16)
    advantage = jnp.dot(weights, scores, preferred_element_type=jnp.float32)
    return (scores, advantage.astype(jnp.bfloat16))


def solution(mesh):
    return jax.shard_map(
        shards,
        mesh=mesh,
        in_specs=(
            P("layer", ("grp", "ex"), None),
            P("layer", ("grp", "ex"), None),
            P("layer", None, None),
            P("layer", None, None),
            P("grp"),
            P("grp"),
        ),
        out_specs=(P(None, ("grp", "ex")), P(None, ("grp", "ex"))),
        check_vma=False,
    )
```

```python
import functools

import jax
import jax.numpy as jnp
from jax import lax
from jax.experimental import pallas as pl
from jax.experimental.pallas import tpu as pltpu
from jax.sharding import PartitionSpec as P

KIN = 32
KOUT = 128
BEST = 4
ROWS = 8
WIDE = KIN * ROWS
PAIR = 2 * KOUT
DEPTH_BLOCK = 512
VMEM_LIMIT = 24 * 1024 * 1024
NT = (((1,), (1,)), ((), ()))


def left_matrix(left):
    row = lax.broadcasted_iota(jnp.int32, (WIDE, KIN), 0)
    column = lax.broadcasted_iota(jnp.int32, (WIDE, KIN), 1)
    spread = jnp.where((row >> 3) == column, 1.0, 0.0).astype(jnp.bfloat16)
    tall = jnp.dot(spread, left, preferred_element_type=jnp.float32).astype(jnp.bfloat16)
    full = lax.dot_general(tall, spread, NT, preferred_element_type=jnp.float32)
    row = lax.broadcasted_iota(jnp.int32, (WIDE, WIDE), 0)
    column = lax.broadcasted_iota(jnp.int32, (WIDE, WIDE), 1)
    return jnp.where((row & (ROWS - 1)) == (column & (ROWS - 1)), full, 0.0).astype(jnp.bfloat16)


def right_matrix(right):
    zero = jnp.zeros_like(right)
    return jnp.concatenate(
        [jnp.concatenate([right, zero], 1), jnp.concatenate([zero, right], 1)], 0
    )


def side_by_side_to_stacked(block):
    tiles = block.reshape(block.shape[0] // ROWS, ROWS, PAIR)
    return jnp.concatenate([tiles[:, :, :KOUT], tiles[:, :, KOUT:]], 1)


def precondition(rows_ref, left, right, half_ref, pre_ref):
    count = rows_ref.shape[0]
    both = right_matrix(right)
    together = 4
    for start in range(0, KIN // 2, together):
        block = jnp.concatenate(
            [rows_ref[:, p * PAIR : (p + 1) * PAIR] for p in range(start, start + together)], 0
        )
        half = jnp.dot(block, both, preferred_element_type=jnp.float32)
        for k in range(together):
            at = 2 * ROWS * (start + k)
            half_ref[:, at : at + 2 * ROWS, :] = side_by_side_to_stacked(
                half[k * count : (k + 1) * count]
            ).astype(jnp.bfloat16)
    mixer = left_matrix(left)

    def groups(index, carry):
        stacked = jnp.concatenate([half_ref[2 * index], half_ref[2 * index + 1]], 1)
        mixed = side_by_side_to_stacked(
            jnp.dot(mixer, stacked, preferred_element_type=jnp.float32)
        ).astype(jnp.bfloat16)
        at = pl.ds(pl.multiple_of(index * 2 * ROWS, 2 * ROWS), 2 * ROWS)
        for i in range(KIN):
            pre_ref[at, i * KOUT : (i + 1) * KOUT] = mixed[i]
        return carry

    lax.fori_loop(0, count // (2 * ROWS), groups, 0, unroll=4)


def precondition_kernel(rows_ref, left_ref, right_ref, pre_ref, half_ref):
    precondition(rows_ref.at[0], left_ref[0], right_ref[0], half_ref, pre_ref)


def dot_kernel(first, pre_ref, store_ref, out_ref, total_ref):
    depth = pre_ref.shape[1]
    columns = total_ref.shape[0]
    for at in range(0, depth, DEPTH_BLOCK):
        block = slice(at, at + DEPTH_BLOCK)
        term = lax.dot_general(
            store_ref[0, first : first + columns, block],
            pre_ref[:, block],
            NT,
            preferred_element_type=jnp.float32,
        )
        if at == 0:
            total_ref[...] = term
        elif at + DEPTH_BLOCK < depth:
            total_ref[...] += term
        else:
            out_ref[...] = (total_ref[...] + term).T


def in_vmem(array):
    return pltpu.with_memory_space_constraint(array, pltpu.VMEM)


def preconditioned(queries, left_inv, right_inv):
    count, depth = queries.shape[1:]
    vmem = pl.BlockSpec(memory_space=pltpu.VMEM)
    return pl.pallas_call(
        precondition_kernel,
        out_shape=jax.ShapeDtypeStruct((count, depth), jnp.bfloat16),
        in_specs=[vmem] * 3,
        out_specs=vmem,
        scratch_shapes=[pltpu.VMEM((count // ROWS, WIDE, KOUT), jnp.bfloat16)],
        compiler_params=pltpu.CompilerParams(vmem_limit_bytes=VMEM_LIMIT),
        cost_estimate=pl.CostEstimate(
            flops=2 * count * depth * 1024, bytes_accessed=4 * depth * count, transcendentals=0
        ),
    )(in_vmem(queries), left_inv, right_inv)


def score(pre, store, first, columns):
    count, depth = pre.shape
    vmem = pl.BlockSpec(memory_space=pltpu.VMEM)
    return pl.pallas_call(
        functools.partial(dot_kernel, first),
        out_shape=jax.ShapeDtypeStruct((count, columns), jnp.float32),
        in_specs=[vmem] * 2,
        out_specs=vmem,
        scratch_shapes=[pltpu.VMEM((columns, count), jnp.float32)],
        compiler_params=pltpu.CompilerParams(vmem_limit_bytes=VMEM_LIMIT),
        cost_estimate=pl.CostEstimate(
            flops=2 * count * depth * columns,
            bytes_accessed=2 * depth * (count + columns),
            transcendentals=0,
        ),
    )(pre, store)


def swap(block, bit):
    route = [(i, i ^ bit) for i in range(lax.axis_size("layer"))]
    return lax.ppermute(block, "layer", route)


class LayerSum:
    def __init__(self, block, bits, index):
        self.block, self.index = block, index
        self.moves = [(bit, True) for bit in bits] + [(bit, False) for bit in reversed(bits)]
        self.steps = len(self.moves)
        if not bits:
            self.block = block.astype(jnp.bfloat16)

    def sizes(self):
        size = self.block.size
        for _, halving in self.moves:
            size = size // 2 if halving else size
            yield 2 * size
            size = size if halving else size * 2

    def send(self, order):
        bit, halving = self.moves[0]
        if halving:
            rows = self.block.shape[0] // 2
            upper = (self.index & bit) // bit
            sent = lax.dynamic_slice_in_dim(self.block, (1 - upper) * rows, rows, 0)
            sent = sent.astype(jnp.bfloat16)
            self.block = lax.dynamic_slice_in_dim(self.block, upper * rows, rows, 0)
        else:
            sent = self.block
        self.received = swap(order.after(sent), bit)

    def take(self, order):
        bit, halving = self.moves.pop(0)
        received = order.mark(self.received)
        if halving:
            self.block = self.block + received.astype(jnp.float32)
            if not (self.moves and self.moves[0][1]):
                self.block = self.block.astype(jnp.bfloat16)
        else:
            low = (self.index & bit) == 0
            mine = self.block
            self.block = jnp.concatenate(
                [jnp.where(low, mine, received), jnp.where(low, received, mine)], 0
            )


class Order:
    def __init__(self):
        self.last = jnp.zeros((), jnp.float32)

    def after(self, value):
        value, _ = lax.optimization_barrier((value, self.last))
        return value

    def mark(self, value):
        value, self.last = lax.optimization_barrier((value, self.last))
        return value


STEP_US = 1.5
BYTES_PER_US = 50000


def sum_layers(chunks):
    order = Order()
    events = []
    for number, (start, chunk) in enumerate(chunks):
        chunk.send(order)
        at = start
        for size in chunk.sizes():
            at += STEP_US + size / BYTES_PER_US
            events.append((at, number))
    order.mark(chunks[-1][1].block)
    for _, number in sorted(events):
        chunk = chunks[number][1]
        chunk.take(order)
        if chunk.moves:
            chunk.send(order)
    return [chunk.block for _, chunk in chunks]


def shards(store, queries, left_inv, right_inv, query_prompt, winner):
    rows = queries.shape[1]
    columns = store.shape[1]
    half = columns // 2
    ex_count = lax.axis_size("ex")
    position = lax.axis_index("ex")
    pre = preconditioned(queries, left_inv, right_inv)
    store = in_vmem(store)
    parts = [
        (position, 0, score(pre, store, 0, half)),
        (position, half, score(pre, store, half, columns - half)),
    ]
    current = pre
    for step in range(1, ex_count):
        route = [((i - 1) % ex_count, i) for i in range(ex_count)]
        current = lax.ppermute(current, "ex", route)
        parts.append(((position - step) % ex_count, 0, score(current, store, 0, columns)))
    count = lax.axis_size("layer")
    index = lax.axis_index("layer")
    bits = [1 << k for k in range(count.bit_length() - 1)]
    done = sum_layers(
        [(2 * k, LayerSum(part, bits, index)) for k, (_, _, part) in enumerate(parts)]
    )
    scores = jnp.zeros((rows * ex_count, columns), jnp.bfloat16)
    for (source, first, _), block in zip(parts, done):
        scores = lax.dynamic_update_slice(scores, block, (source * rows, jnp.int32(first)))
    ids = jnp.arange(scores.shape[0], dtype=jnp.int32)
    prompts = jnp.arange(winner.shape[0], dtype=jnp.int32)
    picks = (winner[:, None] == ids[None, :]).astype(jnp.float32)
    member = (query_prompt[None, :] == prompts[:, None]).astype(jnp.float32)
    weights = (picks - member / BEST).astype(jnp.bfloat16)
    advantage = jnp.dot(weights, scores, preferred_element_type=jnp.float32)
    return (scores, advantage.astype(jnp.bfloat16))


def solution(mesh):
    return jax.shard_map(
        shards,
        mesh=mesh,
        in_specs=(
            P("layer", ("grp", "ex"), None),
            P("layer", ("grp", "ex"), None),
            P("layer", None, None),
            P("layer", None, None),
            P("grp"),
            P("grp"),
        ),
        out_specs=(P(None, ("grp", "ex")), P(None, ("grp", "ex"))),
        check_vma=False,
    )
```

```python
import functools

import jax
import jax.numpy as jnp
from jax import lax
from jax.experimental import pallas as pl
from jax.experimental.pallas import tpu as pltpu
from jax.sharding import PartitionSpec as P

KIN = 32
KOUT = 128
BEST = 4
ROWS = 8
WIDE = KIN * ROWS
PAIR = 2 * KOUT
DEPTH_BLOCK = 512
COLUMNS = 512
VMEM_LIMIT = 32 * 1024 * 1024
NT = (((1,), (1,)), ((), ()))


def left_matrix(left):
    row = lax.broadcasted_iota(jnp.int32, (WIDE, KIN), 0)
    column = lax.broadcasted_iota(jnp.int32, (WIDE, KIN), 1)
    spread = jnp.where((row >> 3) == column, 1.0, 0.0).astype(jnp.bfloat16)
    tall = jnp.dot(spread, left, preferred_element_type=jnp.float32).astype(jnp.bfloat16)
    full = lax.dot_general(tall, spread, NT, preferred_element_type=jnp.float32)
    row = lax.broadcasted_iota(jnp.int32, (WIDE, WIDE), 0)
    column = lax.broadcasted_iota(jnp.int32, (WIDE, WIDE), 1)
    return jnp.where((row & (ROWS - 1)) == (column & (ROWS - 1)), full, 0.0).astype(jnp.bfloat16)


def right_matrix(right):
    zero = jnp.zeros_like(right)
    return jnp.concatenate(
        [jnp.concatenate([right, zero], 1), jnp.concatenate([zero, right], 1)], 0
    )


def side_by_side_to_stacked(block):
    tiles = block.reshape(block.shape[0] // ROWS, ROWS, PAIR)
    return jnp.concatenate([tiles[:, :, :KOUT], tiles[:, :, KOUT:]], 1)


def precondition(rows_ref, left, right, half_ref, pre_ref):
    count = rows_ref.shape[0]
    both = right_matrix(right)
    together = 4
    for start in range(0, KIN // 2, together):
        block = jnp.concatenate(
            [rows_ref[:, p * PAIR : (p + 1) * PAIR] for p in range(start, start + together)], 0
        )
        half = jnp.dot(block, both, preferred_element_type=jnp.float32)
        for k in range(together):
            at = 2 * ROWS * (start + k)
            half_ref[:, at : at + 2 * ROWS, :] = side_by_side_to_stacked(
                half[k * count : (k + 1) * count]
            ).astype(jnp.bfloat16)
    mixer = left_matrix(left)

    def groups(index, carry):
        stacked = jnp.concatenate([half_ref[2 * index], half_ref[2 * index + 1]], 1)
        mixed = side_by_side_to_stacked(
            jnp.dot(mixer, stacked, preferred_element_type=jnp.float32)
        ).astype(jnp.bfloat16)
        at = pl.ds(pl.multiple_of(index * 2 * ROWS, 2 * ROWS), 2 * ROWS)
        for i in range(KIN):
            pre_ref[at, i * KOUT : (i + 1) * KOUT] = mixed[i]
        return carry

    lax.fori_loop(0, count // (2 * ROWS), groups, 0, unroll=4)


def dot(pre_ref, store_ref, first, total_ref, out_ref):
    depth = pre_ref.shape[1]
    columns = total_ref.shape[0]
    for at in range(0, depth, DEPTH_BLOCK):
        block = slice(at, at + DEPTH_BLOCK)
        term = lax.dot_general(
            store_ref[first : first + columns, block],
            pre_ref[:, block],
            NT,
            preferred_element_type=jnp.float32,
        )
        if at == 0:
            total_ref[...] = term
        elif at + DEPTH_BLOCK < depth:
            total_ref[...] += term
        else:
            out_ref[...] = (total_ref[...] + term).T


def first_kernel(
    rows_ref, left_ref, right_ref, store_ref, out_ref, pre_ref, store_vmem, rows_vmem,
    left_vmem, right_vmem, half_ref, total_ref, head_sems, sems,
):
    heads = [
        pltpu.make_async_copy(source.at[0], target, head_sems.at[k])
        for k, (source, target) in enumerate(
            ((right_ref, right_vmem), (left_ref, left_vmem), (rows_ref, rows_vmem))
        )
    ]
    columns = total_ref.shape[0]
    copies = [
        pltpu.make_async_copy(
            store_ref.at[0, pl.ds(first, columns)],
            store_vmem.at[pl.ds(first, columns)],
            sems.at[k],
        )
        for k, first in enumerate(range(0, store_vmem.shape[0], columns))
    ]
    for copy in heads + copies:
        copy.start()
    for copy in heads:
        copy.wait()
    precondition(rows_vmem, left_vmem[...], right_vmem[...], half_ref, pre_ref)
    copies[0].wait()
    dot(pre_ref, store_vmem, 0, total_ref, out_ref)
    for copy in copies[1:]:
        copy.wait()


def later_kernel(first, pre_ref, store_ref, out_ref, total_ref):
    dot(pre_ref, store_ref, first, total_ref, out_ref)


VMEM = pl.BlockSpec(memory_space=pltpu.VMEM)
HBM = pl.BlockSpec(memory_space=pltpu.HBM)


def in_hbm(array):
    return pltpu.with_memory_space_constraint(array, pltpu.HBM)


def first_scores(queries, left_inv, right_inv, store, columns):
    count, depth = queries.shape[1:]
    examples = store.shape[1]
    out, pre, store_vmem, _ = pl.pallas_call(
        first_kernel,
        out_shape=(
            pltpu.VMEM((count, columns), jnp.float32),
            pltpu.VMEM((count, depth), jnp.bfloat16),
            pltpu.VMEM((examples, depth), jnp.bfloat16),
            pltpu.VMEM((count, depth), jnp.bfloat16),
        ),
        in_specs=[HBM] * 4,
        out_specs=(VMEM,) * 4,
        scratch_shapes=[
            pltpu.VMEM((KIN, KIN), jnp.bfloat16),
            pltpu.VMEM((KOUT, KOUT), jnp.bfloat16),
            pltpu.VMEM((count // ROWS, WIDE, KOUT), jnp.bfloat16),
            pltpu.VMEM((columns, count), jnp.float32),
            pltpu.SemaphoreType.DMA((3,)),
            pltpu.SemaphoreType.DMA((examples // columns,)),
        ],
        compiler_params=pltpu.CompilerParams(vmem_limit_bytes=VMEM_LIMIT),
        cost_estimate=pl.CostEstimate(
            flops=2 * count * depth * (columns + 1024),
            bytes_accessed=2 * depth * (2 * count + examples),
            transcendentals=0,
        ),
    )(*map(in_hbm, (queries, left_inv, right_inv, store)))
    return out, pre, store_vmem


def later_scores(pre, store_vmem, first, columns):
    count, depth = pre.shape
    return pl.pallas_call(
        functools.partial(later_kernel, first),
        out_shape=pltpu.VMEM((count, columns), jnp.float32),
        in_specs=[VMEM] * 2,
        out_specs=VMEM,
        scratch_shapes=[pltpu.VMEM((columns, count), jnp.float32)],
        compiler_params=pltpu.CompilerParams(vmem_limit_bytes=VMEM_LIMIT),
        cost_estimate=pl.CostEstimate(
            flops=2 * count * depth * columns,
            bytes_accessed=2 * depth * (count + columns),
            transcendentals=0,
        ),
    )(pre, store_vmem)


def swap(block, bit):
    route = [(i, i ^ bit) for i in range(lax.axis_size("layer"))]
    return lax.ppermute(block, "layer", route)


HALVE, EXCHANGE, DOUBLE = range(3)


class LayerSum:
    def __init__(self, block, bits, index):
        self.block, self.index = block, index
        self.moves = [(bit, HALVE) for bit in bits[:-1]]
        self.moves += [(bit, EXCHANGE) for bit in bits[-1:]]
        self.moves += [(bit, DOUBLE) for bit in reversed(bits[:-1])]
        if len(bits) < 2:
            self.block = block.astype(jnp.bfloat16)

    def send(self, order):
        bit, kind = self.moves[0]
        sent = self.block
        if kind == HALVE:
            rows = self.block.shape[0] // 2
            upper = (self.index & bit) // bit
            sent = lax.dynamic_slice_in_dim(self.block, (1 - upper) * rows, rows, 0)
            sent = sent.astype(jnp.bfloat16)
            self.block = lax.dynamic_slice_in_dim(self.block, upper * rows, rows, 0)
        self.received = swap(order.after(sent), bit)

    def take(self, order):
        bit, kind = self.moves.pop(0)
        received = order.mark(self.received)
        mine = self.block
        if kind == DOUBLE:
            low = (self.index & bit) == 0
            self.block = jnp.concatenate(
                [jnp.where(low, mine, received), jnp.where(low, received, mine)], 0
            )
            return
        self.block = mine.astype(jnp.float32) + received.astype(jnp.float32)
        if not (self.moves and self.moves[0][1] == HALVE):
            self.block = self.block.astype(jnp.bfloat16)


class Order:
    def __init__(self):
        self.last = jnp.zeros((), jnp.float32)

    def after(self, value):
        value, _ = lax.optimization_barrier((value, self.last))
        return value

    def mark(self, value):
        value, self.last = lax.optimization_barrier((value, self.last))
        return value


STEP_US = 1.7
BYTES_PER_US = 50000


def step_times(size, bits):
    at, sent = 0.0, size
    sizes = []
    for _ in range(bits - 1):
        sent //= 2
        sizes.append(sent)
    for size in sizes + [sent] + sizes[::-1]:
        at += STEP_US + 2 * size / BYTES_PER_US
        yield at


def sum_layers(makers, bits, index):
    order = Order()
    chunks = {}
    events = []
    for number, (start, size, _) in enumerate(makers):
        events.append((start, number))
        events.extend((start + 2 + at, number) for at in step_times(size, len(bits)) if bits)
    for _, number in sorted(events):
        if number not in chunks:
            chunk = chunks[number] = LayerSum(makers[number][2](order), bits, index)
        else:
            chunk = chunks[number]
            chunk.take(order)
        if chunk.moves:
            chunk.send(order)
    return [chunks[number].block for number in range(len(makers))]


def shards(store, queries, left_inv, right_inv, query_prompt, winner):
    rows = queries.shape[1]
    columns = store.shape[1]
    width = min(COLUMNS, columns)
    ex_count = lax.axis_size("ex")
    position = lax.axis_index("ex")
    first_part, pre, store_vmem = first_scores(queries, left_inv, right_inv, store, width)
    places, makers = [], []
    current = pre
    for step in range(ex_count):
        if step > 0:
            route = [((i - 1) % ex_count, i) for i in range(ex_count)]
            current = lax.ppermute(current, "ex", route)
        for first in range(0, columns, width):

            def make(order, first=first, step=step, current=current):
                if step == 0 and first == 0:
                    return first_part
                return order.mark(later_scores(order.after(current), store_vmem, first, width))

            start = 4.5 + 4.5 * step + 1.5 * (first // width)
            makers.append((start, rows * width, make))
            places.append(((position - step) % ex_count * rows, jnp.int32(first)))
    count = lax.axis_size("layer")
    bits = [1 << k for k in range(count.bit_length() - 1)]
    done = sum_layers(makers, bits, lax.axis_index("layer"))
    scores = jnp.zeros((rows * ex_count, columns), jnp.bfloat16)
    for place, block in zip(places, done):
        scores = lax.dynamic_update_slice(scores, block, place)
    ids = jnp.arange(scores.shape[0], dtype=jnp.int32)
    prompts = jnp.arange(winner.shape[0], dtype=jnp.int32)
    picks = (winner[:, None] == ids[None, :]).astype(jnp.float32)
    member = (query_prompt[None, :] == prompts[:, None]).astype(jnp.float32)
    weights = (picks - member / BEST).astype(jnp.bfloat16)
    advantage = jnp.dot(weights, scores, preferred_element_type=jnp.float32)
    return (scores, advantage.astype(jnp.bfloat16))


def solution(mesh):
    return jax.shard_map(
        shards,
        mesh=mesh,
        in_specs=(
            P("layer", ("grp", "ex"), None),
            P("layer", ("grp", "ex"), None),
            P("layer", None, None),
            P("layer", None, None),
            P("grp"),
            P("grp"),
        ),
        out_specs=(P(None, ("grp", "ex")), P(None, ("grp", "ex"))),
        check_vma=False,
    )
```

```python
import functools

import jax
import jax.numpy as jnp
from jax import lax
from jax.experimental import pallas as pl
from jax.experimental.pallas import tpu as pltpu
from jax.sharding import PartitionSpec as P

KIN = 32
KOUT = 128
BEST = 4
ROWS = 8
WIDE = KIN * ROWS
PAIR = 2 * KOUT
DEPTH_BLOCK = 512
COLUMNS = 512
COPY_ROWS = 32
VMEM_LIMIT = 32 * 1024 * 1024
NT = (((1,), (1,)), ((), ()))


def left_matrix(left):
    row = lax.broadcasted_iota(jnp.int32, (WIDE, KIN), 0)
    column = lax.broadcasted_iota(jnp.int32, (WIDE, KIN), 1)
    spread = jnp.where((row >> 3) == column, 1.0, 0.0).astype(jnp.bfloat16)
    tall = jnp.dot(spread, left, preferred_element_type=jnp.float32).astype(jnp.bfloat16)
    full = lax.dot_general(tall, spread, NT, preferred_element_type=jnp.float32)
    row = lax.broadcasted_iota(jnp.int32, (WIDE, WIDE), 0)
    column = lax.broadcasted_iota(jnp.int32, (WIDE, WIDE), 1)
    return jnp.where((row & (ROWS - 1)) == (column & (ROWS - 1)), full, 0.0).astype(jnp.bfloat16)


def right_matrix(right):
    zero = jnp.zeros_like(right)
    return jnp.concatenate(
        [jnp.concatenate([right, zero], 1), jnp.concatenate([zero, right], 1)], 0
    )


def side_by_side_to_stacked(block):
    tiles = block.reshape(block.shape[0] // ROWS, ROWS, PAIR)
    return jnp.concatenate([tiles[:, :, :KOUT], tiles[:, :, KOUT:]], 1)


def precondition(rows_ref, left, right, half_ref, pre_ref):
    count = rows_ref.shape[0]
    both = right_matrix(right)
    together = 4
    for start in range(0, KIN // 2, together):
        block = jnp.concatenate(
            [rows_ref[:, p * PAIR : (p + 1) * PAIR] for p in range(start, start + together)], 0
        )
        half = jnp.dot(block, both, preferred_element_type=jnp.float32)
        for k in range(together):
            at = 2 * ROWS * (start + k)
            half_ref[:, at : at + 2 * ROWS, :] = side_by_side_to_stacked(
                half[k * count : (k + 1) * count]
            ).astype(jnp.bfloat16)
    mixer = left_matrix(left)

    def groups(index, carry):
        stacked = jnp.concatenate([half_ref[2 * index], half_ref[2 * index + 1]], 1)
        mixed = side_by_side_to_stacked(
            jnp.dot(mixer, stacked, preferred_element_type=jnp.float32)
        ).astype(jnp.bfloat16)
        at = pl.ds(pl.multiple_of(index * 2 * ROWS, 2 * ROWS), 2 * ROWS)
        for i in range(KIN):
            pre_ref[at, i * KOUT : (i + 1) * KOUT] = mixed[i]
        return carry

    lax.fori_loop(0, count // (2 * ROWS), groups, 0, unroll=4)


def dot(pre_ref, store_ref, first, total_ref, out_ref):
    depth = pre_ref.shape[1]
    columns = total_ref.shape[0]
    for at in range(0, depth, DEPTH_BLOCK):
        block = slice(at, at + DEPTH_BLOCK)
        term = lax.dot_general(
            store_ref[first : first + columns, block],
            pre_ref[:, block],
            NT,
            preferred_element_type=jnp.float32,
        )
        if at == 0:
            total_ref[...] = term
        elif at + DEPTH_BLOCK < depth:
            total_ref[...] += term
        else:
            out_ref[...] = (total_ref[...] + term).T


def copies_of(source_ref, target_ref, sems):
    rows = target_ref.shape[0] // sems.shape[0]
    return [
        pltpu.make_async_copy(
            source_ref.at[0, pl.ds(k * rows, rows)], target_ref.at[pl.ds(k * rows, rows)], sems.at[k]
        )
        for k in range(sems.shape[0])
    ]


def score_kernel(
    rows_ref, left_ref, right_ref, store_ref, *refs,
):
    *out_refs, left_vmem, right_vmem, rows_vmem, store_vmem, half_ref, total_ref = refs[:-4]
    left_sems, right_sems, rows_sems, store_sems = refs[-4:]
    heads = (
        copies_of(right_ref, right_vmem, right_sems)
        + copies_of(left_ref, left_vmem, left_sems)
        + copies_of(rows_ref, rows_vmem, rows_sems)
    )
    copies = copies_of(store_ref, store_vmem, store_sems)
    for copy in heads + copies:
        copy.start()
    for copy in heads:
        copy.wait()
    pre_ref = rows_vmem
    precondition(rows_vmem, left_vmem[...], right_vmem[...], half_ref, pre_ref)
    share = len(copies) // len(out_refs)
    columns = total_ref.shape[0]
    for k, out_ref in enumerate(out_refs):
        for copy in copies[k * share : (k + 1) * share]:
            copy.wait()
        dot(pre_ref, store_vmem, k * columns, total_ref, out_ref)


VMEM = pl.BlockSpec(memory_space=pltpu.VMEM)
HBM = pl.BlockSpec(memory_space=pltpu.HBM)
ANYWHERE = pl.BlockSpec(memory_space=pl.ANY)


def in_hbm(array):
    return pltpu.with_memory_space_constraint(array, pltpu.HBM)


def score(queries, left_inv, right_inv, store, columns):
    count, depth = queries.shape[1:]
    examples = store.shape[1]
    blocks = examples // columns
    return pl.pallas_call(
        score_kernel,
        out_shape=(pltpu.VMEM((count, columns), jnp.float32),) * blocks,
        in_specs=[ANYWHERE] + [HBM] * 3,
        out_specs=(VMEM,) * blocks,
        scratch_shapes=[
            pltpu.VMEM((KIN, KIN), jnp.bfloat16),
            pltpu.VMEM((KOUT, KOUT), jnp.bfloat16),
            pltpu.VMEM((count, depth), jnp.bfloat16),
            pltpu.VMEM((examples, depth), jnp.bfloat16),
            pltpu.VMEM((count // ROWS, WIDE, KOUT), jnp.bfloat16),
            pltpu.VMEM((columns, count), jnp.float32),
            pltpu.SemaphoreType.DMA((1,)),
            pltpu.SemaphoreType.DMA((1,)),
            pltpu.SemaphoreType.DMA((count // COPY_ROWS,)),
            pltpu.SemaphoreType.DMA((examples // COPY_ROWS,)),
        ],
        compiler_params=pltpu.CompilerParams(vmem_limit_bytes=VMEM_LIMIT),
        cost_estimate=pl.CostEstimate(
            flops=2 * count * depth * (examples + 1024),
            bytes_accessed=2 * depth * (2 * count + examples),
            transcendentals=0,
        ),
    )(queries, *map(in_hbm, (left_inv, right_inv, store)))


def swap(block, bit):
    route = [(i, i ^ bit) for i in range(lax.axis_size("layer"))]
    return lax.ppermute(block, "layer", route)


HALVE, EXCHANGE, DOUBLE = range(3)


class LayerSum:
    def __init__(self, block, bits, index):
        self.block, self.index = block, index
        self.moves = [(bit, HALVE) for bit in bits[:-1]]
        self.moves += [(bit, EXCHANGE) for bit in bits[-1:]]
        self.moves += [(bit, DOUBLE) for bit in reversed(bits[:-1])]
        if len(bits) < 2:
            self.block = block.astype(jnp.bfloat16)

    def send(self, order):
        bit, kind = self.moves[0]
        sent = self.block
        if kind == HALVE:
            rows = self.block.shape[0] // 2
            upper = (self.index & bit) // bit
            sent = lax.dynamic_slice_in_dim(self.block, (1 - upper) * rows, rows, 0)
            sent = sent.astype(jnp.bfloat16)
            self.block = lax.dynamic_slice_in_dim(self.block, upper * rows, rows, 0)
        self.received = swap(order.after(sent), bit)

    def take(self, order):
        bit, kind = self.moves.pop(0)
        received = order.mark(self.received)
        mine = self.block
        if kind == DOUBLE:
            low = (self.index & bit) == 0
            self.block = jnp.concatenate(
                [jnp.where(low, mine, received), jnp.where(low, received, mine)], 0
            )
            return
        self.block = mine.astype(jnp.float32) + received.astype(jnp.float32)
        if not (self.moves and self.moves[0][1] == HALVE):
            self.block = self.block.astype(jnp.bfloat16)


class Order:
    def __init__(self):
        self.last = jnp.zeros((), jnp.float32)

    def after(self, value):
        value, _ = lax.optimization_barrier((value, self.last))
        return value

    def mark(self, value):
        value, self.last = lax.optimization_barrier((value, self.last))
        return value


STEP_US = 1.7
BYTES_PER_US = 50000


def step_times(size, bits):
    at, sent = 0.0, size
    sizes = []
    for _ in range(bits - 1):
        sent //= 2
        sizes.append(sent)
    for size in sizes + [sent] + sizes[::-1]:
        at += STEP_US + 2 * size / BYTES_PER_US
        yield at


def sum_layers(makers, bits, index):
    order = Order()
    chunks = {}
    events = []
    for number, (start, ready, size, _) in enumerate(makers):
        events.append((start, number))
        events.extend((ready + 2 + at, number) for at in step_times(size, len(bits)) if bits)
    for _, number in sorted(events):
        if number not in chunks:
            chunk = chunks[number] = LayerSum(makers[number][3](order), bits, index)
        else:
            chunk = chunks[number]
            chunk.take(order)
        if chunk.moves:
            chunk.send(order)
    return [chunks[number].block for number in range(len(makers))]


def shards(store, queries, left_inv, right_inv, query_prompt, winner):
    rows = queries.shape[1]
    columns = store.shape[1]
    width = min(COLUMNS, columns)
    ex_count = lax.axis_size("ex")
    position = lax.axis_index("ex")
    places, makers = [], []
    current = queries
    for step in range(ex_count):
        if step > 0:
            route = [((i - 1) % ex_count, i) for i in range(ex_count)]
            current = lax.ppermute(current, "ex", route)
        made = []
        for number, first in enumerate(range(0, columns, width)):

            def make(order, number=number, step=step, current=current, made=made):
                if number == 0:
                    block = order.after(current) if step else in_hbm(current)
                    made.extend(score(block, left_inv, right_inv, store, width))
                    if step:
                        made[0] = order.mark(made[0])
                return made[number]

            makers.append((6.0 + 2.0 * step, 6.0 + 7.0 * step, rows * width, make))
            places.append(((position - step) % ex_count * rows, jnp.int32(first)))
    count = lax.axis_size("layer")
    bits = [1 << k for k in range(count.bit_length() - 1)]
    done = sum_layers(makers, bits, lax.axis_index("layer"))
    scores = jnp.zeros((rows * ex_count, columns), jnp.bfloat16)
    for place, block in zip(places, done):
        scores = lax.dynamic_update_slice(scores, block, place)
    ids = jnp.arange(scores.shape[0], dtype=jnp.int32)
    prompts = jnp.arange(winner.shape[0], dtype=jnp.int32)
    picks = (winner[:, None] == ids[None, :]).astype(jnp.float32)
    member = (query_prompt[None, :] == prompts[:, None]).astype(jnp.float32)
    weights = (picks - member / BEST).astype(jnp.bfloat16)
    advantage = jnp.dot(weights, scores, preferred_element_type=jnp.float32)
    return (scores, advantage.astype(jnp.bfloat16))


def solution(mesh):
    return jax.shard_map(
        shards,
        mesh=mesh,
        in_specs=(
            P("layer", ("grp", "ex"), None),
            P("layer", ("grp", "ex"), None),
            P("layer", None, None),
            P("layer", None, None),
            P("grp"),
            P("grp"),
        ),
        out_specs=(P(None, ("grp", "ex")), P(None, ("grp", "ex"))),
        check_vma=False,
    )
```

```python
import functools

import jax
import jax.numpy as jnp
from jax import lax
from jax.experimental import pallas as pl
from jax.experimental.pallas import tpu as pltpu
from jax.sharding import PartitionSpec as P

KIN = 32
KOUT = 128
BEST = 4
ROWS = 8
WIDE = KIN * ROWS
PAIR = 2 * KOUT
DEPTH_BLOCK = 512
COLUMNS = 512
COPY_ROWS = 32
QUEUES = 2
VMEM_LIMIT = 32 * 1024 * 1024
NT = (((1,), (1,)), ((), ()))


def left_matrix(left):
    row = lax.broadcasted_iota(jnp.int32, (WIDE, KIN), 0)
    column = lax.broadcasted_iota(jnp.int32, (WIDE, KIN), 1)
    spread = jnp.where((row >> 3) == column, 1.0, 0.0).astype(jnp.bfloat16)
    tall = jnp.dot(spread, left, preferred_element_type=jnp.float32).astype(jnp.bfloat16)
    full = lax.dot_general(tall, spread, NT, preferred_element_type=jnp.float32)
    row = lax.broadcasted_iota(jnp.int32, (WIDE, WIDE), 0)
    column = lax.broadcasted_iota(jnp.int32, (WIDE, WIDE), 1)
    return jnp.where((row & (ROWS - 1)) == (column & (ROWS - 1)), full, 0.0).astype(jnp.bfloat16)


def right_matrix(right):
    zero = jnp.zeros_like(right)
    return jnp.concatenate(
        [jnp.concatenate([right, zero], 1), jnp.concatenate([zero, right], 1)], 0
    )


def side_by_side_to_stacked(block):
    tiles = block.reshape(block.shape[0] // ROWS, ROWS, PAIR)
    return jnp.concatenate([tiles[:, :, :KOUT], tiles[:, :, KOUT:]], 1)


def precondition(rows_ref, left, right, half_ref, pre_ref):
    count = rows_ref.shape[0]
    both = right_matrix(right)
    together = 4
    for start in range(0, KIN // 2, together):
        block = jnp.concatenate(
            [rows_ref[:, p * PAIR : (p + 1) * PAIR] for p in range(start, start + together)], 0
        )
        half = jnp.dot(block, both, preferred_element_type=jnp.float32)
        for k in range(together):
            at = 2 * ROWS * (start + k)
            half_ref[:, at : at + 2 * ROWS, :] = side_by_side_to_stacked(
                half[k * count : (k + 1) * count]
            ).astype(jnp.bfloat16)
    mixer = left_matrix(left)

    def groups(index, carry):
        stacked = jnp.concatenate([half_ref[2 * index], half_ref[2 * index + 1]], 1)
        mixed = side_by_side_to_stacked(
            jnp.dot(mixer, stacked, preferred_element_type=jnp.float32)
        ).astype(jnp.bfloat16)
        at = pl.ds(pl.multiple_of(index * 2 * ROWS, 2 * ROWS), 2 * ROWS)
        for i in range(KIN):
            pre_ref[at, i * KOUT : (i + 1) * KOUT] = mixed[i]
        return carry

    lax.fori_loop(0, count // (2 * ROWS), groups, 0, unroll=4)


def dot(pre_ref, store_ref, first, total_ref, out_ref):
    depth = pre_ref.shape[1]
    columns = total_ref.shape[0]
    for at in range(0, depth, DEPTH_BLOCK):
        block = slice(at, at + DEPTH_BLOCK)
        term = lax.dot_general(
            store_ref[first : first + columns, block],
            pre_ref[:, block],
            NT,
            preferred_element_type=jnp.float32,
        )
        if at == 0:
            total_ref[...] = term
        elif at + DEPTH_BLOCK < depth:
            total_ref[...] += term
        else:
            out_ref[...] = (total_ref[...] + term).T


def copies_of(source_ref, target_ref, sems):
    rows = target_ref.shape[0] // sems.shape[0]
    return [
        pltpu.make_async_copy(
            source_ref.at[0, pl.ds(k * rows, rows)], target_ref.at[pl.ds(k * rows, rows)], sems.at[k]
        )
        for k in range(sems.shape[0])
    ]


def score_kernel(
    fetch, rows_ref, left_ref, right_ref, store_ref, *refs,
):
    *out_refs, left_vmem, right_vmem, rows_vmem, store_vmem, half_ref, total_ref = refs[:-4]
    left_sems, right_sems, rows_sems, store_sems = refs[-4:]
    heads = (
        copies_of(right_ref, right_vmem, right_sems)
        + copies_of(left_ref, left_vmem, left_sems)
        + (copies_of(rows_ref, rows_vmem, rows_sems) if fetch else [])
    )
    copies = copies_of(store_ref, store_vmem, store_sems)
    for k, copy in enumerate(heads + copies):
        copy.start(priority=k % QUEUES)
    for copy in heads:
        copy.wait()
    pre_ref = rows_vmem
    given_ref = rows_vmem if fetch else rows_ref.at[0]
    precondition(given_ref, left_vmem[...], right_vmem[...], half_ref, pre_ref)
    share = len(copies) // len(out_refs)
    columns = total_ref.shape[0]
    for k, out_ref in enumerate(out_refs):
        for copy in copies[k * share : (k + 1) * share]:
            copy.wait()
        dot(pre_ref, store_vmem, k * columns, total_ref, out_ref)


VMEM = pl.BlockSpec(memory_space=pltpu.VMEM)
HBM = pl.BlockSpec(memory_space=pltpu.HBM)


def in_hbm(array):
    return pltpu.with_memory_space_constraint(array, pltpu.HBM)


def in_vmem(array):
    return pltpu.with_memory_space_constraint(array, pltpu.VMEM)


def score(queries, fetch, left_inv, right_inv, store, columns):
    count, depth = queries.shape[1:]
    examples = store.shape[1]
    blocks = examples // columns
    return pl.pallas_call(
        functools.partial(score_kernel, fetch),
        out_shape=(pltpu.VMEM((count, columns), jnp.float32),) * blocks,
        in_specs=[HBM if fetch else VMEM] + [HBM] * 3,
        out_specs=(VMEM,) * blocks,
        scratch_shapes=[
            pltpu.VMEM((KIN, KIN), jnp.bfloat16),
            pltpu.VMEM((KOUT, KOUT), jnp.bfloat16),
            pltpu.VMEM((count, depth), jnp.bfloat16),
            pltpu.VMEM((examples, depth), jnp.bfloat16),
            pltpu.VMEM((count // ROWS, WIDE, KOUT), jnp.bfloat16),
            pltpu.VMEM((columns, count), jnp.float32),
            pltpu.SemaphoreType.DMA((1,)),
            pltpu.SemaphoreType.DMA((1,)),
            pltpu.SemaphoreType.DMA((count // COPY_ROWS,)),
            pltpu.SemaphoreType.DMA((examples // COPY_ROWS,)),
        ],
        compiler_params=pltpu.CompilerParams(vmem_limit_bytes=VMEM_LIMIT),
        cost_estimate=pl.CostEstimate(
            flops=2 * count * depth * (examples + 1024),
            bytes_accessed=2 * depth * (2 * count + examples),
            transcendentals=0,
        ),
    )(in_hbm(queries) if fetch else in_vmem(queries), *map(in_hbm, (left_inv, right_inv, store)))


def swap(block, bit):
    route = [(i, i ^ bit) for i in range(lax.axis_size("layer"))]
    return lax.ppermute(block, "layer", route)


HALVE, EXCHANGE, DOUBLE = range(3)


class LayerSum:
    def __init__(self, block, bits, index):
        self.block, self.index = block, index
        self.moves = [(bit, HALVE) for bit in bits[:-1]]
        self.moves += [(bit, EXCHANGE) for bit in bits[-1:]]
        self.moves += [(bit, DOUBLE) for bit in reversed(bits[:-1])]
        if len(bits) < 2:
            self.block = block.astype(jnp.bfloat16)

    def send(self, order):
        bit, kind = self.moves[0]
        sent = self.block
        if kind == HALVE:
            rows = self.block.shape[0] // 2
            upper = (self.index & bit) // bit
            sent = lax.dynamic_slice_in_dim(self.block, (1 - upper) * rows, rows, 0)
            sent = sent.astype(jnp.bfloat16)
            self.block = lax.dynamic_slice_in_dim(self.block, upper * rows, rows, 0)
        self.received = swap(order.after(sent), bit)

    def take(self, order):
        bit, kind = self.moves.pop(0)
        received = order.mark(self.received)
        mine = self.block
        if kind == DOUBLE:
            low = (self.index & bit) == 0
            self.block = jnp.concatenate(
                [jnp.where(low, mine, received), jnp.where(low, received, mine)], 0
            )
            return
        self.block = mine.astype(jnp.float32) + received.astype(jnp.float32)
        if not (self.moves and self.moves[0][1] == HALVE):
            self.block = self.block.astype(jnp.bfloat16)


class Order:
    def __init__(self):
        self.last = jnp.zeros((), jnp.float32)

    def after(self, value):
        value, _ = lax.optimization_barrier((value, self.last))
        return value

    def mark(self, value):
        value, self.last = lax.optimization_barrier((value, self.last))
        return value


STEP_US = 1.7
BYTES_PER_US = 50000


def step_times(size, bits):
    at, sent = 0.0, size
    sizes = []
    for _ in range(bits - 1):
        sent //= 2
        sizes.append(sent)
    for size in sizes + [sent] + sizes[::-1]:
        at += STEP_US + 2 * size / BYTES_PER_US
        yield at


def sum_layers(makers, bits, index):
    order = Order()
    chunks = {}
    events = []
    for number, (start, ready, size, _) in enumerate(makers):
        events.append((start, number))
        events.extend((ready + 2 + at, number) for at in step_times(size, len(bits)) if bits)
    for _, number in sorted(events):
        if number not in chunks:
            chunk = chunks[number] = LayerSum(makers[number][3](order), bits, index)
        else:
            chunk = chunks[number]
            chunk.take(order)
        if chunk.moves:
            chunk.send(order)
    return [chunks[number].block for number in range(len(makers))]


def shards(store, queries, left_inv, right_inv, query_prompt, winner):
    rows = queries.shape[1]
    columns = store.shape[1]
    width = min(COLUMNS, columns)
    ex_count = lax.axis_size("ex")
    position = lax.axis_index("ex")
    places, makers = [], []
    current = queries
    for step in range(ex_count):
        if step > 0:
            route = [((i - 1) % ex_count, i) for i in range(ex_count)]
            current = lax.ppermute(current, "ex", route)
        made = []
        for number, first in enumerate(range(0, columns, width)):

            def make(order, number=number, step=step, current=current, made=made):
                if number == 0:
                    block = order.after(current) if step else current
                    made.extend(score(block, step == 0, left_inv, right_inv, store, width))
                    if step:
                        made[0] = order.mark(made[0])
                return made[number]

            makers.append((6.0 + 2.0 * step, 6.0 + 7.0 * step, rows * width, make))
            places.append(((position - step) % ex_count * rows, jnp.int32(first)))
    count = lax.axis_size("layer")
    bits = [1 << k for k in range(count.bit_length() - 1)]
    done = sum_layers(makers, bits, lax.axis_index("layer"))
    scores = jnp.zeros((rows * ex_count, columns), jnp.bfloat16)
    for place, block in zip(places, done):
        scores = lax.dynamic_update_slice(scores, block, place)
    ids = jnp.arange(scores.shape[0], dtype=jnp.int32)
    prompts = jnp.arange(winner.shape[0], dtype=jnp.int32)
    picks = (winner[:, None] == ids[None, :]).astype(jnp.float32)
    member = (query_prompt[None, :] == prompts[:, None]).astype(jnp.float32)
    weights = (picks - member / BEST).astype(jnp.bfloat16)
    advantage = jnp.dot(weights, scores, preferred_element_type=jnp.float32)
    return (scores, advantage.astype(jnp.bfloat16))


def solution(mesh):
    return jax.shard_map(
        shards,
        mesh=mesh,
        in_specs=(
            P("layer", ("grp", "ex"), None),
            P("layer", ("grp", "ex"), None),
            P("layer", None, None),
            P("layer", None, None),
            P("grp"),
            P("grp"),
        ),
        out_specs=(P(None, ("grp", "ex")), P(None, ("grp", "ex"))),
        check_vma=False,
    )
```

```python
import functools

import jax
import jax.numpy as jnp
from jax import lax
from jax.experimental import pallas as pl
from jax.experimental.pallas import tpu as pltpu
from jax.sharding import PartitionSpec as P

KIN = 32
KOUT = 128
BEST = 4
ROWS = 8
WIDE = KIN * ROWS
PAIR = 2 * KOUT
DEPTH_BLOCK = 512
COLUMNS = 512
VMEM_LIMIT = 28 * 1024 * 1024
NT = (((1,), (1,)), ((), ()))


def left_matrix(left):
    row = lax.broadcasted_iota(jnp.int32, (WIDE, KIN), 0)
    column = lax.broadcasted_iota(jnp.int32, (WIDE, KIN), 1)
    spread = jnp.where((row >> 3) == column, 1.0, 0.0).astype(jnp.bfloat16)
    tall = jnp.dot(spread, left, preferred_element_type=jnp.float32).astype(jnp.bfloat16)
    full = lax.dot_general(tall, spread, NT, preferred_element_type=jnp.float32)
    row = lax.broadcasted_iota(jnp.int32, (WIDE, WIDE), 0)
    column = lax.broadcasted_iota(jnp.int32, (WIDE, WIDE), 1)
    return jnp.where((row & (ROWS - 1)) == (column & (ROWS - 1)), full, 0.0).astype(jnp.bfloat16)


def right_matrix(right):
    zero = jnp.zeros_like(right)
    return jnp.concatenate(
        [jnp.concatenate([right, zero], 1), jnp.concatenate([zero, right], 1)], 0
    )


def side_by_side_to_stacked(block):
    tiles = block.reshape(block.shape[0] // ROWS, ROWS, PAIR)
    return jnp.concatenate([tiles[:, :, :KOUT], tiles[:, :, KOUT:]], 1)


def precondition(rows_ref, left, right, half_ref, pre_ref):
    count = rows_ref.shape[0]
    both = right_matrix(right)
    together = 4
    for start in range(0, KIN // 2, together):
        block = jnp.concatenate(
            [rows_ref[:, p * PAIR : (p + 1) * PAIR] for p in range(start, start + together)], 0
        )
        half = jnp.dot(block, both, preferred_element_type=jnp.float32)
        for k in range(together):
            at = 2 * ROWS * (start + k)
            half_ref[:, at : at + 2 * ROWS, :] = side_by_side_to_stacked(
                half[k * count : (k + 1) * count]
            ).astype(jnp.bfloat16)
    mixer = left_matrix(left)

    def groups(index, carry):
        stacked = jnp.concatenate([half_ref[2 * index], half_ref[2 * index + 1]], 1)
        mixed = side_by_side_to_stacked(
            jnp.dot(mixer, stacked, preferred_element_type=jnp.float32)
        ).astype(jnp.bfloat16)
        at = pl.ds(pl.multiple_of(index * 2 * ROWS, 2 * ROWS), 2 * ROWS)
        for i in range(KIN):
            pre_ref[at, i * KOUT : (i + 1) * KOUT] = mixed[i]
        return carry

    lax.fori_loop(0, count // (2 * ROWS), groups, 0, unroll=4)


def dot(pre_ref, store_ref, first, total_ref, out_ref):
    depth = pre_ref.shape[1]
    columns = total_ref.shape[0]
    for at in range(0, depth, DEPTH_BLOCK):
        block = slice(at, at + DEPTH_BLOCK)
        term = lax.dot_general(
            store_ref[first : first + columns, block],
            pre_ref[:, block],
            NT,
            preferred_element_type=jnp.float32,
        )
        if at == 0:
            total_ref[...] = term
        elif at + DEPTH_BLOCK < depth:
            total_ref[...] += term
        else:
            out_ref[...] = (total_ref[...] + term).T


def precondition_kernel(rows_ref, left_ref, right_ref, pre_ref, left_vmem, right_vmem, half_ref, sems):
    heads = [
        pltpu.make_async_copy(source.at[0], target, sems.at[k])
        for k, (source, target) in enumerate(((right_ref, right_vmem), (left_ref, left_vmem)))
    ]
    for copy in heads:
        copy.start()
    for copy in heads:
        copy.wait()
    precondition(rows_ref.at[0], left_vmem[...], right_vmem[...], half_ref, pre_ref)


def score_kernel(pre_ref, store_ref, *refs):
    *out_refs, total_ref = refs
    columns = total_ref.shape[0]
    for k, out_ref in enumerate(out_refs):
        dot(pre_ref, store_ref.at[0], k * columns, total_ref, out_ref)


VMEM = pl.BlockSpec(memory_space=pltpu.VMEM)
HBM = pl.BlockSpec(memory_space=pltpu.HBM)


def in_hbm(array):
    return pltpu.with_memory_space_constraint(array, pltpu.HBM)


def preconditioned(queries, left_inv, right_inv):
    count, depth = queries.shape[1:]
    return pl.pallas_call(
        precondition_kernel,
        out_shape=jax.ShapeDtypeStruct((count, depth), jnp.bfloat16),
        in_specs=[VMEM, HBM, HBM],
        out_specs=VMEM,
        scratch_shapes=[
            pltpu.VMEM((KIN, KIN), jnp.bfloat16),
            pltpu.VMEM((KOUT, KOUT), jnp.bfloat16),
            pltpu.VMEM((count // ROWS, WIDE, KOUT), jnp.bfloat16),
            pltpu.SemaphoreType.DMA((2,)),
        ],
        compiler_params=pltpu.CompilerParams(vmem_limit_bytes=VMEM_LIMIT),
        cost_estimate=pl.CostEstimate(
            flops=2 * count * depth * 1024, bytes_accessed=4 * depth * count, transcendentals=0
        ),
    )(queries, in_hbm(left_inv), in_hbm(right_inv))


def score(pre, store, columns):
    count, depth = pre.shape
    examples = store.shape[1]
    blocks = examples // columns
    return pl.pallas_call(
        score_kernel,
        out_shape=(jax.ShapeDtypeStruct((count, columns), jnp.float32),) * blocks,
        in_specs=[VMEM] * 2,
        out_specs=(VMEM,) * blocks,
        scratch_shapes=[pltpu.VMEM((columns, count), jnp.float32)],
        compiler_params=pltpu.CompilerParams(vmem_limit_bytes=VMEM_LIMIT),
        cost_estimate=pl.CostEstimate(
            flops=2 * count * depth * examples,
            bytes_accessed=2 * depth * (count + examples),
            transcendentals=0,
        ),
    )(pre, store)


def swap(block, bit):
    route = [(i, i ^ bit) for i in range(lax.axis_size("layer"))]
    return lax.ppermute(block, "layer", route)


HALVE, EXCHANGE, DOUBLE = range(3)


class LayerSum:
    def __init__(self, block, bits, index):
        self.block, self.index = block, index
        self.moves = [(bit, HALVE) for bit in bits[:-1]]
        self.moves += [(bit, EXCHANGE) for bit in bits[-1:]]
        self.moves += [(bit, DOUBLE) for bit in reversed(bits[:-1])]
        if len(bits) < 2:
            self.block = block.astype(jnp.bfloat16)

    def send(self, order):
        bit, kind = self.moves[0]
        sent = self.block
        if kind == HALVE:
            rows = self.block.shape[0] // 2
            upper = (self.index & bit) // bit
            sent = lax.dynamic_slice_in_dim(self.block, (1 - upper) * rows, rows, 0)
            sent = sent.astype(jnp.bfloat16)
            self.block = lax.dynamic_slice_in_dim(self.block, upper * rows, rows, 0)
        self.received = swap(order.after(sent), bit)

    def take(self, order):
        bit, kind = self.moves.pop(0)
        received = order.mark(self.received)
        mine = self.block
        if kind == DOUBLE:
            low = (self.index & bit) == 0
            self.block = jnp.concatenate(
                [jnp.where(low, mine, received), jnp.where(low, received, mine)], 0
            )
            return
        self.block = mine.astype(jnp.float32) + received.astype(jnp.float32)
        if not (self.moves and self.moves[0][1] == HALVE):
            self.block = self.block.astype(jnp.bfloat16)


class Order:
    def __init__(self):
        self.last = jnp.zeros((), jnp.float32)

    def after(self, value):
        value, _ = lax.optimization_barrier((value, self.last))
        return value

    def mark(self, value):
        value, self.last = lax.optimization_barrier((value, self.last))
        return value


STEP_US = 1.7
BYTES_PER_US = 50000


def step_times(size, bits):
    at, sent = 0.0, size
    sizes = []
    for _ in range(bits - 1):
        sent //= 2
        sizes.append(sent)
    for size in sizes + [sent] + sizes[::-1]:
        at += STEP_US + 2 * size / BYTES_PER_US
        yield at


def sum_layers(makers, bits, index):
    order = Order()
    chunks = {}
    events = []
    for number, (start, ready, size, _) in enumerate(makers):
        events.append((start, number))
        events.extend((ready + 2 + at, number) for at in step_times(size, len(bits)) if bits)
    for _, number in sorted(events):
        if number not in chunks:
            chunk = chunks[number] = LayerSum(makers[number][3](order), bits, index)
        else:
            chunk = chunks[number]
            chunk.take(order)
        if chunk.moves:
            chunk.send(order)
    return [chunks[number].block for number in range(len(makers))]


def shards(store, queries, left_inv, right_inv, query_prompt, winner):
    rows = queries.shape[1]
    columns = store.shape[1]
    width = min(COLUMNS, columns)
    ex_count = lax.axis_size("ex")
    position = lax.axis_index("ex")
    places, makers = [], []
    current = preconditioned(queries, left_inv, right_inv)
    for step in range(ex_count):
        if step > 0:
            route = [((i - 1) % ex_count, i) for i in range(ex_count)]
            current = lax.ppermute(current, "ex", route)
        made = []
        for number, first in enumerate(range(0, columns, width)):

            def make(order, number=number, step=step, current=current, made=made):
                if number == 0:
                    block = order.after(current) if step else current
                    made.extend(score(block, store, width))
                    if step:
                        made[0] = order.mark(made[0])
                return made[number]

            makers.append((6.0 + 2.0 * step, 6.0 + 7.0 * step, rows * width, make))
            places.append(((position - step) % ex_count * rows, jnp.int32(first)))
    count = lax.axis_size("layer")
    bits = [1 << k for k in range(count.bit_length() - 1)]
    done = sum_layers(makers, bits, lax.axis_index("layer"))
    scores = jnp.zeros((rows * ex_count, columns), jnp.bfloat16)
    for place, block in zip(places, done):
        scores = lax.dynamic_update_slice(scores, block, place)
    ids = jnp.arange(scores.shape[0], dtype=jnp.int32)
    prompts = jnp.arange(winner.shape[0], dtype=jnp.int32)
    picks = (winner[:, None] == ids[None, :]).astype(jnp.float32)
    member = (query_prompt[None, :] == prompts[:, None]).astype(jnp.float32)
    weights = (picks - member / BEST).astype(jnp.bfloat16)
    advantage = jnp.dot(weights, scores, preferred_element_type=jnp.float32)
    return (scores, advantage.astype(jnp.bfloat16))


def solution(mesh):
    return jax.shard_map(
        shards,
        mesh=mesh,
        in_specs=(
            P("layer", ("grp", "ex"), None),
            P("layer", ("grp", "ex"), None),
            P("layer", None, None),
            P("layer", None, None),
            P("grp"),
            P("grp"),
        ),
        out_specs=(P(None, ("grp", "ex")), P(None, ("grp", "ex"))),
        check_vma=False,
    )
```

```python
import functools

import jax
import jax.numpy as jnp
from jax import lax
from jax.experimental import pallas as pl
from jax.experimental.pallas import tpu as pltpu
from jax.sharding import PartitionSpec as P

KIN = 32
KOUT = 128
BEST = 4
ROWS = 8
WIDE = KIN * ROWS
PAIR = 2 * KOUT
DEPTH_BLOCK = 1024
TOGETHER = 4
COLUMNS = 512
CUTS = ((False,), (True, True))
VMEM_LIMIT = 32 * 1024 * 1024
NT = (((1,), (1,)), ((), ()))


def left_matrix(left):
    row = lax.broadcasted_iota(jnp.int32, (WIDE, KIN), 0)
    column = lax.broadcasted_iota(jnp.int32, (WIDE, KIN), 1)
    spread = jnp.where((row >> 3) == column, 1.0, 0.0).astype(jnp.bfloat16)
    tall = jnp.dot(spread, left, preferred_element_type=jnp.float32).astype(jnp.bfloat16)
    full = lax.dot_general(tall, spread, NT, preferred_element_type=jnp.float32)
    row = lax.broadcasted_iota(jnp.int32, (WIDE, WIDE), 0)
    column = lax.broadcasted_iota(jnp.int32, (WIDE, WIDE), 1)
    return jnp.where((row & (ROWS - 1)) == (column & (ROWS - 1)), full, 0.0).astype(jnp.bfloat16)


def right_matrix(right):
    zero = jnp.zeros_like(right)
    return jnp.concatenate(
        [jnp.concatenate([right, zero], 1), jnp.concatenate([zero, right], 1)], 0
    )


def side_by_side_to_stacked(block):
    tiles = block.reshape(block.shape[0] // ROWS, ROWS, PAIR)
    return jnp.concatenate([tiles[:, :, :KOUT], tiles[:, :, KOUT:]], 1)


def precondition(rows_ref, left, right, half_ref, pre_ref):
    count = rows_ref.shape[0]
    both = right_matrix(right)

    def pairs(step, carry):
        first = step * TOGETHER
        block = jnp.concatenate(
            [
                rows_ref[:, pl.ds(pl.multiple_of((first + k) * PAIR, PAIR), PAIR)]
                for k in range(TOGETHER)
            ],
            0,
        )
        half = jnp.dot(block, both, preferred_element_type=jnp.float32)
        for k in range(TOGETHER):
            at = pl.ds(pl.multiple_of((first + k) * 2 * ROWS, 2 * ROWS), 2 * ROWS)
            half_ref[:, at, :] = side_by_side_to_stacked(
                half[k * count : (k + 1) * count]
            ).astype(jnp.bfloat16)
        return carry

    lax.fori_loop(0, KIN // 2 // TOGETHER, pairs, 0)
    mixer = left_matrix(left)

    def groups(index, carry):
        stacked = jnp.concatenate([half_ref[2 * index], half_ref[2 * index + 1]], 1)
        mixed = side_by_side_to_stacked(
            jnp.dot(mixer, stacked, preferred_element_type=jnp.float32)
        ).astype(jnp.bfloat16)
        at = pl.ds(pl.multiple_of(index * 2 * ROWS, 2 * ROWS), 2 * ROWS)
        for i in range(KIN):
            pre_ref[at, i * KOUT : (i + 1) * KOUT] = mixed[i]
        return carry

    lax.fori_loop(0, count // (2 * ROWS), groups, 0, unroll=4)


def dot(pre_ref, store_ref, first, total_ref, out_ref):
    columns, count = total_ref.shape
    rows = pl.ds(pl.multiple_of(first, columns), columns)
    total_ref[...] = jnp.zeros_like(total_ref)

    def depth_blocks(step, carry):
        at = pl.ds(pl.multiple_of(step * DEPTH_BLOCK, DEPTH_BLOCK), DEPTH_BLOCK)
        total_ref[...] += lax.dot_general(
            store_ref[rows, at], pre_ref[:, at], NT, preferred_element_type=jnp.float32
        )
        return carry

    lax.fori_loop(0, pre_ref.shape[1] // DEPTH_BLOCK, depth_blocks, 0)
    out_ref[:, rows] = total_ref[...].T


def copies_of(source_ref, target_ref, sems):
    rows = target_ref.shape[0] // sems.shape[0]
    return [
        pltpu.make_async_copy(
            source_ref.at[0, pl.ds(k * rows, rows)], target_ref.at[pl.ds(k * rows, rows)], sems.at[k]
        )
        for k in range(sems.shape[0])
    ]


def score_kernel(
    fetch, rows_ref, left_ref, right_ref, store_ref, out_ref,
    left_vmem, right_vmem, rows_vmem, store_vmem, half_ref, total_ref,
    left_sems, right_sems, rows_sems, store_sems,
):
    heads = copies_of(right_ref, right_vmem, right_sems) + copies_of(left_ref, left_vmem, left_sems)
    if fetch:
        heads += copies_of(rows_ref, rows_vmem, rows_sems)
    copies = copies_of(store_ref, store_vmem, store_sems)
    for copy in heads + copies:
        copy.start()
    for copy in heads:
        copy.wait()
    given_ref = rows_vmem if fetch else rows_ref.at[0]
    precondition(given_ref, left_vmem[...], right_vmem[...], half_ref, rows_vmem)
    for copy in copies:
        copy.wait()

    def blocks(step, carry):
        dot(rows_vmem, store_vmem, step * total_ref.shape[0], total_ref, out_ref)
        return carry

    lax.fori_loop(0, out_ref.shape[1] // total_ref.shape[0], blocks, 0)


VMEM = pl.BlockSpec(memory_space=pltpu.VMEM)
HBM = pl.BlockSpec(memory_space=pltpu.HBM)


def in_hbm(array):
    return pltpu.with_memory_space_constraint(array, pltpu.HBM)


def score(queries, fetch, left_inv, right_inv, store):
    count, depth = queries.shape[1:]
    examples = store.shape[1]
    return pl.pallas_call(
        functools.partial(score_kernel, fetch),
        out_shape=jax.ShapeDtypeStruct((count, examples), jnp.float32),
        in_specs=[HBM if fetch else VMEM] + [HBM] * 3,
        out_specs=VMEM,
        scratch_shapes=[
            pltpu.VMEM((KIN, KIN), jnp.bfloat16),
            pltpu.VMEM((KOUT, KOUT), jnp.bfloat16),
            pltpu.VMEM((count, depth), jnp.bfloat16),
            pltpu.VMEM((examples, depth), jnp.bfloat16),
            pltpu.VMEM((count // ROWS, WIDE, KOUT), jnp.bfloat16),
            pltpu.VMEM((min(COLUMNS, examples), count), jnp.float32),
            pltpu.SemaphoreType.DMA((1,)),
            pltpu.SemaphoreType.DMA((1,)),
            pltpu.SemaphoreType.DMA((2,)),
            pltpu.SemaphoreType.DMA((2,)),
        ],
        compiler_params=pltpu.CompilerParams(vmem_limit_bytes=VMEM_LIMIT),
        cost_estimate=pl.CostEstimate(
            flops=2 * count * depth * (examples + 1024),
            bytes_accessed=2 * depth * (count + examples),
            transcendentals=0,
        ),
    )(in_hbm(queries) if fetch else queries, *map(in_hbm, (left_inv, right_inv, store)))


def swap(block, bit):
    route = [(i, i ^ bit) for i in range(lax.axis_size("layer"))]
    return lax.ppermute(block, "layer", route)


HALVE, EXCHANGE, DOUBLE = range(3)


class LayerSum:
    def __init__(self, block, bits, index):
        self.block, self.index = block, index
        self.moves = [(bit, HALVE) for bit in bits[:-1]]
        self.moves += [(bit, EXCHANGE) for bit in bits[-1:]]
        self.moves += [(bit, DOUBLE) for bit in reversed(bits[:-1])]
        if len(bits) < 2:
            self.block = block.astype(jnp.bfloat16)

    def send(self, order):
        bit, kind = self.moves[0]
        sent = self.block
        if kind == HALVE:
            rows = self.block.shape[0] // 2
            upper = (self.index & bit) // bit
            sent = lax.dynamic_slice_in_dim(self.block, (1 - upper) * rows, rows, 0)
            sent = sent.astype(jnp.bfloat16)
            self.block = lax.dynamic_slice_in_dim(self.block, upper * rows, rows, 0)
        self.received = swap(order.after(sent), bit)

    def take(self, order):
        bit, kind = self.moves.pop(0)
        received = order.mark(self.received)
        mine = self.block
        if kind == DOUBLE:
            low = (self.index & bit) == 0
            self.block = jnp.concatenate(
                [jnp.where(low, mine, received), jnp.where(low, received, mine)], 0
            )
            return
        self.block = mine.astype(jnp.float32) + received.astype(jnp.float32)
        if not (self.moves and self.moves[0][1] == HALVE):
            self.block = self.block.astype(jnp.bfloat16)


class Order:
    def __init__(self):
        self.last = jnp.zeros((), jnp.float32)

    def after(self, value):
        value, _ = lax.optimization_barrier((value, self.last))
        return value

    def mark(self, value):
        value, self.last = lax.optimization_barrier((value, self.last))
        return value


STEP_US = 1.7
BYTES_PER_US = 50000


def step_times(size, bits):
    at, sent = 0.0, size
    sizes = []
    for _ in range(bits - 1):
        sent //= 2
        sizes.append(sent)
    for size in sizes + [sent] + sizes[::-1]:
        at += STEP_US + 2 * size / BYTES_PER_US
        yield at


def sum_layers(makers, index):
    order = Order()
    chunks = {}
    events = []
    for number, (start, ready, size, bits, _) in enumerate(makers):
        events.append((start, number))
        events.extend((ready + at, number) for at in step_times(size, len(bits)) if bits)
    for _, number in sorted(events):
        if number not in chunks:
            chunk = chunks[number] = LayerSum(makers[number][4](order), makers[number][3], index)
        else:
            chunk = chunks[number]
            chunk.take(order)
        if chunk.moves:
            chunk.send(order)
    return [chunks[number].block for number in range(len(makers))]


def shards(store, queries, left_inv, right_inv, query_prompt, winner):
    rows = queries.shape[1]
    columns = store.shape[1]
    ex_count = lax.axis_size("ex")
    position = lax.axis_index("ex")
    count = lax.axis_size("layer")
    bits = [1 << k for k in range(count.bit_length() - 1)]
    swapped = bits[1:2] + bits[:1] + bits[2:]
    places, makers = [], []
    current = queries
    for step in range(ex_count):
        if step > 0:
            route = [((i - 1) % ex_count, i) for i in range(ex_count)]
            current = lax.ppermute(current, "ex", route)
        made = []
        cuts = CUTS[min(step, len(CUTS) - 1)]
        width = columns // len(cuts)
        for number, y_first in enumerate(cuts):

            def make(order, number=number, width=width, step=step, current=current, made=made):
                if number == 0:
                    block = order.after(current) if step else current
                    part = score(block, step == 0, left_inv, right_inv, store)
                    made.append(order.mark(part) if step else part)
                return made[0][:, number * width : (number + 1) * width]

            start, ready = 6.0 + 2.0 * step, 6.0 + 7.0 * step + 1.0 * number
            makers.append((start, ready, rows * width, bits if y_first else swapped, make))
            places.append(((position - step) % ex_count * rows, jnp.int32(number * width)))
    done = sum_layers(makers, lax.axis_index("layer"))
    scores = jnp.zeros((rows * ex_count, columns), jnp.bfloat16)
    for place, block in zip(places, done):
        scores = lax.dynamic_update_slice(scores, block, place)
    ids = jnp.arange(scores.shape[0], dtype=jnp.int32)
    prompts = jnp.arange(winner.shape[0], dtype=jnp.int32)
    picks = (winner[:, None] == ids[None, :]).astype(jnp.float32)
    member = (query_prompt[None, :] == prompts[:, None]).astype(jnp.float32)
    weights = (picks - member / BEST).astype(jnp.bfloat16)
    advantage = jnp.dot(weights, scores, preferred_element_type=jnp.float32)
    return (scores, advantage.astype(jnp.bfloat16))


def solution(mesh):
    return jax.shard_map(
        shards,
        mesh=mesh,
        in_specs=(
            P("layer", ("grp", "ex"), None),
            P("layer", ("grp", "ex"), None),
            P("layer", None, None),
            P("layer", None, None),
            P("grp"),
            P("grp"),
        ),
        out_specs=(P(None, ("grp", "ex")), P(None, ("grp", "ex"))),
        check_vma=False,
    )
```

```python
import functools

import jax
import jax.numpy as jnp
from jax import lax
from jax.experimental import pallas as pl
from jax.experimental.pallas import tpu as pltpu
from jax.sharding import PartitionSpec as P

KIN = 32
KOUT = 128
BEST = 4
ROWS = 8
WIDE = KIN * ROWS
PAIR = 2 * KOUT
DEPTH_BLOCK = 1024
TOGETHER = 4
COLUMNS = 512
CUTS = ((False,), (True, True))
VMEM_LIMIT = 32 * 1024 * 1024
NT = (((1,), (1,)), ((), ()))


def left_matrix(left):
    row = lax.broadcasted_iota(jnp.int32, (WIDE, KIN), 0)
    column = lax.broadcasted_iota(jnp.int32, (WIDE, KIN), 1)
    spread = jnp.where((row >> 3) == column, 1.0, 0.0).astype(jnp.bfloat16)
    tall = jnp.dot(spread, left, preferred_element_type=jnp.float32).astype(jnp.bfloat16)
    full = lax.dot_general(tall, spread, NT, preferred_element_type=jnp.float32)
    row = lax.broadcasted_iota(jnp.int32, (WIDE, WIDE), 0)
    column = lax.broadcasted_iota(jnp.int32, (WIDE, WIDE), 1)
    return jnp.where((row & (ROWS - 1)) == (column & (ROWS - 1)), full, 0.0).astype(jnp.bfloat16)


def right_matrix(right):
    zero = jnp.zeros_like(right)
    return jnp.concatenate(
        [jnp.concatenate([right, zero], 1), jnp.concatenate([zero, right], 1)], 0
    )


def side_by_side_to_stacked(block):
    tiles = block.reshape(block.shape[0] // ROWS, ROWS, PAIR)
    return jnp.concatenate([tiles[:, :, :KOUT], tiles[:, :, KOUT:]], 1)


def precondition(rows_ref, left, right, half_ref, pre_ref):
    count = rows_ref.shape[0]
    both = right_matrix(right)

    def pairs(step, carry):
        first = step * TOGETHER
        block = jnp.concatenate(
            [
                rows_ref[:, pl.ds(pl.multiple_of((first + k) * PAIR, PAIR), PAIR)]
                for k in range(TOGETHER)
            ],
            0,
        )
        half = jnp.dot(block, both, preferred_element_type=jnp.float32)
        for k in range(TOGETHER):
            at = pl.ds(pl.multiple_of((first + k) * 2 * ROWS, 2 * ROWS), 2 * ROWS)
            half_ref[:, at, :] = side_by_side_to_stacked(
                half[k * count : (k + 1) * count]
            ).astype(jnp.bfloat16)
        return carry

    lax.fori_loop(0, KIN // 2 // TOGETHER, pairs, 0)
    mixer = left_matrix(left)

    def groups(index, carry):
        stacked = jnp.concatenate([half_ref[2 * index], half_ref[2 * index + 1]], 1)
        mixed = side_by_side_to_stacked(
            jnp.dot(mixer, stacked, preferred_element_type=jnp.float32)
        ).astype(jnp.bfloat16)
        at = pl.ds(pl.multiple_of(index * 2 * ROWS, 2 * ROWS), 2 * ROWS)
        for i in range(KIN):
            pre_ref[at, i * KOUT : (i + 1) * KOUT] = mixed[i]
        return carry

    lax.fori_loop(0, count // (2 * ROWS), groups, 0, unroll=4)


def dot(pre_ref, store_ref, first, total_ref, out_ref):
    columns, count = total_ref.shape
    rows = pl.ds(pl.multiple_of(first, columns), columns)
    total_ref[...] = jnp.zeros_like(total_ref)

    def depth_blocks(step, carry):
        at = pl.ds(pl.multiple_of(step * DEPTH_BLOCK, DEPTH_BLOCK), DEPTH_BLOCK)
        total_ref[...] += lax.dot_general(
            store_ref[rows, at], pre_ref[:, at], NT, preferred_element_type=jnp.float32
        )
        return carry

    lax.fori_loop(0, pre_ref.shape[1] // DEPTH_BLOCK, depth_blocks, 0)
    out_ref[:, rows] = total_ref[...].T


def copies_of(source_ref, target_ref, sems):
    rows = target_ref.shape[0] // sems.shape[0]
    return [
        pltpu.make_async_copy(
            source_ref.at[0, pl.ds(k * rows, rows)], target_ref.at[pl.ds(k * rows, rows)], sems.at[k]
        )
        for k in range(sems.shape[0])
    ]


def score_kernel(
    fetch, rows_ref, left_ref, right_ref, store_ref, out_ref, rows_vmem, store_vmem,
    left_vmem, right_vmem, half_ref, total_ref,
    left_sems, right_sems, rows_sems, store_sems,
):
    heads = copies_of(right_ref, right_vmem, right_sems) + copies_of(left_ref, left_vmem, left_sems)
    if fetch:
        heads += copies_of(rows_ref, rows_vmem, rows_sems)
    copies = copies_of(store_ref, store_vmem, store_sems)
    for copy in heads + copies:
        copy.start()
    for copy in heads:
        copy.wait()
    given_ref = rows_vmem if fetch else rows_ref.at[0]
    precondition(given_ref, left_vmem[...], right_vmem[...], half_ref, rows_vmem)
    for copy in copies:
        copy.wait()

    def blocks(step, carry):
        dot(rows_vmem, store_vmem, step * total_ref.shape[0], total_ref, out_ref)
        return carry

    lax.fori_loop(0, out_ref.shape[1] // total_ref.shape[0], blocks, 0)


VMEM = pl.BlockSpec(memory_space=pltpu.VMEM)
HBM = pl.BlockSpec(memory_space=pltpu.HBM)


def in_hbm(array):
    return pltpu.with_memory_space_constraint(array, pltpu.HBM)


def score(queries, fetch, left_inv, right_inv, store):
    count, depth = queries.shape[1:]
    examples = store.shape[1]
    return pl.pallas_call(
        functools.partial(score_kernel, fetch),
        out_shape=(
            pltpu.VMEM((count, examples), jnp.float32),
            pltpu.VMEM((count, depth), jnp.bfloat16),
            pltpu.VMEM((examples, depth), jnp.bfloat16),
        ),
        in_specs=[HBM if fetch else VMEM] + [HBM] * 3,
        out_specs=(VMEM,) * 3,
        scratch_shapes=[
            pltpu.VMEM((KIN, KIN), jnp.bfloat16),
            pltpu.VMEM((KOUT, KOUT), jnp.bfloat16),
            pltpu.VMEM((count // ROWS, WIDE, KOUT), jnp.bfloat16),
            pltpu.VMEM((min(COLUMNS, examples), count), jnp.float32),
            pltpu.SemaphoreType.DMA((1,)),
            pltpu.SemaphoreType.DMA((1,)),
            pltpu.SemaphoreType.DMA((2,)),
            pltpu.SemaphoreType.DMA((2,)),
        ],
        compiler_params=pltpu.CompilerParams(vmem_limit_bytes=VMEM_LIMIT),
        cost_estimate=pl.CostEstimate(
            flops=2 * count * depth * (examples + 1024),
            bytes_accessed=2 * depth * (count + examples),
            transcendentals=0,
        ),
    )(in_hbm(queries) if fetch else queries, *map(in_hbm, (left_inv, right_inv, store)))[0]


def swap(block, bit):
    route = [(i, i ^ bit) for i in range(lax.axis_size("layer"))]
    return lax.ppermute(block, "layer", route)


HALVE, EXCHANGE, DOUBLE = range(3)


class LayerSum:
    def __init__(self, block, bits, index):
        self.block, self.index = block, index
        self.moves = [(bit, HALVE) for bit in bits[:-1]]
        self.moves += [(bit, EXCHANGE) for bit in bits[-1:]]
        self.moves += [(bit, DOUBLE) for bit in reversed(bits[:-1])]
        if len(bits) < 2:
            self.block = block.astype(jnp.bfloat16)

    def send(self, order):
        bit, kind = self.moves[0]
        sent = self.block
        if kind == HALVE:
            rows = self.block.shape[0] // 2
            upper = (self.index & bit) // bit
            sent = lax.dynamic_slice_in_dim(self.block, (1 - upper) * rows, rows, 0)
            sent = sent.astype(jnp.bfloat16)
            self.block = lax.dynamic_slice_in_dim(self.block, upper * rows, rows, 0)
        self.received = swap(order.after(sent), bit)

    def take(self, order):
        bit, kind = self.moves.pop(0)
        received = order.mark(self.received)
        mine = self.block
        if kind == DOUBLE:
            low = (self.index & bit) == 0
            self.block = jnp.concatenate(
                [jnp.where(low, mine, received), jnp.where(low, received, mine)], 0
            )
            return
        self.block = mine.astype(jnp.float32) + received.astype(jnp.float32)
        if not (self.moves and self.moves[0][1] == HALVE):
            self.block = self.block.astype(jnp.bfloat16)


class Order:
    def __init__(self):
        self.last = jnp.zeros((), jnp.float32)

    def after(self, value):
        value, _ = lax.optimization_barrier((value, self.last))
        return value

    def mark(self, value):
        value, self.last = lax.optimization_barrier((value, self.last))
        return value


STEP_US = 1.7
BYTES_PER_US = 50000


def step_times(size, bits):
    at, sent = 0.0, size
    sizes = []
    for _ in range(bits - 1):
        sent //= 2
        sizes.append(sent)
    for size in sizes + [sent] + sizes[::-1]:
        at += STEP_US + 2 * size / BYTES_PER_US
        yield at


def sum_layers(makers, index):
    order = Order()
    chunks = {}
    events = []
    for number, (start, ready, size, bits, _) in enumerate(makers):
        events.append((start, number))
        events.extend((ready + at, number) for at in step_times(size, len(bits)) if bits)
    for _, number in sorted(events):
        if number not in chunks:
            chunk = chunks[number] = LayerSum(makers[number][4](order), makers[number][3], index)
        else:
            chunk = chunks[number]
            chunk.take(order)
        if chunk.moves:
            chunk.send(order)
    return [chunks[number].block for number in range(len(makers))]


def shards(store, queries, left_inv, right_inv, query_prompt, winner):
    rows = queries.shape[1]
    columns = store.shape[1]
    ex_count = lax.axis_size("ex")
    position = lax.axis_index("ex")
    count = lax.axis_size("layer")
    bits = [1 << k for k in range(count.bit_length() - 1)]
    swapped = bits[1:2] + bits[:1] + bits[2:]
    places, makers = [], []
    current = queries
    for step in range(ex_count):
        if step > 0:
            route = [((i - 1) % ex_count, i) for i in range(ex_count)]
            current = lax.ppermute(current, "ex", route)
        made = []
        cuts = CUTS[min(step, len(CUTS) - 1)]
        width = columns // len(cuts)
        for number, y_first in enumerate(cuts):

            def make(order, number=number, width=width, step=step, current=current, made=made):
                if number == 0:
                    block = order.after(current) if step else current
                    part = score(block, step == 0, left_inv, right_inv, store)
                    made.append(order.mark(part) if step else part)
                return made[0][:, number * width : (number + 1) * width]

            start, ready = 6.0 + 2.0 * step, 6.0 + 7.0 * step + 1.0 * number
            makers.append((start, ready, rows * width, bits if y_first else swapped, make))
            places.append(((position - step) % ex_count * rows, jnp.int32(number * width)))
    done = sum_layers(makers, lax.axis_index("layer"))
    scores = jnp.zeros((rows * ex_count, columns), jnp.bfloat16)
    for place, block in zip(places, done):
        scores = lax.dynamic_update_slice(scores, block, place)
    ids = jnp.arange(scores.shape[0], dtype=jnp.int32)
    prompts = jnp.arange(winner.shape[0], dtype=jnp.int32)
    picks = (winner[:, None] == ids[None, :]).astype(jnp.float32)
    member = (query_prompt[None, :] == prompts[:, None]).astype(jnp.float32)
    weights = (picks - member / BEST).astype(jnp.bfloat16)
    advantage = jnp.dot(weights, scores, preferred_element_type=jnp.float32)
    return (scores, advantage.astype(jnp.bfloat16))


def solution(mesh):
    return jax.shard_map(
        shards,
        mesh=mesh,
        in_specs=(
            P("layer", ("grp", "ex"), None),
            P("layer", ("grp", "ex"), None),
            P("layer", None, None),
            P("layer", None, None),
            P("grp"),
            P("grp"),
        ),
        out_specs=(P(None, ("grp", "ex")), P(None, ("grp", "ex"))),
        check_vma=False,
    )
```

```python
import functools

import jax
import jax.numpy as jnp
from jax import lax
from jax.experimental import pallas as pl
from jax.experimental.pallas import tpu as pltpu
from jax.sharding import PartitionSpec as P

KIN = 32
KOUT = 128
BEST = 4
ROWS = 8
WIDE = KIN * ROWS
PAIR = 2 * KOUT
DEPTH_BLOCK = 1024
TOGETHER = 4
COLUMNS = 512
CUTS = ((False,), (True, True))
VMEM_LIMIT = 16 * 1024 * 1024
NT = (((1,), (1,)), ((), ()))


def left_matrix(left):
    row = lax.broadcasted_iota(jnp.int32, (WIDE, KIN), 0)
    column = lax.broadcasted_iota(jnp.int32, (WIDE, KIN), 1)
    spread = jnp.where((row >> 3) == column, 1.0, 0.0).astype(jnp.bfloat16)
    tall = jnp.dot(spread, left, preferred_element_type=jnp.float32).astype(jnp.bfloat16)
    full = lax.dot_general(tall, spread, NT, preferred_element_type=jnp.float32)
    row = lax.broadcasted_iota(jnp.int32, (WIDE, WIDE), 0)
    column = lax.broadcasted_iota(jnp.int32, (WIDE, WIDE), 1)
    return jnp.where((row & (ROWS - 1)) == (column & (ROWS - 1)), full, 0.0).astype(jnp.bfloat16)


def right_matrix(right):
    zero = jnp.zeros_like(right)
    return jnp.concatenate(
        [jnp.concatenate([right, zero], 1), jnp.concatenate([zero, right], 1)], 0
    )


def side_by_side_to_stacked(block):
    tiles = block.reshape(block.shape[0] // ROWS, ROWS, PAIR)
    return jnp.concatenate([tiles[:, :, :KOUT], tiles[:, :, KOUT:]], 1)


def precondition(rows_ref, left, right, half_ref, pre_ref):
    count = rows_ref.shape[0]
    both = right_matrix(right)

    def pairs(step, carry):
        first = step * TOGETHER
        block = jnp.concatenate(
            [
                rows_ref[:, pl.ds(pl.multiple_of((first + k) * PAIR, PAIR), PAIR)]
                for k in range(TOGETHER)
            ],
            0,
        )
        half = jnp.dot(block, both, preferred_element_type=jnp.float32)
        for k in range(TOGETHER):
            at = pl.ds(pl.multiple_of((first + k) * 2 * ROWS, 2 * ROWS), 2 * ROWS)
            half_ref[:, at, :] = side_by_side_to_stacked(
                half[k * count : (k + 1) * count]
            ).astype(jnp.bfloat16)
        return carry

    lax.fori_loop(0, KIN // 2 // TOGETHER, pairs, 0)
    mixer = left_matrix(left)

    def groups(index, carry):
        stacked = jnp.concatenate([half_ref[2 * index], half_ref[2 * index + 1]], 1)
        mixed = side_by_side_to_stacked(
            jnp.dot(mixer, stacked, preferred_element_type=jnp.float32)
        ).astype(jnp.bfloat16)
        at = pl.ds(pl.multiple_of(index * 2 * ROWS, 2 * ROWS), 2 * ROWS)
        for i in range(KIN):
            pre_ref[at, i * KOUT : (i + 1) * KOUT] = mixed[i]
        return carry

    lax.fori_loop(0, count // (2 * ROWS), groups, 0, unroll=4)


def dot(pre_ref, store_ref, first, total_ref, out_ref):
    columns, count = total_ref.shape
    rows = pl.ds(pl.multiple_of(first, columns), columns)
    total_ref[...] = jnp.zeros_like(total_ref)

    def depth_blocks(step, carry):
        at = pl.ds(pl.multiple_of(step * DEPTH_BLOCK, DEPTH_BLOCK), DEPTH_BLOCK)
        total_ref[...] += lax.dot_general(
            store_ref[rows, at], pre_ref[:, at], NT, preferred_element_type=jnp.float32
        )
        return carry

    lax.fori_loop(0, pre_ref.shape[1] // DEPTH_BLOCK, depth_blocks, 0)
    out_ref[:, rows] = total_ref[...].T


def precondition_kernel(rows_ref, left_ref, right_ref, pre_ref, left_vmem, right_vmem, half_ref, sems):
    heads = [
        pltpu.make_async_copy(source.at[0], target, sems.at[k])
        for k, (source, target) in enumerate(((right_ref, right_vmem), (left_ref, left_vmem)))
    ]
    for copy in heads:
        copy.start()
    for copy in heads:
        copy.wait()
    precondition(rows_ref.at[0], left_vmem[...], right_vmem[...], half_ref, pre_ref)


def score_kernel(pre_ref, store_ref, out_ref, total_ref):
    def blocks(step, carry):
        dot(pre_ref, store_ref.at[0], step * total_ref.shape[0], total_ref, out_ref)
        return carry

    lax.fori_loop(0, out_ref.shape[1] // total_ref.shape[0], blocks, 0)


VMEM = pl.BlockSpec(memory_space=pltpu.VMEM)
HBM = pl.BlockSpec(memory_space=pltpu.HBM)


def in_hbm(array):
    return pltpu.with_memory_space_constraint(array, pltpu.HBM)


def preconditioned(queries, left_inv, right_inv):
    count, depth = queries.shape[1:]
    return pl.pallas_call(
        precondition_kernel,
        out_shape=jax.ShapeDtypeStruct((count, depth), jnp.bfloat16),
        in_specs=[VMEM, HBM, HBM],
        out_specs=VMEM,
        scratch_shapes=[
            pltpu.VMEM((KIN, KIN), jnp.bfloat16),
            pltpu.VMEM((KOUT, KOUT), jnp.bfloat16),
            pltpu.VMEM((count // ROWS, WIDE, KOUT), jnp.bfloat16),
            pltpu.SemaphoreType.DMA((2,)),
        ],
        compiler_params=pltpu.CompilerParams(vmem_limit_bytes=VMEM_LIMIT),
        cost_estimate=pl.CostEstimate(
            flops=2 * count * depth * 1024, bytes_accessed=4 * depth * count, transcendentals=0
        ),
    )(queries, in_hbm(left_inv), in_hbm(right_inv))


def score(pre, store):
    count, depth = pre.shape
    examples = store.shape[1]
    return pl.pallas_call(
        score_kernel,
        out_shape=jax.ShapeDtypeStruct((count, examples), jnp.float32),
        in_specs=[VMEM] * 2,
        out_specs=VMEM,
        scratch_shapes=[pltpu.VMEM((min(COLUMNS, examples), count), jnp.float32)],
        compiler_params=pltpu.CompilerParams(vmem_limit_bytes=VMEM_LIMIT),
        cost_estimate=pl.CostEstimate(
            flops=2 * count * depth * examples,
            bytes_accessed=2 * depth * (count + examples),
            transcendentals=0,
        ),
    )(pre, store)


def swap(block, bit):
    route = [(i, i ^ bit) for i in range(lax.axis_size("layer"))]
    return lax.ppermute(block, "layer", route)


HALVE, EXCHANGE, DOUBLE = range(3)


class LayerSum:
    def __init__(self, block, bits, index):
        self.block, self.index = block, index
        self.moves = [(bit, HALVE) for bit in bits[:-1]]
        self.moves += [(bit, EXCHANGE) for bit in bits[-1:]]
        self.moves += [(bit, DOUBLE) for bit in reversed(bits[:-1])]
        if len(bits) < 2:
            self.block = block.astype(jnp.bfloat16)

    def send(self, order):
        bit, kind = self.moves[0]
        sent = self.block
        if kind == HALVE:
            rows = self.block.shape[0] // 2
            upper = (self.index & bit) // bit
            sent = lax.dynamic_slice_in_dim(self.block, (1 - upper) * rows, rows, 0)
            sent = sent.astype(jnp.bfloat16)
            self.block = lax.dynamic_slice_in_dim(self.block, upper * rows, rows, 0)
        self.received = swap(order.after(sent), bit)

    def take(self, order):
        bit, kind = self.moves.pop(0)
        received = order.mark(self.received)
        mine = self.block
        if kind == DOUBLE:
            low = (self.index & bit) == 0
            self.block = jnp.concatenate(
                [jnp.where(low, mine, received), jnp.where(low, received, mine)], 0
            )
            return
        self.block = mine.astype(jnp.float32) + received.astype(jnp.float32)
        if not (self.moves and self.moves[0][1] == HALVE):
            self.block = self.block.astype(jnp.bfloat16)


class Order:
    def __init__(self):
        self.last = jnp.zeros((), jnp.float32)

    def after(self, value):
        value, _ = lax.optimization_barrier((value, self.last))
        return value

    def mark(self, value):
        value, self.last = lax.optimization_barrier((value, self.last))
        return value


STEP_US = 1.7
BYTES_PER_US = 50000


def step_times(size, bits):
    at, sent = 0.0, size
    sizes = []
    for _ in range(bits - 1):
        sent //= 2
        sizes.append(sent)
    for size in sizes + [sent] + sizes[::-1]:
        at += STEP_US + 2 * size / BYTES_PER_US
        yield at


def sum_layers(makers, index):
    order = Order()
    chunks = {}
    events = []
    for number, (start, ready, size, bits, _) in enumerate(makers):
        events.append((start, number))
        events.extend((ready + at, number) for at in step_times(size, len(bits)) if bits)
    for _, number in sorted(events):
        if number not in chunks:
            chunk = chunks[number] = LayerSum(makers[number][4](order), makers[number][3], index)
        else:
            chunk = chunks[number]
            chunk.take(order)
        if chunk.moves:
            chunk.send(order)
    return [chunks[number].block for number in range(len(makers))]


def shards(store, queries, left_inv, right_inv, query_prompt, winner):
    rows = queries.shape[1]
    columns = store.shape[1]
    ex_count = lax.axis_size("ex")
    position = lax.axis_index("ex")
    count = lax.axis_size("layer")
    bits = [1 << k for k in range(count.bit_length() - 1)]
    swapped = bits[1:2] + bits[:1] + bits[2:]
    places, makers = [], []
    current = preconditioned(queries, left_inv, right_inv)
    for step in range(ex_count):
        if step > 0:
            route = [((i - 1) % ex_count, i) for i in range(ex_count)]
            current = lax.ppermute(current, "ex", route)
        made = []
        cuts = CUTS[min(step, len(CUTS) - 1)]
        width = columns // len(cuts)
        for number, y_first in enumerate(cuts):

            def make(order, number=number, width=width, step=step, current=current, made=made):
                if number == 0:
                    block = order.after(current) if step else current
                    part = score(block, store)
                    made.append(order.mark(part) if step else part)
                return made[0][:, number * width : (number + 1) * width]

            start, ready = 6.0 + 2.0 * step, 6.0 + 7.0 * step + 1.0 * number
            makers.append((start, ready, rows * width, bits if y_first else swapped, make))
            places.append(((position - step) % ex_count * rows, jnp.int32(number * width)))
    done = sum_layers(makers, lax.axis_index("layer"))
    scores = jnp.zeros((rows * ex_count, columns), jnp.bfloat16)
    for place, block in zip(places, done):
        scores = lax.dynamic_update_slice(scores, block, place)
    ids = jnp.arange(scores.shape[0], dtype=jnp.int32)
    prompts = jnp.arange(winner.shape[0], dtype=jnp.int32)
    picks = (winner[:, None] == ids[None, :]).astype(jnp.float32)
    member = (query_prompt[None, :] == prompts[:, None]).astype(jnp.float32)
    weights = (picks - member / BEST).astype(jnp.bfloat16)
    advantage = jnp.dot(weights, scores, preferred_element_type=jnp.float32)
    return (scores, advantage.astype(jnp.bfloat16))


def solution(mesh):
    return jax.shard_map(
        shards,
        mesh=mesh,
        in_specs=(
            P("layer", ("grp", "ex"), None),
            P("layer", ("grp", "ex"), None),
            P("layer", None, None),
            P("layer", None, None),
            P("grp"),
            P("grp"),
        ),
        out_specs=(P(None, ("grp", "ex")), P(None, ("grp", "ex"))),
        check_vma=False,
    )
```

```python
import functools

import jax
import jax.numpy as jnp
from jax import lax
from jax.experimental import pallas as pl
from jax.experimental.pallas import tpu as pltpu
from jax.sharding import PartitionSpec as P

KIN = 32
KOUT = 128
BEST = 4
ROWS = 8
WIDE = KIN * ROWS
PAIR = 2 * KOUT
DEPTH_BLOCK = 512
COLUMNS = 512
CUTS = 1
ROW_COPIES = 2
STORE_COPIES = 4
VMEM_LIMIT = 32 * 1024 * 1024
NT = (((1,), (1,)), ((), ()))


def left_matrix(left):
    row = lax.broadcasted_iota(jnp.int32, (WIDE, KIN), 0)
    column = lax.broadcasted_iota(jnp.int32, (WIDE, KIN), 1)
    spread = jnp.where((row >> 3) == column, 1.0, 0.0).astype(jnp.bfloat16)
    tall = jnp.dot(spread, left, preferred_element_type=jnp.float32).astype(jnp.bfloat16)
    full = lax.dot_general(tall, spread, NT, preferred_element_type=jnp.float32)
    row = lax.broadcasted_iota(jnp.int32, (WIDE, WIDE), 0)
    column = lax.broadcasted_iota(jnp.int32, (WIDE, WIDE), 1)
    return jnp.where((row & (ROWS - 1)) == (column & (ROWS - 1)), full, 0.0).astype(jnp.bfloat16)


def right_matrix(right):
    zero = jnp.zeros_like(right)
    return jnp.concatenate(
        [jnp.concatenate([right, zero], 1), jnp.concatenate([zero, right], 1)], 0
    )


def side_by_side_to_stacked(block):
    tiles = block.reshape(block.shape[0] // ROWS, ROWS, PAIR)
    return jnp.concatenate([tiles[:, :, :KOUT], tiles[:, :, KOUT:]], 1)


def precondition(rows_ref, both, mixer, half_ref, pre_ref):
    count = rows_ref.shape[0]
    together = 4
    for start in range(0, KIN // 2, together):
        block = jnp.concatenate(
            [rows_ref[:, p * PAIR : (p + 1) * PAIR] for p in range(start, start + together)], 0
        )
        half = jnp.dot(block, both, preferred_element_type=jnp.float32)
        for k in range(together):
            at = 2 * ROWS * (start + k)
            half_ref[:, at : at + 2 * ROWS, :] = side_by_side_to_stacked(
                half[k * count : (k + 1) * count]
            ).astype(jnp.bfloat16)

    def groups(index, carry):
        stacked = jnp.concatenate([half_ref[2 * index], half_ref[2 * index + 1]], 1)
        mixed = side_by_side_to_stacked(
            jnp.dot(mixer, stacked, preferred_element_type=jnp.float32)
        ).astype(jnp.bfloat16)
        at = pl.ds(pl.multiple_of(index * 2 * ROWS, 2 * ROWS), 2 * ROWS)
        for i in range(KIN):
            pre_ref[at, i * KOUT : (i + 1) * KOUT] = mixed[i]
        return carry

    lax.fori_loop(0, count // (2 * ROWS), groups, 0, unroll=4)


def dot(pre_ref, store_ref, first, total_ref, out_ref):
    depth = pre_ref.shape[1]
    columns = total_ref.shape[0]
    for at in range(0, depth, DEPTH_BLOCK):
        block = slice(at, at + DEPTH_BLOCK)
        term = lax.dot_general(
            store_ref[first : first + columns, block],
            pre_ref[:, block],
            NT,
            preferred_element_type=jnp.float32,
        )
        if at == 0:
            total_ref[...] = term
        elif at + DEPTH_BLOCK < depth:
            total_ref[...] += term
        else:
            out_ref[:, first : first + columns] = (total_ref[...] + term).T


def copies_of(source_ref, target_ref, sems):
    rows = target_ref.shape[0] // sems.shape[0]
    return [
        pltpu.make_async_copy(
            source_ref.at[pl.ds(k * rows, rows)], target_ref.at[pl.ds(k * rows, rows)], sems.at[k]
        )
        for k in range(sems.shape[0])
    ]


def start(copies):
    for copy in copies:
        copy.start()


def wait(copies):
    for copy in copies:
        copy.wait()


def dots(pre_ref, store_vmem, copies, total_ref, out_ref):
    columns = total_ref.shape[0]
    share = len(copies) * columns // store_vmem.shape[0]
    for k, first in enumerate(range(0, store_vmem.shape[0], columns)):
        wait(copies[k * share : (k + 1) * share])
        dot(pre_ref, store_vmem, first, total_ref, out_ref)


def first_kernel(
    rows_ref, left_ref, right_ref, store_ref, out_ref, both_ref, mixer_ref,
    left_vmem, right_vmem, rows_vmem, store_vmem, half_ref, total_ref,
    left_sems, right_sems, rows_sems, store_sems,
):
    heads = copies_of(right_ref.at[0], right_vmem, right_sems)
    heads += copies_of(left_ref.at[0], left_vmem, left_sems)
    rows = copies_of(rows_ref.at[0], rows_vmem, rows_sems)
    copies = copies_of(store_ref.at[0], store_vmem, store_sems)
    start(heads + rows)
    wait(heads)
    both_ref[...] = right_matrix(right_vmem[...])
    mixer_ref[...] = left_matrix(left_vmem[...])
    wait(rows)
    start(copies)
    precondition(rows_vmem, both_ref[...], mixer_ref[...], half_ref, rows_vmem)
    dots(rows_vmem, store_vmem, copies, total_ref, out_ref)


def later_kernel(
    rows_ref, both_ref, mixer_ref, store_ref, out_ref,
    pre_ref, store_vmem, half_ref, total_ref, store_sems,
):
    copies = copies_of(store_ref.at[0], store_vmem, store_sems)
    start(copies)
    precondition(rows_ref.at[0], both_ref[...], mixer_ref[...], half_ref, pre_ref)
    dots(pre_ref, store_vmem, copies, total_ref, out_ref)


VMEM = pl.BlockSpec(memory_space=pltpu.VMEM)
HBM = pl.BlockSpec(memory_space=pltpu.HBM)


def in_hbm(array):
    return pltpu.with_memory_space_constraint(array, pltpu.HBM)


def call(kernel, queries, store, outs, in_specs, scratch, operands):
    count, depth = queries.shape[1:]
    examples = store.shape[1]
    return pl.pallas_call(
        kernel,
        out_shape=(jax.ShapeDtypeStruct((count, examples), jnp.float32),) + outs,
        in_specs=in_specs,
        out_specs=(VMEM,) * (1 + len(outs)),
        scratch_shapes=scratch,
        compiler_params=pltpu.CompilerParams(vmem_limit_bytes=VMEM_LIMIT),
        cost_estimate=pl.CostEstimate(
            flops=2 * count * depth * (examples + 1024),
            bytes_accessed=2 * depth * (count + examples),
            transcendentals=0,
        ),
    )(*operands)


def buffers(queries, store):
    count, depth = queries.shape[1:]
    examples = store.shape[1]
    return [
        pltpu.VMEM((count, depth), jnp.bfloat16),
        pltpu.VMEM((examples, depth), jnp.bfloat16),
        pltpu.VMEM((count // ROWS, WIDE, KOUT), jnp.bfloat16),
        pltpu.VMEM((min(COLUMNS, examples), count), jnp.float32),
    ]


def first_scores(queries, left_inv, right_inv, store):
    small = [pltpu.VMEM((KIN, KIN), jnp.bfloat16), pltpu.VMEM((KOUT, KOUT), jnp.bfloat16)]
    sems = [pltpu.SemaphoreType.DMA((n,)) for n in (1, 1, ROW_COPIES, STORE_COPIES)]
    outs = (
        jax.ShapeDtypeStruct((PAIR, PAIR), jnp.bfloat16),
        jax.ShapeDtypeStruct((WIDE, WIDE), jnp.bfloat16),
    )
    operands = [in_hbm(a) for a in (queries, left_inv, right_inv, store)]
    return call(
        first_kernel, queries, store, outs, [HBM] * 4,
        small + buffers(queries, store) + sems, operands,
    )


def later_scores(queries, both, mixer, store):
    sems = [pltpu.SemaphoreType.DMA((STORE_COPIES,))]
    return call(
        later_kernel, queries, store, (), [VMEM] * 3 + [HBM],
        buffers(queries, store) + sems, [queries, both, mixer, in_hbm(store)],
    )[0]


def swap(block, bit):
    route = [(i, i ^ bit) for i in range(lax.axis_size("layer"))]
    return lax.ppermute(block, "layer", route)


HALVE, EXCHANGE, DOUBLE = range(3)


class LayerSum:
    def __init__(self, block, bits, index):
        self.block, self.index = block, index
        self.moves = [(bit, HALVE) for bit in bits[:-1]]
        self.moves += [(bit, EXCHANGE) for bit in bits[-1:]]
        self.moves += [(bit, DOUBLE) for bit in reversed(bits[:-1])]
        if len(bits) < 2:
            self.block = block.astype(jnp.bfloat16)

    def send(self, order):
        bit, kind = self.moves[0]
        sent = self.block
        if kind == HALVE:
            rows = self.block.shape[0] // 2
            upper = (self.index & bit) // bit
            sent = lax.dynamic_slice_in_dim(self.block, (1 - upper) * rows, rows, 0)
            sent = sent.astype(jnp.bfloat16)
            self.block = lax.dynamic_slice_in_dim(self.block, upper * rows, rows, 0)
        self.received = swap(order.after(sent), bit)

    def take(self, order):
        bit, kind = self.moves.pop(0)
        received = order.mark(self.received)
        mine = self.block
        if kind == DOUBLE:
            low = (self.index & bit) == 0
            self.block = jnp.concatenate(
                [jnp.where(low, mine, received), jnp.where(low, received, mine)], 0
            )
            return
        self.block = mine.astype(jnp.float32) + received.astype(jnp.float32)
        if not (self.moves and self.moves[0][1] == HALVE):
            self.block = self.block.astype(jnp.bfloat16)


class Order:
    def __init__(self):
        self.last = jnp.zeros((), jnp.float32)

    def after(self, value):
        value, _ = lax.optimization_barrier((value, self.last))
        return value

    def mark(self, value):
        value, self.last = lax.optimization_barrier((value, self.last))
        return value


def cut(columns):
    return [columns * k // CUTS for k in range(CUTS + 1)]


def rotate(chunks, order):
    for chunk in chunks:
        if chunk.moves:
            chunk.take(order)
            if chunk.moves:
                chunk.send(order)


def shards(store, queries, left_inv, right_inv, query_prompt, winner):
    rows = queries.shape[1]
    columns = store.shape[1]
    ex_count = lax.axis_size("ex")
    position = lax.axis_index("ex")
    count = lax.axis_size("layer")
    index = lax.axis_index("layer")
    bits = [1 << k for k in range(count.bit_length() - 1)]
    bits = bits[1:2] + bits[:1] + bits[2:]
    order = Order()
    chunks, places = [], []
    current = queries
    cuts = cut(columns)
    for step in range(ex_count):
        if step == 0:
            part, both, mixer = first_scores(queries, left_inv, right_inv, store)
        else:
            route = [((i - 1) % ex_count, i) for i in range(ex_count)]
            current = lax.ppermute(current, "ex", route)
            part = order.mark(later_scores(order.after(current), both, mixer, store))
            rotate(chunks, order)
        for first, end in zip(cuts[:-1], cuts[1:]):
            chunk = LayerSum(part[:, first:end], bits, index)
            if chunk.moves:
                chunk.send(order)
            chunks.append(chunk)
            places.append(((position - step) % ex_count * rows, jnp.int32(first)))
    while any(chunk.moves for chunk in chunks):
        rotate(chunks, order)
    done = [chunk.block for chunk in chunks]
    scores = jnp.zeros((rows * ex_count, columns), jnp.bfloat16)
    for place, block in zip(places, done):
        scores = lax.dynamic_update_slice(scores, block, place)
    ids = jnp.arange(scores.shape[0], dtype=jnp.int32)
    prompts = jnp.arange(winner.shape[0], dtype=jnp.int32)
    picks = (winner[:, None] == ids[None, :]).astype(jnp.float32)
    member = (query_prompt[None, :] == prompts[:, None]).astype(jnp.float32)
    weights = (picks - member / BEST).astype(jnp.bfloat16)
    advantage = jnp.dot(weights, scores, preferred_element_type=jnp.float32)
    return (scores, advantage.astype(jnp.bfloat16))


def solution(mesh):
    return jax.shard_map(
        shards,
        mesh=mesh,
        in_specs=(
            P("layer", ("grp", "ex"), None),
            P("layer", ("grp", "ex"), None),
            P("layer", None, None),
            P("layer", None, None),
            P("grp"),
            P("grp"),
        ),
        out_specs=(P(None, ("grp", "ex")), P(None, ("grp", "ex"))),
        check_vma=False,
    )
```

```python
import functools

import jax
import jax.numpy as jnp
from jax import lax
from jax.experimental import pallas as pl
from jax.experimental.pallas import tpu as pltpu
from jax.sharding import PartitionSpec as P

KIN = 32
KOUT = 128
BEST = 4
ROWS = 8
WIDE = KIN * ROWS
PAIR = 2 * KOUT
DEPTH_BLOCK = 512
COLUMNS = 512
CUTS = 2
ROW_COPIES = 2
STORE_COPIES = 4
VMEM_LIMIT = 32 * 1024 * 1024
NT = (((1,), (1,)), ((), ()))


def left_matrix(left):
    row = lax.broadcasted_iota(jnp.int32, (WIDE, KIN), 0)
    column = lax.broadcasted_iota(jnp.int32, (WIDE, KIN), 1)
    spread = jnp.where((row >> 3) == column, 1.0, 0.0).astype(jnp.bfloat16)
    tall = jnp.dot(spread, left, preferred_element_type=jnp.float32).astype(jnp.bfloat16)
    full = lax.dot_general(tall, spread, NT, preferred_element_type=jnp.float32)
    row = lax.broadcasted_iota(jnp.int32, (WIDE, WIDE), 0)
    column = lax.broadcasted_iota(jnp.int32, (WIDE, WIDE), 1)
    return jnp.where((row & (ROWS - 1)) == (column & (ROWS - 1)), full, 0.0).astype(jnp.bfloat16)


def right_matrix(right):
    zero = jnp.zeros_like(right)
    return jnp.concatenate(
        [jnp.concatenate([right, zero], 1), jnp.concatenate([zero, right], 1)], 0
    )


def side_by_side_to_stacked(block):
    tiles = block.reshape(block.shape[0] // ROWS, ROWS, PAIR)
    return jnp.concatenate([tiles[:, :, :KOUT], tiles[:, :, KOUT:]], 1)


def precondition(rows_ref, both, mixer, half_ref, pre_ref):
    count = rows_ref.shape[0]
    together = 4
    for start in range(0, KIN // 2, together):
        block = jnp.concatenate(
            [rows_ref[:, p * PAIR : (p + 1) * PAIR] for p in range(start, start + together)], 0
        )
        half = jnp.dot(block, both, preferred_element_type=jnp.float32)
        for k in range(together):
            at = 2 * ROWS * (start + k)
            half_ref[:, at : at + 2 * ROWS, :] = side_by_side_to_stacked(
                half[k * count : (k + 1) * count]
            ).astype(jnp.bfloat16)

    def groups(index, carry):
        stacked = jnp.concatenate([half_ref[2 * index], half_ref[2 * index + 1]], 1)
        mixed = side_by_side_to_stacked(
            jnp.dot(mixer, stacked, preferred_element_type=jnp.float32)
        ).astype(jnp.bfloat16)
        at = pl.ds(pl.multiple_of(index * 2 * ROWS, 2 * ROWS), 2 * ROWS)
        for i in range(KIN):
            pre_ref[at, i * KOUT : (i + 1) * KOUT] = mixed[i]
        return carry

    lax.fori_loop(0, count // (2 * ROWS), groups, 0, unroll=4)


def dot(pre_ref, store_ref, first, total_ref, out_ref):
    depth = pre_ref.shape[1]
    columns = total_ref.shape[0]
    for at in range(0, depth, DEPTH_BLOCK):
        block = slice(at, at + DEPTH_BLOCK)
        term = lax.dot_general(
            store_ref[first : first + columns, block],
            pre_ref[:, block],
            NT,
            preferred_element_type=jnp.float32,
        )
        if at == 0:
            total_ref[...] = term
        elif at + DEPTH_BLOCK < depth:
            total_ref[...] += term
        else:
            out_ref[:, first : first + columns] = (total_ref[...] + term).T


def copies_of(source_ref, target_ref, sems):
    rows = target_ref.shape[0] // sems.shape[0]
    return [
        pltpu.make_async_copy(
            source_ref.at[pl.ds(k * rows, rows)], target_ref.at[pl.ds(k * rows, rows)], sems.at[k]
        )
        for k in range(sems.shape[0])
    ]


def start(copies):
    for copy in copies:
        copy.start()


def wait(copies):
    for copy in copies:
        copy.wait()


def dots(pre_ref, store_vmem, copies, total_ref, out_ref):
    columns = total_ref.shape[0]
    share = len(copies) * columns // store_vmem.shape[0]
    for k, first in enumerate(range(0, store_vmem.shape[0], columns)):
        wait(copies[k * share : (k + 1) * share])
        dot(pre_ref, store_vmem, first, total_ref, out_ref)


def first_kernel(
    rows_ref, left_ref, right_ref, store_ref, out_ref, both_ref, mixer_ref,
    left_vmem, right_vmem, rows_vmem, store_vmem, half_ref, total_ref,
    left_sems, right_sems, rows_sems, store_sems,
):
    heads = copies_of(right_ref.at[0], right_vmem, right_sems)
    heads += copies_of(left_ref.at[0], left_vmem, left_sems)
    rows = copies_of(rows_ref.at[0], rows_vmem, rows_sems)
    copies = copies_of(store_ref.at[0], store_vmem, store_sems)
    start(heads + rows)
    wait(heads)
    both_ref[...] = right_matrix(right_vmem[...])
    mixer_ref[...] = left_matrix(left_vmem[...])
    wait(rows)
    start(copies)
    precondition(rows_vmem, both_ref[...], mixer_ref[...], half_ref, rows_vmem)
    dots(rows_vmem, store_vmem, copies, total_ref, out_ref)


def later_kernel(
    sent, rows_ref, both_ref, mixer_ref, store_ref, *refs,
):
    out_ref, pre_ref, store_vmem, half_ref, total_ref, store_sems = refs[sent:]
    copies = copies_of(store_ref.at[0], store_vmem, store_sems)
    start(copies)
    precondition(rows_ref.at[0], both_ref[...], mixer_ref[...], half_ref, pre_ref)
    dots(pre_ref, store_vmem, copies, total_ref, out_ref)


VMEM = pl.BlockSpec(memory_space=pltpu.VMEM)
HBM = pl.BlockSpec(memory_space=pltpu.HBM)
ANYWHERE = pl.BlockSpec(memory_space=pl.ANY)


def in_hbm(array):
    return pltpu.with_memory_space_constraint(array, pltpu.HBM)


def call(kernel, queries, store, outs, in_specs, scratch, operands):
    count, depth = queries.shape[1:]
    examples = store.shape[1]
    return pl.pallas_call(
        kernel,
        out_shape=(jax.ShapeDtypeStruct((count, examples), jnp.float32),) + outs,
        in_specs=in_specs,
        out_specs=(VMEM,) * (1 + len(outs)),
        scratch_shapes=scratch,
        compiler_params=pltpu.CompilerParams(vmem_limit_bytes=VMEM_LIMIT),
        cost_estimate=pl.CostEstimate(
            flops=2 * count * depth * (examples + 1024),
            bytes_accessed=2 * depth * (count + examples),
            transcendentals=0,
        ),
    )(*operands)


def buffers(queries, store):
    count, depth = queries.shape[1:]
    examples = store.shape[1]
    return [
        pltpu.VMEM((count, depth), jnp.bfloat16),
        pltpu.VMEM((examples, depth), jnp.bfloat16),
        pltpu.VMEM((count // ROWS, WIDE, KOUT), jnp.bfloat16),
        pltpu.VMEM((min(COLUMNS, examples), count), jnp.float32),
    ]


def first_scores(queries, left_inv, right_inv, store):
    small = [pltpu.VMEM((KIN, KIN), jnp.bfloat16), pltpu.VMEM((KOUT, KOUT), jnp.bfloat16)]
    sems = [pltpu.SemaphoreType.DMA((n,)) for n in (1, 1, ROW_COPIES, STORE_COPIES)]
    outs = (
        jax.ShapeDtypeStruct((PAIR, PAIR), jnp.bfloat16),
        jax.ShapeDtypeStruct((WIDE, WIDE), jnp.bfloat16),
    )
    operands = [in_hbm(a) for a in (queries, left_inv, right_inv, store)]
    return call(
        first_kernel, queries, store, outs, [HBM] * 4,
        small + buffers(queries, store) + sems, operands,
    )


def later_scores(queries, both, mixer, store, sent):
    sems = [pltpu.SemaphoreType.DMA((STORE_COPIES,))]
    return call(
        functools.partial(later_kernel, len(sent)), queries, store, (),
        [VMEM] * 3 + [HBM] + [ANYWHERE] * len(sent), buffers(queries, store) + sems,
        [queries, both, mixer, in_hbm(store), *sent],
    )[0]


def swap(block, bit):
    route = [(i, i ^ bit) for i in range(lax.axis_size("layer"))]
    return lax.ppermute(block, "layer", route)


HALVE, EXCHANGE, DOUBLE = range(3)


class LayerSum:
    def __init__(self, block, bits, index):
        self.block, self.index = block, index
        self.moves = [(bit, HALVE) for bit in bits[:-1]]
        self.moves += [(bit, EXCHANGE) for bit in bits[-1:]]
        self.moves += [(bit, DOUBLE) for bit in reversed(bits[:-1])]
        if len(bits) < 2:
            self.block = block.astype(jnp.bfloat16)

    def send(self, order):
        bit, kind = self.moves[0]
        sent = self.block
        if kind == HALVE:
            rows = self.block.shape[0] // 2
            upper = (self.index & bit) // bit
            sent = lax.dynamic_slice_in_dim(self.block, (1 - upper) * rows, rows, 0)
            sent = sent.astype(jnp.bfloat16)
            self.block = lax.dynamic_slice_in_dim(self.block, upper * rows, rows, 0)
        self.sent = order.mark(sent)
        self.received = swap(self.sent, bit)

    def take(self, order):
        bit, kind = self.moves.pop(0)
        received = order.mark(self.received)
        mine = self.block
        if kind == DOUBLE:
            low = (self.index & bit) == 0
            self.block = jnp.concatenate(
                [jnp.where(low, mine, received), jnp.where(low, received, mine)], 0
            )
            return
        self.block = mine.astype(jnp.float32) + received.astype(jnp.float32)
        if not (self.moves and self.moves[0][1] == HALVE):
            self.block = self.block.astype(jnp.bfloat16)


class Order:
    def __init__(self):
        self.last = jnp.zeros((), jnp.float32)

    def after(self, value):
        value, _ = lax.optimization_barrier((value, self.last))
        return value

    def mark(self, value):
        value, self.last = lax.optimization_barrier((value, self.last))
        return value


def cut(columns):
    return [columns * k // CUTS for k in range(CUTS + 1)]


def rotate(chunks, order):
    for chunk in chunks:
        if chunk.moves:
            chunk.take(order)
            if chunk.moves:
                chunk.send(order)


def shards(store, queries, left_inv, right_inv, query_prompt, winner):
    rows = queries.shape[1]
    columns = store.shape[1]
    ex_count = lax.axis_size("ex")
    position = lax.axis_index("ex")
    count = lax.axis_size("layer")
    index = lax.axis_index("layer")
    bits = [1 << k for k in range(count.bit_length() - 1)]
    orders = [bits[1:2] + bits[:1] + bits[2:], bits]
    order = Order()
    chunks, places = [], []
    current = queries
    cuts = cut(columns)
    for step in range(ex_count):
        if step == 0:
            part, both, mixer = first_scores(queries, left_inv, right_inv, store)
        else:
            route = [((i - 1) % ex_count, i) for i in range(ex_count)]
            current = lax.ppermute(current, "ex", route)
            sent = [chunk.sent for chunk in chunks if chunk.moves]
            part = order.mark(later_scores(order.after(current), both, mixer, store, sent))
            rotate(chunks, order)
        for number, (first, end) in enumerate(zip(cuts[:-1], cuts[1:])):
            chunk = LayerSum(part[:, first:end], orders[number % 2], index)
            if chunk.moves:
                chunk.send(order)
            chunks.append(chunk)
            places.append(((position - step) % ex_count * rows, jnp.int32(first)))
    while any(chunk.moves for chunk in chunks):
        rotate(chunks, order)
    done = [chunk.block for chunk in chunks]
    scores = jnp.zeros((rows * ex_count, columns), jnp.bfloat16)
    for place, block in zip(places, done):
        scores = lax.dynamic_update_slice(scores, block, place)
    ids = jnp.arange(scores.shape[0], dtype=jnp.int32)
    prompts = jnp.arange(winner.shape[0], dtype=jnp.int32)
    picks = (winner[:, None] == ids[None, :]).astype(jnp.float32)
    member = (query_prompt[None, :] == prompts[:, None]).astype(jnp.float32)
    weights = (picks - member / BEST).astype(jnp.bfloat16)
    advantage = jnp.dot(weights, scores, preferred_element_type=jnp.float32)
    return (scores, advantage.astype(jnp.bfloat16))


def solution(mesh):
    return jax.shard_map(
        shards,
        mesh=mesh,
        in_specs=(
            P("layer", ("grp", "ex"), None),
            P("layer", ("grp", "ex"), None),
            P("layer", None, None),
            P("layer", None, None),
            P("grp"),
            P("grp"),
        ),
        out_specs=(P(None, ("grp", "ex")), P(None, ("grp", "ex"))),
        check_vma=False,
    )
```

```python
import functools

import jax
import jax.numpy as jnp
from jax import lax
from jax.experimental import pallas as pl
from jax.experimental.pallas import tpu as pltpu
from jax.sharding import PartitionSpec as P

KIN = 32
KOUT = 128
BEST = 4
ROWS = 8
WIDE = KIN * ROWS
PAIR = 2 * KOUT
DEPTH_BLOCK = 512
COLUMNS = 512
CUTS = 2
PIECES = 4
STORE_COPIES = 8
VMEM_LIMIT = 32 * 1024 * 1024
NT = (((1,), (1,)), ((), ()))


def left_matrix(left):
    row = lax.broadcasted_iota(jnp.int32, (WIDE, KIN), 0)
    column = lax.broadcasted_iota(jnp.int32, (WIDE, KIN), 1)
    spread = jnp.where((row >> 3) == column, 1.0, 0.0).astype(jnp.bfloat16)
    tall = jnp.dot(spread, left, preferred_element_type=jnp.float32).astype(jnp.bfloat16)
    full = lax.dot_general(tall, spread, NT, preferred_element_type=jnp.float32)
    row = lax.broadcasted_iota(jnp.int32, (WIDE, WIDE), 0)
    column = lax.broadcasted_iota(jnp.int32, (WIDE, WIDE), 1)
    return jnp.where((row & (ROWS - 1)) == (column & (ROWS - 1)), full, 0.0).astype(jnp.bfloat16)


def right_matrix(right):
    zero = jnp.zeros_like(right)
    return jnp.concatenate(
        [jnp.concatenate([right, zero], 1), jnp.concatenate([zero, right], 1)], 0
    )


def side_by_side_to_stacked(block):
    tiles = block.reshape(block.shape[0] // ROWS, ROWS, PAIR)
    return jnp.concatenate([tiles[:, :, :KOUT], tiles[:, :, KOUT:]], 1)


def precondition(rows_ref, both, mixer, half_ref, pre_ref, before):
    rows = rows_ref.shape[0] // PIECES

    def piece(step, carry):
        before(step)
        at = pl.ds(pl.multiple_of(step * rows, rows), rows)
        block = jnp.concatenate(
            [rows_ref[at, p * PAIR : (p + 1) * PAIR] for p in range(KIN // 2)], 0
        )
        half = jnp.dot(block, both, preferred_element_type=jnp.float32)
        groups = pl.ds(step * (rows // ROWS), rows // ROWS)
        for p in range(KIN // 2):
            half_ref[groups, 2 * ROWS * p : 2 * ROWS * (p + 1), :] = side_by_side_to_stacked(
                half[p * rows : (p + 1) * rows]
            ).astype(jnp.bfloat16)
        return carry

    lax.fori_loop(0, PIECES, piece, 0)

    def groups(index, carry):
        stacked = jnp.concatenate([half_ref[2 * index], half_ref[2 * index + 1]], 1)
        mixed = side_by_side_to_stacked(
            jnp.dot(mixer, stacked, preferred_element_type=jnp.float32)
        ).astype(jnp.bfloat16)
        at = pl.ds(pl.multiple_of(index * 2 * ROWS, 2 * ROWS), 2 * ROWS)
        for i in range(KIN):
            pre_ref[at, i * KOUT : (i + 1) * KOUT] = mixed[i]
        return carry

    lax.fori_loop(0, rows_ref.shape[0] // (2 * ROWS), groups, 0, unroll=4)


def copy_of(source_ref, target_ref, sems, step):
    rows = target_ref.shape[0] // sems.shape[0]
    at = pl.ds(pl.multiple_of(step * rows, rows), rows)
    return pltpu.make_async_copy(source_ref.at[at], target_ref.at[at], sems.at[step])


def start_store(store_ref, store_vmem, sems, step):
    share = sems.shape[0] // PIECES
    for k in range(share):
        copy_of(store_ref.at[0], store_vmem, sems, step * share + k).start()


def dots(pre_ref, store_ref, store_vmem, sems, total_ref, out_ref):
    columns = total_ref.shape[0]
    depth = pre_ref.shape[1]
    blocks = store_vmem.shape[0] // columns
    share = sems.shape[0] // blocks

    def block(step, carry):
        for k in range(share):
            copy_of(store_ref.at[0], store_vmem, sems, step * share + k).wait()
        rows = pl.ds(pl.multiple_of(step * columns, columns), columns)
        for at in range(0, depth, DEPTH_BLOCK):
            term = lax.dot_general(
                store_vmem[rows, at : at + DEPTH_BLOCK],
                pre_ref[:, at : at + DEPTH_BLOCK],
                NT,
                preferred_element_type=jnp.float32,
            )
            if at == 0:
                total_ref[...] = term
            elif at + DEPTH_BLOCK < depth:
                total_ref[...] += term
            else:
                out_ref[:, rows] = (total_ref[...] + term).T
        return carry

    lax.fori_loop(0, blocks, block, 0)


def first_kernel(
    rows_ref, left_ref, right_ref, store_ref, out_ref, both_ref, mixer_ref,
    left_vmem, right_vmem, rows_vmem, store_vmem, half_ref, total_ref,
    left_sems, right_sems, rows_sems, store_sems,
):
    right = copy_of(right_ref.at[0], right_vmem, right_sems, 0)
    left = copy_of(left_ref.at[0], left_vmem, left_sems, 0)
    right.start()
    left.start()
    for step in range(PIECES):
        copy_of(rows_ref.at[0], rows_vmem, rows_sems, step).start()
    right.wait()
    both_ref[...] = right_matrix(right_vmem[...])
    left.wait()
    mixer_ref[...] = left_matrix(left_vmem[...])

    def before(step):
        copy_of(rows_ref.at[0], rows_vmem, rows_sems, step).wait()
        start_store(store_ref, store_vmem, store_sems, step)

    precondition(rows_vmem, both_ref[...], mixer_ref[...], half_ref, rows_vmem, before)
    dots(rows_vmem, store_ref, store_vmem, store_sems, total_ref, out_ref)


def later_kernel(
    sent, rows_ref, both_ref, mixer_ref, store_ref, *refs,
):
    out_ref, pre_ref, store_vmem, half_ref, total_ref, store_sems = refs[sent:]

    def before(step):
        start_store(store_ref, store_vmem, store_sems, step)

    precondition(rows_ref.at[0], both_ref[...], mixer_ref[...], half_ref, pre_ref, before)
    dots(pre_ref, store_ref, store_vmem, store_sems, total_ref, out_ref)


VMEM = pl.BlockSpec(memory_space=pltpu.VMEM)
HBM = pl.BlockSpec(memory_space=pltpu.HBM)
ANYWHERE = pl.BlockSpec(memory_space=pl.ANY)


def in_hbm(array):
    return pltpu.with_memory_space_constraint(array, pltpu.HBM)


def call(kernel, queries, store, outs, in_specs, scratch, operands):
    count, depth = queries.shape[1:]
    examples = store.shape[1]
    return pl.pallas_call(
        kernel,
        out_shape=(jax.ShapeDtypeStruct((count, examples), jnp.float32),) + outs,
        in_specs=in_specs,
        out_specs=(VMEM,) * (1 + len(outs)),
        scratch_shapes=scratch,
        compiler_params=pltpu.CompilerParams(vmem_limit_bytes=VMEM_LIMIT),
        cost_estimate=pl.CostEstimate(
            flops=2 * count * depth * (examples + 1024),
            bytes_accessed=2 * depth * (count + examples),
            transcendentals=0,
        ),
    )(*operands)


def buffers(queries, store):
    count, depth = queries.shape[1:]
    examples = store.shape[1]
    return [
        pltpu.VMEM((count, depth), jnp.bfloat16),
        pltpu.VMEM((examples, depth), jnp.bfloat16),
        pltpu.VMEM((count // ROWS, WIDE, KOUT), jnp.bfloat16),
        pltpu.VMEM((min(COLUMNS, examples), count), jnp.float32),
    ]


def first_scores(queries, left_inv, right_inv, store):
    small = [pltpu.VMEM((KIN, KIN), jnp.bfloat16), pltpu.VMEM((KOUT, KOUT), jnp.bfloat16)]
    sems = [pltpu.SemaphoreType.DMA((n,)) for n in (1, 1, PIECES, STORE_COPIES)]
    outs = (
        jax.ShapeDtypeStruct((PAIR, PAIR), jnp.bfloat16),
        jax.ShapeDtypeStruct((WIDE, WIDE), jnp.bfloat16),
    )
    operands = [in_hbm(a) for a in (queries, left_inv, right_inv, store)]
    return call(
        first_kernel, queries, store, outs, [HBM] * 4,
        small + buffers(queries, store) + sems, operands,
    )


def later_scores(queries, both, mixer, store, sent):
    sems = [pltpu.SemaphoreType.DMA((STORE_COPIES,))]
    return call(
        functools.partial(later_kernel, len(sent)), queries, store, (),
        [VMEM] * 3 + [HBM] + [ANYWHERE] * len(sent), buffers(queries, store) + sems,
        [queries, both, mixer, in_hbm(store), *sent],
    )[0]


def swap(block, bit):
    route = [(i, i ^ bit) for i in range(lax.axis_size("layer"))]
    return lax.ppermute(block, "layer", route)


HALVE, EXCHANGE, DOUBLE = range(3)


class LayerSum:
    def __init__(self, block, bits, index):
        self.block, self.index = block, index
        self.moves = [(bit, HALVE) for bit in bits[:-1]]
        self.moves += [(bit, EXCHANGE) for bit in bits[-1:]]
        self.moves += [(bit, DOUBLE) for bit in reversed(bits[:-1])]
        if len(bits) < 2:
            self.block = block.astype(jnp.bfloat16)

    def send(self, order):
        bit, kind = self.moves[0]
        sent = self.block
        if kind == HALVE:
            rows = self.block.shape[0] // 2
            upper = (self.index & bit) // bit
            sent = lax.dynamic_slice_in_dim(self.block, (1 - upper) * rows, rows, 0)
            sent = sent.astype(jnp.bfloat16)
            self.block = lax.dynamic_slice_in_dim(self.block, upper * rows, rows, 0)
        self.sent = order.mark(sent)
        self.received = swap(self.sent, bit)

    def take(self, order):
        bit, kind = self.moves.pop(0)
        received = order.mark(self.received)
        mine = self.block
        if kind == DOUBLE:
            low = (self.index & bit) == 0
            self.block = jnp.concatenate(
                [jnp.where(low, mine, received), jnp.where(low, received, mine)], 0
            )
            return
        self.block = mine.astype(jnp.float32) + received.astype(jnp.float32)
        if not (self.moves and self.moves[0][1] == HALVE):
            self.block = self.block.astype(jnp.bfloat16)


class Order:
    def __init__(self):
        self.last = jnp.zeros((), jnp.float32)

    def after(self, value):
        value, _ = lax.optimization_barrier((value, self.last))
        return value

    def mark(self, value):
        value, self.last = lax.optimization_barrier((value, self.last))
        return value


def cut(columns):
    return [columns * k // CUTS for k in range(CUTS + 1)]


def rotate(chunks, order):
    for chunk in chunks:
        if chunk.moves:
            chunk.take(order)
            if chunk.moves:
                chunk.send(order)


def shards(store, queries, left_inv, right_inv, query_prompt, winner):
    rows = queries.shape[1]
    columns = store.shape[1]
    ex_count = lax.axis_size("ex")
    position = lax.axis_index("ex")
    count = lax.axis_size("layer")
    index = lax.axis_index("layer")
    bits = [1 << k for k in range(count.bit_length() - 1)]
    orders = [bits[1:2] + bits[:1] + bits[2:], bits]
    order = Order()
    chunks, places = [], []
    current = queries
    cuts = cut(columns)
    for step in range(ex_count):
        if step == 0:
            part, both, mixer = first_scores(queries, left_inv, right_inv, store)
        else:
            route = [((i - 1) % ex_count, i) for i in range(ex_count)]
            current = lax.ppermute(current, "ex", route)
            sent = [chunk.sent for chunk in chunks if chunk.moves]
            part = order.mark(later_scores(order.after(current), both, mixer, store, sent))
            rotate(chunks, order)
        for number, (first, end) in enumerate(zip(cuts[:-1], cuts[1:])):
            chunk = LayerSum(part[:, first:end], orders[number % 2], index)
            if chunk.moves:
                chunk.send(order)
            chunks.append(chunk)
            places.append(((position - step) % ex_count * rows, jnp.int32(first)))
    while any(chunk.moves for chunk in chunks):
        rotate(chunks, order)
    done = [chunk.block for chunk in chunks]
    scores = jnp.zeros((rows * ex_count, columns), jnp.bfloat16)
    for place, block in zip(places, done):
        scores = lax.dynamic_update_slice(scores, block, place)
    ids = jnp.arange(scores.shape[0], dtype=jnp.int32)
    prompts = jnp.arange(winner.shape[0], dtype=jnp.int32)
    picks = (winner[:, None] == ids[None, :]).astype(jnp.float32)
    member = (query_prompt[None, :] == prompts[:, None]).astype(jnp.float32)
    weights = (picks - member / BEST).astype(jnp.bfloat16)
    advantage = jnp.dot(weights, scores, preferred_element_type=jnp.float32)
    return (scores, advantage.astype(jnp.bfloat16))


def solution(mesh):
    return jax.shard_map(
        shards,
        mesh=mesh,
        in_specs=(
            P("layer", ("grp", "ex"), None),
            P("layer", ("grp", "ex"), None),
            P("layer", None, None),
            P("layer", None, None),
            P("grp"),
            P("grp"),
        ),
        out_specs=(P(None, ("grp", "ex")), P(None, ("grp", "ex"))),
        check_vma=False,
    )
```

```python
import functools

import jax
import jax.numpy as jnp
from jax import lax
from jax.experimental import pallas as pl
from jax.experimental.pallas import tpu as pltpu
from jax.sharding import PartitionSpec as P

KIN = 32
KOUT = 128
BEST = 4
ROWS = 8
WIDE = KIN * ROWS
PAIR = 2 * KOUT
DEPTH_BLOCK = 512
COLUMNS = 512
ORDERS = ((0,), (1, 0))
LANES = 128
NEAR_START_US = 1.1
FAR_START_US = 1.5
LATENCY_US = 0.5
NEAR_BYTES_PER_US = 50000
FAR_BYTES_PER_US = 25000
KERNEL_US = 5.3
PIECES = 4
STORE_COPIES = 8
VMEM_LIMIT = 32 * 1024 * 1024
NT = (((1,), (1,)), ((), ()))


def left_matrix(left):
    row = lax.broadcasted_iota(jnp.int32, (WIDE, KIN), 0)
    column = lax.broadcasted_iota(jnp.int32, (WIDE, KIN), 1)
    spread = jnp.where((row >> 3) == column, 1.0, 0.0).astype(jnp.bfloat16)
    tall = jnp.dot(spread, left, preferred_element_type=jnp.float32).astype(jnp.bfloat16)
    full = lax.dot_general(tall, spread, NT, preferred_element_type=jnp.float32)
    row = lax.broadcasted_iota(jnp.int32, (WIDE, WIDE), 0)
    column = lax.broadcasted_iota(jnp.int32, (WIDE, WIDE), 1)
    return jnp.where((row & (ROWS - 1)) == (column & (ROWS - 1)), full, 0.0).astype(jnp.bfloat16)


def right_matrix(right):
    zero = jnp.zeros_like(right)
    return jnp.concatenate(
        [jnp.concatenate([right, zero], 1), jnp.concatenate([zero, right], 1)], 0
    )


def side_by_side_to_stacked(block):
    tiles = block.reshape(block.shape[0] // ROWS, ROWS, PAIR)
    return jnp.concatenate([tiles[:, :, :KOUT], tiles[:, :, KOUT:]], 1)


def precondition(rows_ref, both, mixer, half_ref, pre_ref, before):
    rows = rows_ref.shape[0] // PIECES

    def piece(step, carry):
        before(step)
        at = pl.ds(pl.multiple_of(step * rows, rows), rows)
        block = jnp.concatenate(
            [rows_ref[at, p * PAIR : (p + 1) * PAIR] for p in range(KIN // 2)], 0
        )
        half = jnp.dot(block, both, preferred_element_type=jnp.float32)
        groups = pl.ds(step * (rows // ROWS), rows // ROWS)
        for p in range(KIN // 2):
            half_ref[groups, 2 * ROWS * p : 2 * ROWS * (p + 1), :] = side_by_side_to_stacked(
                half[p * rows : (p + 1) * rows]
            ).astype(jnp.bfloat16)
        return carry

    lax.fori_loop(0, PIECES, piece, 0)

    def groups(index, carry):
        stacked = jnp.concatenate([half_ref[2 * index], half_ref[2 * index + 1]], 1)
        mixed = side_by_side_to_stacked(
            jnp.dot(mixer, stacked, preferred_element_type=jnp.float32)
        ).astype(jnp.bfloat16)
        at = pl.ds(pl.multiple_of(index * 2 * ROWS, 2 * ROWS), 2 * ROWS)
        for i in range(KIN):
            pre_ref[at, i * KOUT : (i + 1) * KOUT] = mixed[i]
        return carry

    lax.fori_loop(0, rows_ref.shape[0] // (2 * ROWS), groups, 0, unroll=4)


def copy_of(source_ref, target_ref, sems, step):
    rows = target_ref.shape[0] // sems.shape[0]
    at = pl.ds(pl.multiple_of(step * rows, rows), rows)
    return pltpu.make_async_copy(source_ref.at[at], target_ref.at[at], sems.at[step])


def start_store(store_ref, store_vmem, sems, step):
    share = sems.shape[0] // PIECES
    for k in range(share):
        copy_of(store_ref.at[0], store_vmem, sems, step * share + k).start()


def dots(pre_ref, store_ref, store_vmem, sems, total_ref, out_ref):
    columns = total_ref.shape[0]
    depth = pre_ref.shape[1]
    blocks = store_vmem.shape[0] // columns
    share = sems.shape[0] // blocks

    def block(step, carry):
        for k in range(share):
            copy_of(store_ref.at[0], store_vmem, sems, step * share + k).wait()
        rows = pl.ds(pl.multiple_of(step * columns, columns), columns)
        for at in range(0, depth, DEPTH_BLOCK):
            term = lax.dot_general(
                store_vmem[rows, at : at + DEPTH_BLOCK],
                pre_ref[:, at : at + DEPTH_BLOCK],
                NT,
                preferred_element_type=jnp.float32,
            )
            if at == 0:
                total_ref[...] = term
            elif at + DEPTH_BLOCK < depth:
                total_ref[...] += term
            else:
                out_ref[:, rows] = (total_ref[...] + term).T
        return carry

    lax.fori_loop(0, blocks, block, 0)


def first_kernel(
    rows_ref, left_ref, right_ref, store_ref, out_ref, both_ref, mixer_ref,
    left_vmem, right_vmem, rows_vmem, store_vmem, half_ref, total_ref,
    left_sems, right_sems, rows_sems, store_sems,
):
    right = copy_of(right_ref.at[0], right_vmem, right_sems, 0)
    left = copy_of(left_ref.at[0], left_vmem, left_sems, 0)
    right.start()
    left.start()
    for step in range(PIECES):
        copy_of(rows_ref.at[0], rows_vmem, rows_sems, step).start()
    right.wait()
    both_ref[...] = right_matrix(right_vmem[...])
    left.wait()
    mixer_ref[...] = left_matrix(left_vmem[...])

    def before(step):
        copy_of(rows_ref.at[0], rows_vmem, rows_sems, step).wait()
        start_store(store_ref, store_vmem, store_sems, step)

    precondition(rows_vmem, both_ref[...], mixer_ref[...], half_ref, rows_vmem, before)
    dots(rows_vmem, store_ref, store_vmem, store_sems, total_ref, out_ref)


def later_kernel(
    sent, rows_ref, both_ref, mixer_ref, store_ref, *refs,
):
    out_ref, pre_ref, store_vmem, half_ref, total_ref, store_sems = refs[sent:]

    def before(step):
        start_store(store_ref, store_vmem, store_sems, step)

    precondition(rows_ref.at[0], both_ref[...], mixer_ref[...], half_ref, pre_ref, before)
    dots(pre_ref, store_ref, store_vmem, store_sems, total_ref, out_ref)


VMEM = pl.BlockSpec(memory_space=pltpu.VMEM)
HBM = pl.BlockSpec(memory_space=pltpu.HBM)
ANYWHERE = pl.BlockSpec(memory_space=pl.ANY)


def in_hbm(array):
    return pltpu.with_memory_space_constraint(array, pltpu.HBM)


def call(kernel, queries, store, outs, in_specs, scratch, operands):
    count, depth = queries.shape[1:]
    examples = store.shape[1]
    return pl.pallas_call(
        kernel,
        out_shape=(jax.ShapeDtypeStruct((count, examples), jnp.float32),) + outs,
        in_specs=in_specs,
        out_specs=(VMEM,) * (1 + len(outs)),
        scratch_shapes=scratch,
        compiler_params=pltpu.CompilerParams(vmem_limit_bytes=VMEM_LIMIT),
        cost_estimate=pl.CostEstimate(
            flops=2 * count * depth * (examples + 1024),
            bytes_accessed=2 * depth * (count + examples),
            transcendentals=0,
        ),
    )(*operands)


def buffers(queries, store):
    count, depth = queries.shape[1:]
    examples = store.shape[1]
    return [
        pltpu.VMEM((count, depth), jnp.bfloat16),
        pltpu.VMEM((examples, depth), jnp.bfloat16),
        pltpu.VMEM((count // ROWS, WIDE, KOUT), jnp.bfloat16),
        pltpu.VMEM((min(COLUMNS, examples), count), jnp.float32),
    ]


def first_scores(queries, left_inv, right_inv, store):
    small = [pltpu.VMEM((KIN, KIN), jnp.bfloat16), pltpu.VMEM((KOUT, KOUT), jnp.bfloat16)]
    sems = [pltpu.SemaphoreType.DMA((n,)) for n in (1, 1, PIECES, STORE_COPIES)]
    outs = (
        jax.ShapeDtypeStruct((PAIR, PAIR), jnp.bfloat16),
        jax.ShapeDtypeStruct((WIDE, WIDE), jnp.bfloat16),
    )
    operands = [in_hbm(a) for a in (queries, left_inv, right_inv, store)]
    return call(
        first_kernel, queries, store, outs, [HBM] * 4,
        small + buffers(queries, store) + sems, operands,
    )


def later_scores(queries, both, mixer, store, sent):
    sems = [pltpu.SemaphoreType.DMA((STORE_COPIES,))]
    return call(
        functools.partial(later_kernel, len(sent)), queries, store, (),
        [VMEM] * 3 + [HBM] + [ANYWHERE] * len(sent), buffers(queries, store) + sems,
        [queries, both, mixer, in_hbm(store), *sent],
    )[0]


def swap(block, bit):
    route = [(i, i ^ bit) for i in range(lax.axis_size("layer"))]
    return lax.ppermute(block, "layer", route)


HALVE, EXCHANGE, DOUBLE = range(3)


class LayerSum:
    def __init__(self, block, bits, index):
        self.block, self.index = block, index
        self.moves = [(bit, HALVE) for bit in bits[:-1]]
        self.moves += [(bit, EXCHANGE) for bit in bits[-1:]]
        self.moves += [(bit, DOUBLE) for bit in reversed(bits[:-1])]
        if len(bits) < 2:
            self.block = block.astype(jnp.bfloat16)

    def send(self, order):
        bit, kind = self.moves[0]
        sent = self.block
        if kind == HALVE:
            rows = self.block.shape[0] // 2
            upper = (self.index & bit) // bit
            sent = lax.dynamic_slice_in_dim(self.block, (1 - upper) * rows, rows, 0)
            sent = sent.astype(jnp.bfloat16)
            self.block = lax.dynamic_slice_in_dim(self.block, upper * rows, rows, 0)
        sent = order.mark(sent)
        self.token = sent[: 2 * ROWS, :LANES]
        self.received = swap(sent, bit)

    def bytes_of_move(self):
        size = self.block.size
        return size if self.moves[0][1] == HALVE else 2 * size

    def take(self, order):
        bit, kind = self.moves.pop(0)
        received = order.mark(self.received)
        mine = self.block
        if kind == DOUBLE:
            low = (self.index & bit) == 0
            self.block = jnp.concatenate(
                [jnp.where(low, mine, received), jnp.where(low, received, mine)], 0
            )
            return
        self.block = mine.astype(jnp.float32) + received.astype(jnp.float32)
        if not (self.moves and self.moves[0][1] == HALVE):
            self.block = self.block.astype(jnp.bfloat16)


class Order:
    def __init__(self):
        self.last = jnp.zeros((), jnp.float32)

    def after(self, value):
        value, _ = lax.optimization_barrier((value, self.last))
        return value

    def mark(self, value):
        value, self.last = lax.optimization_barrier((value, self.last))
        return value


class Clock:
    def __init__(self):
        self.now = 0.0
        self.links = {}
        self.arrivals = {}

    def send(self, chunk):
        bit, _ = chunk.moves[0]
        far = bit > 2
        self.now += FAR_START_US if far else NEAR_START_US
        begin = max(self.now, self.links.get(bit, 0.0))
        end = begin + chunk.bytes_of_move() / (FAR_BYTES_PER_US if far else NEAR_BYTES_PER_US)
        self.links[bit] = end
        self.arrivals[chunk] = end + (2 * LATENCY_US if far else LATENCY_US)

    def take(self, chunk):
        self.now = max(self.now, self.arrivals.pop(chunk))


def send(chunk, order, clock):
    if chunk.moves:
        clock.send(chunk)
        chunk.send(order)


def shards(store, queries, left_inv, right_inv, query_prompt, winner):
    rows = queries.shape[1]
    columns = store.shape[1]
    ex_count = lax.axis_size("ex")
    position = lax.axis_index("ex")
    count = lax.axis_size("layer")
    index = lax.axis_index("layer")
    bits = [1 << k for k in range(count.bit_length() - 1)]
    orders = [bits, bits[1:2] + bits[:1] + bits[2:]]
    order, clock = Order(), Clock()
    chunks, places = [], []
    current = queries
    for step in range(ex_count):
        if step == 0:
            part, both, mixer = first_scores(queries, left_inv, right_inv, store)
        else:
            route = [((i - 1) % ex_count, i) for i in range(ex_count)]
            current = lax.ppermute(current, "ex", route)
            tokens = [chunk.token for chunk in chunks if chunk.moves]
            part = order.mark(later_scores(order.after(current), both, mixer, store, tokens))
            clock.now += KERNEL_US
        choices = ORDERS[min(step, len(ORDERS) - 1)]
        width = columns // len(choices)
        for number, choice in enumerate(choices):
            first = number * width
            chunk = LayerSum(part[:, first : first + width], orders[choice], index)
            send(chunk, order, clock)
            chunks.append(chunk)
            places.append(((position - step) % ex_count * rows, jnp.int32(first)))
    while clock.arrivals:
        chunk = min(clock.arrivals, key=clock.arrivals.get)
        clock.take(chunk)
        chunk.take(order)
        send(chunk, order, clock)
    done = [chunk.block for chunk in chunks]
    scores = jnp.zeros((rows * ex_count, columns), jnp.bfloat16)
    for place, block in zip(places, done):
        scores = lax.dynamic_update_slice(scores, block, place)
    ids = jnp.arange(scores.shape[0], dtype=jnp.int32)
    prompts = jnp.arange(winner.shape[0], dtype=jnp.int32)
    picks = (winner[:, None] == ids[None, :]).astype(jnp.float32)
    member = (query_prompt[None, :] == prompts[:, None]).astype(jnp.float32)
    weights = (picks - member / BEST).astype(jnp.bfloat16)
    advantage = jnp.dot(weights, scores, preferred_element_type=jnp.float32)
    return (scores, advantage.astype(jnp.bfloat16))


def solution(mesh):
    return jax.shard_map(
        shards,
        mesh=mesh,
        in_specs=(
            P("layer", ("grp", "ex"), None),
            P("layer", ("grp", "ex"), None),
            P("layer", None, None),
            P("layer", None, None),
            P("grp"),
            P("grp"),
        ),
        out_specs=(P(None, ("grp", "ex")), P(None, ("grp", "ex"))),
        check_vma=False,
    )
```

```python
import functools

import jax
import jax.numpy as jnp
from jax import lax
from jax.experimental import pallas as pl
from jax.experimental.pallas import tpu as pltpu
from jax.sharding import PartitionSpec as P

KIN = 32
KOUT = 128
BEST = 4
ROWS = 8
WIDE = KIN * ROWS
PAIR = 2 * KOUT
DEPTH_BLOCK = 512
COLUMNS = 512
ORDERS = ((1, 0), (1, 0))
LANES = 128
NEAR_START_US = 1.1
FAR_START_US = 1.5
LATENCY_US = 0.5
NEAR_BYTES_PER_US = 50000
FAR_BYTES_PER_US = 25000
KERNEL_US = 5.3
PIECES = 4
STORE_COPIES = 8
VMEM_LIMIT = 32 * 1024 * 1024
NT = (((1,), (1,)), ((), ()))


def left_matrix(left):
    row = lax.broadcasted_iota(jnp.int32, (WIDE, KIN), 0)
    column = lax.broadcasted_iota(jnp.int32, (WIDE, KIN), 1)
    spread = jnp.where((row >> 3) == column, 1.0, 0.0).astype(jnp.bfloat16)
    tall = jnp.dot(spread, left, preferred_element_type=jnp.float32).astype(jnp.bfloat16)
    full = lax.dot_general(tall, spread, NT, preferred_element_type=jnp.float32)
    row = lax.broadcasted_iota(jnp.int32, (WIDE, WIDE), 0)
    column = lax.broadcasted_iota(jnp.int32, (WIDE, WIDE), 1)
    return jnp.where((row & (ROWS - 1)) == (column & (ROWS - 1)), full, 0.0).astype(jnp.bfloat16)


def right_matrix(right):
    zero = jnp.zeros_like(right)
    return jnp.concatenate(
        [jnp.concatenate([right, zero], 1), jnp.concatenate([zero, right], 1)], 0
    )


def side_by_side_to_stacked(block):
    tiles = block.reshape(block.shape[0] // ROWS, ROWS, PAIR)
    return jnp.concatenate([tiles[:, :, :KOUT], tiles[:, :, KOUT:]], 1)


def precondition(rows_ref, both, mixer, half_ref, pre_ref, before):
    rows = rows_ref.shape[0] // PIECES

    def piece(step, carry):
        before(step)
        at = pl.ds(pl.multiple_of(step * rows, rows), rows)
        block = jnp.concatenate(
            [rows_ref[at, p * PAIR : (p + 1) * PAIR] for p in range(KIN // 2)], 0
        )
        half = jnp.dot(block, both, preferred_element_type=jnp.float32)
        groups = pl.ds(step * (rows // ROWS), rows // ROWS)
        for p in range(KIN // 2):
            half_ref[groups, 2 * ROWS * p : 2 * ROWS * (p + 1), :] = side_by_side_to_stacked(
                half[p * rows : (p + 1) * rows]
            ).astype(jnp.bfloat16)
        return carry

    lax.fori_loop(0, PIECES, piece, 0)

    def groups(index, carry):
        stacked = jnp.concatenate([half_ref[2 * index], half_ref[2 * index + 1]], 1)
        mixed = side_by_side_to_stacked(
            jnp.dot(mixer, stacked, preferred_element_type=jnp.float32)
        ).astype(jnp.bfloat16)
        at = pl.ds(pl.multiple_of(index * 2 * ROWS, 2 * ROWS), 2 * ROWS)
        for i in range(KIN):
            pre_ref[at, i * KOUT : (i + 1) * KOUT] = mixed[i]
        return carry

    lax.fori_loop(0, rows_ref.shape[0] // (2 * ROWS), groups, 0, unroll=4)


def copy_of(source_ref, target_ref, sems, step):
    rows = target_ref.shape[0] // sems.shape[0]
    at = pl.ds(pl.multiple_of(step * rows, rows), rows)
    return pltpu.make_async_copy(source_ref.at[at], target_ref.at[at], sems.at[step])


def start_store(store_ref, store_vmem, sems, step):
    share = sems.shape[0] // PIECES
    for k in range(share):
        copy_of(store_ref.at[0], store_vmem, sems, step * share + k).start()


def dots(pre_ref, store_ref, store_vmem, sems, total_ref, out_ref):
    columns = total_ref.shape[0]
    depth = pre_ref.shape[1]
    blocks = store_vmem.shape[0] // columns
    share = sems.shape[0] // blocks

    def block(step, carry):
        for k in range(share):
            copy_of(store_ref.at[0], store_vmem, sems, step * share + k).wait()
        rows = pl.ds(pl.multiple_of(step * columns, columns), columns)
        for at in range(0, depth, DEPTH_BLOCK):
            term = lax.dot_general(
                store_vmem[rows, at : at + DEPTH_BLOCK],
                pre_ref[:, at : at + DEPTH_BLOCK],
                NT,
                preferred_element_type=jnp.float32,
            )
            if at == 0:
                total_ref[...] = term
            elif at + DEPTH_BLOCK < depth:
                total_ref[...] += term
            else:
                out_ref[:, rows] = (total_ref[...] + term).T
        return carry

    lax.fori_loop(0, blocks, block, 0)


def first_kernel(
    rows_ref, left_ref, right_ref, store_ref, out_ref, both_ref, mixer_ref,
    left_vmem, right_vmem, rows_vmem, store_vmem, half_ref, total_ref,
    left_sems, right_sems, rows_sems, store_sems,
):
    right = copy_of(right_ref.at[0], right_vmem, right_sems, 0)
    left = copy_of(left_ref.at[0], left_vmem, left_sems, 0)
    right.start()
    left.start()
    for step in range(PIECES):
        copy_of(rows_ref.at[0], rows_vmem, rows_sems, step).start()
    right.wait()
    both_ref[...] = right_matrix(right_vmem[...])
    left.wait()
    mixer_ref[...] = left_matrix(left_vmem[...])

    def before(step):
        copy_of(rows_ref.at[0], rows_vmem, rows_sems, step).wait()
        start_store(store_ref, store_vmem, store_sems, step)

    precondition(rows_vmem, both_ref[...], mixer_ref[...], half_ref, rows_vmem, before)
    dots(rows_vmem, store_ref, store_vmem, store_sems, total_ref, out_ref)


def later_kernel(
    held, rows_ref, both_ref, mixer_ref, store_ref, *refs,
):
    out_ref, *refs = refs[held:]
    pre_ref, store_vmem, half_ref, total_ref, store_sems = refs[held:]

    def before(step):
        start_store(store_ref, store_vmem, store_sems, step)

    precondition(rows_ref.at[0], both_ref[...], mixer_ref[...], half_ref, pre_ref, before)
    dots(pre_ref, store_ref, store_vmem, store_sems, total_ref, out_ref)


VMEM = pl.BlockSpec(memory_space=pltpu.VMEM)
HBM = pl.BlockSpec(memory_space=pltpu.HBM)
ANYWHERE = pl.BlockSpec(memory_space=pl.ANY)


def in_hbm(array):
    return pltpu.with_memory_space_constraint(array, pltpu.HBM)


def call(kernel, queries, store, outs, in_specs, scratch, operands, out_specs, aliases):
    count, depth = queries.shape[1:]
    examples = store.shape[1]
    return pl.pallas_call(
        kernel,
        out_shape=(jax.ShapeDtypeStruct((count, examples), jnp.float32),) + outs,
        in_specs=in_specs,
        out_specs=out_specs,
        input_output_aliases=aliases,
        scratch_shapes=scratch,
        compiler_params=pltpu.CompilerParams(vmem_limit_bytes=VMEM_LIMIT),
        cost_estimate=pl.CostEstimate(
            flops=2 * count * depth * (examples + 1024),
            bytes_accessed=2 * depth * (count + examples),
            transcendentals=0,
        ),
    )(*operands)


def buffers(queries, store):
    count, depth = queries.shape[1:]
    examples = store.shape[1]
    return [
        pltpu.VMEM((count, depth), jnp.bfloat16),
        pltpu.VMEM((examples, depth), jnp.bfloat16),
        pltpu.VMEM((count // ROWS, WIDE, KOUT), jnp.bfloat16),
        pltpu.VMEM((min(COLUMNS, examples), count), jnp.float32),
    ]


def first_scores(queries, left_inv, right_inv, store):
    small = [pltpu.VMEM((KIN, KIN), jnp.bfloat16), pltpu.VMEM((KOUT, KOUT), jnp.bfloat16)]
    sems = [pltpu.SemaphoreType.DMA((n,)) for n in (1, 1, PIECES, STORE_COPIES)]
    outs = (
        jax.ShapeDtypeStruct((PAIR, PAIR), jnp.bfloat16),
        jax.ShapeDtypeStruct((WIDE, WIDE), jnp.bfloat16),
    )
    operands = [in_hbm(a) for a in (queries, left_inv, right_inv, store)]
    return call(
        first_kernel, queries, store, outs, [HBM] * 4,
        small + buffers(queries, store) + sems, operands, (VMEM,) * 3, {},
    )


def later_scores(queries, both, mixer, store, held):
    sems = [pltpu.SemaphoreType.DMA((STORE_COPIES,))]
    outs = tuple(jax.ShapeDtypeStruct(a.shape, a.dtype) for a in held)
    return call(
        functools.partial(later_kernel, len(held)), queries, store, outs,
        [VMEM] * 3 + [HBM] + [ANYWHERE] * len(held), buffers(queries, store) + sems,
        [queries, both, mixer, in_hbm(store), *held],
        (VMEM,) + (ANYWHERE,) * len(held), {4 + k: 1 + k for k in range(len(held))},
    )


def swap(block, bit):
    route = [(i, i ^ bit) for i in range(lax.axis_size("layer"))]
    return lax.ppermute(block, "layer", route)


HALVE, EXCHANGE, DOUBLE = range(3)


class LayerSum:
    def __init__(self, block, bits, index):
        self.block, self.index = block, index
        self.moves = [(bit, HALVE) for bit in bits[:-1]]
        self.moves += [(bit, EXCHANGE) for bit in bits[-1:]]
        self.moves += [(bit, DOUBLE) for bit in reversed(bits[:-1])]
        if len(bits) < 2:
            self.block = block.astype(jnp.bfloat16)

    def send(self, order):
        bit, kind = self.moves[0]
        sent = self.block
        if kind == HALVE:
            rows = self.block.shape[0] // 2
            upper = (self.index & bit) // bit
            sent = lax.dynamic_slice_in_dim(self.block, (1 - upper) * rows, rows, 0)
            sent = sent.astype(jnp.bfloat16)
            self.block = lax.dynamic_slice_in_dim(self.block, upper * rows, rows, 0)
        self.received = swap(order.mark(sent), bit)

    def bytes_of_move(self):
        size = self.block.size
        return size if self.moves[0][1] == HALVE else 2 * size

    def take(self, order):
        bit, kind = self.moves.pop(0)
        received = order.mark(self.received)
        mine = self.block
        if kind == DOUBLE:
            low = (self.index & bit) == 0
            self.block = jnp.concatenate(
                [jnp.where(low, mine, received), jnp.where(low, received, mine)], 0
            )
            return
        self.block = mine.astype(jnp.float32) + received.astype(jnp.float32)
        if not (self.moves and self.moves[0][1] == HALVE):
            self.block = self.block.astype(jnp.bfloat16)


class Order:
    def __init__(self):
        self.last = jnp.zeros((), jnp.float32)

    def after(self, value):
        value, _ = lax.optimization_barrier((value, self.last))
        return value

    def mark(self, value):
        value, self.last = lax.optimization_barrier((value, self.last))
        return value


class Clock:
    def __init__(self):
        self.now = 0.0
        self.links = {}
        self.arrivals = {}

    def send(self, chunk):
        bit, _ = chunk.moves[0]
        far = bit > 2
        self.now += FAR_START_US if far else NEAR_START_US
        begin = max(self.now, self.links.get(bit, 0.0))
        end = begin + chunk.bytes_of_move() / (FAR_BYTES_PER_US if far else NEAR_BYTES_PER_US)
        self.links[bit] = end
        self.arrivals[chunk] = end + (2 * LATENCY_US if far else LATENCY_US)

    def take(self, chunk):
        self.now = max(self.now, self.arrivals.pop(chunk))


def send(chunk, order, clock):
    if chunk.moves:
        clock.send(chunk)
        chunk.send(order)


def shards(store, queries, left_inv, right_inv, query_prompt, winner):
    rows = queries.shape[1]
    columns = store.shape[1]
    ex_count = lax.axis_size("ex")
    position = lax.axis_index("ex")
    count = lax.axis_size("layer")
    index = lax.axis_index("layer")
    bits = [1 << k for k in range(count.bit_length() - 1)]
    orders = [bits, bits[1:2] + bits[:1] + bits[2:]]
    order, clock = Order(), Clock()
    chunks, places = [], []
    current = queries
    for step in range(ex_count):
        if step == 0:
            part, both, mixer = first_scores(queries, left_inv, right_inv, store)
        else:
            route = [((i - 1) % ex_count, i) for i in range(ex_count)]
            current = lax.ppermute(current, "ex", route)
            held = [chunk.block for chunk in chunks]
            part, *held = later_scores(order.after(current), both, mixer, store, held)
            part = order.mark(part)
            for chunk, block in zip(chunks, held):
                chunk.block = block
            clock.now += KERNEL_US
            for chunk in chunks:
                clock.take(chunk)
                chunk.take(order)
                send(chunk, order, clock)
        choices = ORDERS[min(step, len(ORDERS) - 1)]
        width = columns // len(choices)
        for number, choice in enumerate(choices):
            first = number * width
            chunk = LayerSum(part[:, first : first + width], orders[choice], index)
            send(chunk, order, clock)
            chunks.append(chunk)
            places.append(((position - step) % ex_count * rows, jnp.int32(first)))
    while clock.arrivals:
        there = [c for c, at in clock.arrivals.items() if at <= clock.now]
        chunk = there[-1] if there else min(clock.arrivals, key=clock.arrivals.get)
        clock.take(chunk)
        chunk.take(order)
        send(chunk, order, clock)
    done = [chunk.block for chunk in chunks]
    scores = jnp.zeros((rows * ex_count, columns), jnp.bfloat16)
    for place, block in zip(places, done):
        scores = lax.dynamic_update_slice(scores, block, place)
    ids = jnp.arange(scores.shape[0], dtype=jnp.int32)
    prompts = jnp.arange(winner.shape[0], dtype=jnp.int32)
    picks = (winner[:, None] == ids[None, :]).astype(jnp.float32)
    member = (query_prompt[None, :] == prompts[:, None]).astype(jnp.float32)
    weights = (picks - member / BEST).astype(jnp.bfloat16)
    advantage = jnp.dot(weights, scores, preferred_element_type=jnp.float32)
    return (scores, advantage.astype(jnp.bfloat16))


def solution(mesh):
    return jax.shard_map(
        shards,
        mesh=mesh,
        in_specs=(
            P("layer", ("grp", "ex"), None),
            P("layer", ("grp", "ex"), None),
            P("layer", None, None),
            P("layer", None, None),
            P("grp"),
            P("grp"),
        ),
        out_specs=(P(None, ("grp", "ex")), P(None, ("grp", "ex"))),
        check_vma=False,
    )
```

```python
import functools

import jax
import jax.numpy as jnp
from jax import lax
from jax.experimental import pallas as pl
from jax.experimental.pallas import tpu as pltpu
from jax.sharding import PartitionSpec as P

KIN = 32
KOUT = 128
BEST = 4
ROWS = 8
WIDE = KIN * ROWS
PAIR = 2 * KOUT
DEPTH_BLOCK = 512
COLUMNS = 512
ORDERS = ((1, 0), (1, 0))
NEAR_START_US = 1.1
FAR_START_US = 1.5
LATENCY_US = 0.5
NEAR_BYTES_PER_US = 50000
FAR_BYTES_PER_US = 25000
KERNEL_US = 5.3
PIECES = 4
STORE_COPIES = 8
VMEM_LIMIT = 32 * 1024 * 1024
NT = (((1,), (1,)), ((), ()))


def left_matrix(left):
    row = lax.broadcasted_iota(jnp.int32, (WIDE, KIN), 0)
    column = lax.broadcasted_iota(jnp.int32, (WIDE, KIN), 1)
    spread = jnp.where((row >> 3) == column, 1.0, 0.0).astype(jnp.bfloat16)
    tall = jnp.dot(spread, left, preferred_element_type=jnp.float32).astype(jnp.bfloat16)
    full = lax.dot_general(tall, spread, NT, preferred_element_type=jnp.float32)
    row = lax.broadcasted_iota(jnp.int32, (WIDE, WIDE), 0)
    column = lax.broadcasted_iota(jnp.int32, (WIDE, WIDE), 1)
    return jnp.where((row & (ROWS - 1)) == (column & (ROWS - 1)), full, 0.0).astype(jnp.bfloat16)


def right_matrix(right):
    zero = jnp.zeros_like(right)
    return jnp.concatenate(
        [jnp.concatenate([right, zero], 1), jnp.concatenate([zero, right], 1)], 0
    )


def side_by_side_to_stacked(block):
    tiles = block.reshape(block.shape[0] // ROWS, ROWS, PAIR)
    return jnp.concatenate([tiles[:, :, :KOUT], tiles[:, :, KOUT:]], 1)


def precondition(rows_ref, both, mixer, half_ref, pre_ref, before):
    rows = rows_ref.shape[0] // PIECES

    def piece(step, carry):
        before(step)
        at = pl.ds(pl.multiple_of(step * rows, rows), rows)
        block = jnp.concatenate(
            [rows_ref[at, p * PAIR : (p + 1) * PAIR] for p in range(KIN // 2)], 0
        )
        half = jnp.dot(block, both, preferred_element_type=jnp.float32)
        groups = pl.ds(step * (rows // ROWS), rows // ROWS)
        for p in range(KIN // 2):
            half_ref[groups, 2 * ROWS * p : 2 * ROWS * (p + 1), :] = side_by_side_to_stacked(
                half[p * rows : (p + 1) * rows]
            ).astype(jnp.bfloat16)
        return carry

    lax.fori_loop(0, PIECES, piece, 0)

    def groups(index, carry):
        stacked = jnp.concatenate([half_ref[2 * index], half_ref[2 * index + 1]], 1)
        mixed = side_by_side_to_stacked(
            jnp.dot(mixer, stacked, preferred_element_type=jnp.float32)
        ).astype(jnp.bfloat16)
        at = pl.ds(pl.multiple_of(index * 2 * ROWS, 2 * ROWS), 2 * ROWS)
        for i in range(KIN):
            pre_ref[at, i * KOUT : (i + 1) * KOUT] = mixed[i]
        return carry

    lax.fori_loop(0, rows_ref.shape[0] // (2 * ROWS), groups, 0, unroll=4)


def copy_of(source_ref, target_ref, sems, step):
    rows = target_ref.shape[0] // sems.shape[0]
    at = pl.ds(pl.multiple_of(step * rows, rows), rows)
    return pltpu.make_async_copy(source_ref.at[at], target_ref.at[at], sems.at[step])


def start_store(store_ref, store_vmem, sems, step):
    share = sems.shape[0] // PIECES
    for k in range(share):
        copy_of(store_ref.at[0], store_vmem, sems, step * share + k).start()


def dots(pre_ref, store_ref, store_vmem, sems, total_ref, out_ref):
    columns = total_ref.shape[0]
    depth = pre_ref.shape[1]
    blocks = store_vmem.shape[0] // columns
    share = sems.shape[0] // blocks

    def block(step, carry):
        for k in range(share):
            copy_of(store_ref.at[0], store_vmem, sems, step * share + k).wait()
        rows = pl.ds(pl.multiple_of(step * columns, columns), columns)
        for at in range(0, depth, DEPTH_BLOCK):
            term = lax.dot_general(
                store_vmem[rows, at : at + DEPTH_BLOCK],
                pre_ref[:, at : at + DEPTH_BLOCK],
                NT,
                preferred_element_type=jnp.float32,
            )
            if at == 0:
                total_ref[...] = term
            elif at + DEPTH_BLOCK < depth:
                total_ref[...] += term
            else:
                out_ref[:, rows] = (total_ref[...] + term).T
        return carry

    lax.fori_loop(0, blocks, block, 0)


def first_kernel(
    rows_ref, left_ref, right_ref, store_ref, out_ref, both_ref, mixer_ref,
    left_vmem, right_vmem, rows_vmem, store_vmem, half_ref, total_ref,
    left_sems, right_sems, rows_sems, store_sems,
):
    right = copy_of(right_ref.at[0], right_vmem, right_sems, 0)
    left = copy_of(left_ref.at[0], left_vmem, left_sems, 0)
    right.start()
    left.start()
    for step in range(PIECES):
        copy_of(rows_ref.at[0], rows_vmem, rows_sems, step).start()
    right.wait()
    both_ref[...] = right_matrix(right_vmem[...])
    left.wait()
    mixer_ref[...] = left_matrix(left_vmem[...])

    def before(step):
        copy_of(rows_ref.at[0], rows_vmem, rows_sems, step).wait()
        start_store(store_ref, store_vmem, store_sems, step)

    precondition(rows_vmem, both_ref[...], mixer_ref[...], half_ref, rows_vmem, before)
    dots(rows_vmem, store_ref, store_vmem, store_sems, total_ref, out_ref)


def later_kernel(
    sent, rows_ref, both_ref, mixer_ref, store_ref, *refs,
):
    out_ref, pre_ref, store_vmem, half_ref, total_ref, store_sems = refs[sent:]

    def before(step):
        start_store(store_ref, store_vmem, store_sems, step)

    precondition(rows_ref.at[0], both_ref[...], mixer_ref[...], half_ref, pre_ref, before)
    dots(pre_ref, store_ref, store_vmem, store_sems, total_ref, out_ref)


VMEM = pl.BlockSpec(memory_space=pltpu.VMEM)
HBM = pl.BlockSpec(memory_space=pltpu.HBM)


def in_hbm(array):
    return pltpu.with_memory_space_constraint(array, pltpu.HBM)


def call(kernel, queries, store, outs, in_specs, scratch, operands):
    count, depth = queries.shape[1:]
    examples = store.shape[1]
    return pl.pallas_call(
        kernel,
        out_shape=(jax.ShapeDtypeStruct((count, examples), jnp.float32),) + outs,
        in_specs=in_specs,
        out_specs=(VMEM,) * (1 + len(outs)),
        scratch_shapes=scratch,
        compiler_params=pltpu.CompilerParams(vmem_limit_bytes=VMEM_LIMIT),
        cost_estimate=pl.CostEstimate(
            flops=2 * count * depth * (examples + 1024),
            bytes_accessed=2 * depth * (count + examples),
            transcendentals=0,
        ),
    )(*operands)


def buffers(queries, store):
    count, depth = queries.shape[1:]
    examples = store.shape[1]
    return [
        pltpu.VMEM((count, depth), jnp.bfloat16),
        pltpu.VMEM((examples, depth), jnp.bfloat16),
        pltpu.VMEM((count // ROWS, WIDE, KOUT), jnp.bfloat16),
        pltpu.VMEM((min(COLUMNS, examples), count), jnp.float32),
    ]


def first_scores(queries, left_inv, right_inv, store):
    small = [pltpu.VMEM((KIN, KIN), jnp.bfloat16), pltpu.VMEM((KOUT, KOUT), jnp.bfloat16)]
    sems = [pltpu.SemaphoreType.DMA((n,)) for n in (1, 1, PIECES, STORE_COPIES)]
    outs = (
        jax.ShapeDtypeStruct((PAIR, PAIR), jnp.bfloat16),
        jax.ShapeDtypeStruct((WIDE, WIDE), jnp.bfloat16),
    )
    operands = [in_hbm(a) for a in (queries, left_inv, right_inv, store)]
    return call(
        first_kernel, queries, store, outs, [HBM] * 4,
        small + buffers(queries, store) + sems, operands,
    )


def later_scores(queries, both, mixer, store, sent):
    sems = [pltpu.SemaphoreType.DMA((STORE_COPIES,))]
    return call(
        functools.partial(later_kernel, len(sent)), queries, store, (),
        [VMEM] * 3 + [HBM] + [VMEM] * len(sent), buffers(queries, store) + sems,
        [queries, both, mixer, in_hbm(store), *sent],
    )[0]


def swap(block, bit):
    route = [(i, i ^ bit) for i in range(lax.axis_size("layer"))]
    return lax.ppermute(block, "layer", route)


HALVE, EXCHANGE, DOUBLE = range(3)


class LayerSum:
    def __init__(self, block, bits, index):
        self.block, self.index = block, index
        self.moves = [(bit, HALVE) for bit in bits[:-1]]
        self.moves += [(bit, EXCHANGE) for bit in bits[-1:]]
        self.moves += [(bit, DOUBLE) for bit in reversed(bits[:-1])]
        if len(bits) < 2:
            self.block = block.astype(jnp.bfloat16)

    def send(self, order):
        bit, kind = self.moves[0]
        sent = self.block
        if kind == HALVE:
            rows = self.block.shape[0] // 2
            upper = (self.index & bit) // bit
            sent = lax.dynamic_slice_in_dim(self.block, (1 - upper) * rows, rows, 0)
            sent = sent.astype(jnp.bfloat16)
            self.block = lax.dynamic_slice_in_dim(self.block, upper * rows, rows, 0)
        self.sent = order.mark(sent)
        self.received = swap(self.sent, bit)

    def bytes_of_move(self):
        size = self.block.size
        return size if self.moves[0][1] == HALVE else 2 * size

    def take(self, order):
        bit, kind = self.moves.pop(0)
        received = order.mark(self.received)
        mine = self.block
        if kind == DOUBLE:
            low = (self.index & bit) == 0
            self.block = jnp.concatenate(
                [jnp.where(low, mine, received), jnp.where(low, received, mine)], 0
            )
            return
        self.block = mine.astype(jnp.float32) + received.astype(jnp.float32)
        if not (self.moves and self.moves[0][1] == HALVE):
            self.block = self.block.astype(jnp.bfloat16)


class Order:
    def __init__(self):
        self.last = jnp.zeros((), jnp.float32)

    def after(self, value):
        value, _ = lax.optimization_barrier((value, self.last))
        return value

    def mark(self, value):
        value, self.last = lax.optimization_barrier((value, self.last))
        return value


class Clock:
    def __init__(self):
        self.now = 0.0
        self.links = {}
        self.arrivals = {}

    def send(self, chunk):
        bit, _ = chunk.moves[0]
        far = bit > 2
        self.now += FAR_START_US if far else NEAR_START_US
        begin = max(self.now, self.links.get(bit, 0.0))
        end = begin + chunk.bytes_of_move() / (FAR_BYTES_PER_US if far else NEAR_BYTES_PER_US)
        self.links[bit] = end
        self.arrivals[chunk] = end + (2 * LATENCY_US if far else LATENCY_US)

    def next(self):
        there = [chunk for chunk, at in self.arrivals.items() if at <= self.now]
        return there[-1] if there else min(self.arrivals, key=self.arrivals.get)

    def take(self, chunk):
        self.now = max(self.now, self.arrivals.pop(chunk))


def send(chunk, order, clock):
    if chunk.moves:
        clock.send(chunk)
        chunk.send(order)


def shards(store, queries, left_inv, right_inv, query_prompt, winner):
    rows = queries.shape[1]
    columns = store.shape[1]
    ex_count = lax.axis_size("ex")
    position = lax.axis_index("ex")
    count = lax.axis_size("layer")
    index = lax.axis_index("layer")
    bits = [1 << k for k in range(count.bit_length() - 1)]
    orders = [bits, bits[1:2] + bits[:1] + bits[2:]]
    order, clock = Order(), Clock()
    chunks, places = [], []
    current = queries
    for step in range(ex_count):
        if step == 0:
            part, both, mixer = first_scores(queries, left_inv, right_inv, store)
        else:
            route = [((i - 1) % ex_count, i) for i in range(ex_count)]
            current = lax.ppermute(current, "ex", route)
            sent = [chunk.sent for chunk in chunks if chunk.moves]
            part = order.mark(later_scores(order.after(current), both, mixer, store, sent))
            clock.now += KERNEL_US
            for chunk in chunks:
                clock.take(chunk)
                chunk.take(order)
                send(chunk, order, clock)
        choices = ORDERS[min(step, len(ORDERS) - 1)]
        width = columns // len(choices)
        for number, choice in enumerate(choices):
            first = number * width
            chunk = LayerSum(part[:, first : first + width], orders[choice], index)
            send(chunk, order, clock)
            chunks.append(chunk)
            places.append(((position - step) % ex_count * rows, jnp.int32(first)))
    while clock.arrivals:
        chunk = clock.next()
        clock.take(chunk)
        chunk.take(order)
        send(chunk, order, clock)
    done = [chunk.block for chunk in chunks]
    scores = jnp.zeros((rows * ex_count, columns), jnp.bfloat16)
    for place, block in zip(places, done):
        scores = lax.dynamic_update_slice(scores, block, place)
    ids = jnp.arange(scores.shape[0], dtype=jnp.int32)
    prompts = jnp.arange(winner.shape[0], dtype=jnp.int32)
    picks = (winner[:, None] == ids[None, :]).astype(jnp.float32)
    member = (query_prompt[None, :] == prompts[:, None]).astype(jnp.float32)
    weights = (picks - member / BEST).astype(jnp.bfloat16)
    advantage = jnp.dot(weights, scores, preferred_element_type=jnp.float32)
    return (scores, advantage.astype(jnp.bfloat16))


def solution(mesh):
    return jax.shard_map(
        shards,
        mesh=mesh,
        in_specs=(
            P("layer", ("grp", "ex"), None),
            P("layer", ("grp", "ex"), None),
            P("layer", None, None),
            P("layer", None, None),
            P("grp"),
            P("grp"),
        ),
        out_specs=(P(None, ("grp", "ex")), P(None, ("grp", "ex"))),
        check_vma=False,
    )
```

```python
import functools

import jax
import jax.numpy as jnp
from jax import lax
from jax.experimental import pallas as pl
from jax.experimental.pallas import tpu as pltpu
from jax.sharding import PartitionSpec as P

KIN = 32
KOUT = 128
BEST = 4
ROWS = 8
WIDE = KIN * ROWS
PAIR = 2 * KOUT
DEPTH_BLOCK = 2048
COLUMNS = 512
ORDERS = ((1, 0), (1, 0))
NEAR_START_US = 1.1
FAR_START_US = 1.5
LATENCY_US = 0.5
NEAR_BYTES_PER_US = 50000
FAR_BYTES_PER_US = 25000
KERNEL_US = 5.3
PIECES = 4
STORE_COPIES = 8
VMEM_LIMIT = 32 * 1024 * 1024
NT = (((1,), (1,)), ((), ()))


def left_matrix(left):
    row = lax.broadcasted_iota(jnp.int32, (WIDE, KIN), 0)
    column = lax.broadcasted_iota(jnp.int32, (WIDE, KIN), 1)
    spread = jnp.where((row >> 3) == column, 1.0, 0.0).astype(jnp.bfloat16)
    tall = jnp.dot(spread, left, preferred_element_type=jnp.float32).astype(jnp.bfloat16)
    full = lax.dot_general(tall, spread, NT, preferred_element_type=jnp.float32)
    row = lax.broadcasted_iota(jnp.int32, (WIDE, WIDE), 0)
    column = lax.broadcasted_iota(jnp.int32, (WIDE, WIDE), 1)
    return jnp.where((row & (ROWS - 1)) == (column & (ROWS - 1)), full, 0.0).astype(jnp.bfloat16)


def right_matrix(right):
    zero = jnp.zeros_like(right)
    return jnp.concatenate(
        [jnp.concatenate([right, zero], 1), jnp.concatenate([zero, right], 1)], 0
    )


def side_by_side_to_stacked(block):
    tiles = block.reshape(block.shape[0] // ROWS, ROWS, PAIR)
    return jnp.concatenate([tiles[:, :, :KOUT], tiles[:, :, KOUT:]], 1)


def precondition(rows_ref, both, mixer, half_ref, pre_ref, before):
    rows = rows_ref.shape[0] // PIECES

    def piece(step, carry):
        before(step)
        at = pl.ds(pl.multiple_of(step * rows, rows), rows)
        block = jnp.concatenate(
            [rows_ref[at, p * PAIR : (p + 1) * PAIR] for p in range(KIN // 2)], 0
        )
        half = jnp.dot(block, both, preferred_element_type=jnp.float32)
        groups = pl.ds(step * (rows // ROWS), rows // ROWS)
        for p in range(KIN // 2):
            half_ref[groups, 2 * ROWS * p : 2 * ROWS * (p + 1), :] = side_by_side_to_stacked(
                half[p * rows : (p + 1) * rows]
            ).astype(jnp.bfloat16)
        return carry

    lax.fori_loop(0, PIECES, piece, 0)

    def groups(index, carry):
        stacked = jnp.concatenate([half_ref[2 * index], half_ref[2 * index + 1]], 1)
        mixed = side_by_side_to_stacked(
            jnp.dot(mixer, stacked, preferred_element_type=jnp.float32)
        ).astype(jnp.bfloat16)
        at = pl.ds(pl.multiple_of(index * 2 * ROWS, 2 * ROWS), 2 * ROWS)
        for i in range(KIN):
            pre_ref[at, i * KOUT : (i + 1) * KOUT] = mixed[i]
        return carry

    lax.fori_loop(0, rows_ref.shape[0] // (2 * ROWS), groups, 0, unroll=8)


def copy_of(source_ref, target_ref, sems, step):
    rows = target_ref.shape[0] // sems.shape[0]
    at = pl.ds(pl.multiple_of(step * rows, rows), rows)
    return pltpu.make_async_copy(source_ref.at[at], target_ref.at[at], sems.at[step])


def start_store(store_ref, store_vmem, sems, step):
    share = sems.shape[0] // PIECES
    for k in range(share):
        copy_of(store_ref.at[0], store_vmem, sems, step * share + k).start()


def dots(pre_ref, store_ref, store_vmem, sems, total_ref, out_ref):
    columns = total_ref.shape[0]
    depth = pre_ref.shape[1]
    blocks = store_vmem.shape[0] // columns
    share = sems.shape[0] // blocks

    def block(step, carry):
        for k in range(share):
            copy_of(store_ref.at[0], store_vmem, sems, step * share + k).wait()
        rows = pl.ds(pl.multiple_of(step * columns, columns), columns)
        for at in range(0, depth, DEPTH_BLOCK):
            term = lax.dot_general(
                store_vmem[rows, at : at + DEPTH_BLOCK],
                pre_ref[:, at : at + DEPTH_BLOCK],
                NT,
                preferred_element_type=jnp.float32,
            )
            if at == 0:
                total_ref[...] = term
            elif at + DEPTH_BLOCK < depth:
                total_ref[...] += term
            else:
                out_ref[:, rows] = (total_ref[...] + term).T
        return carry

    lax.fori_loop(0, blocks, block, 0)


def first_kernel(
    rows_ref, left_ref, right_ref, store_ref, out_ref, both_ref, mixer_ref,
    left_vmem, right_vmem, rows_vmem, store_vmem, half_ref, total_ref,
    left_sems, right_sems, rows_sems, store_sems,
):
    right = copy_of(right_ref.at[0], right_vmem, right_sems, 0)
    left = copy_of(left_ref.at[0], left_vmem, left_sems, 0)
    right.start()
    left.start()
    for step in range(PIECES):
        copy_of(rows_ref.at[0], rows_vmem, rows_sems, step).start()
    right.wait()
    both_ref[...] = right_matrix(right_vmem[...])
    left.wait()
    mixer_ref[...] = left_matrix(left_vmem[...])

    def before(step):
        copy_of(rows_ref.at[0], rows_vmem, rows_sems, step).wait()
        start_store(store_ref, store_vmem, store_sems, step)

    precondition(rows_vmem, both_ref[...], mixer_ref[...], half_ref, rows_vmem, before)
    dots(rows_vmem, store_ref, store_vmem, store_sems, total_ref, out_ref)


def later_kernel(
    sent, rows_ref, both_ref, mixer_ref, store_ref, *refs,
):
    out_ref, pre_ref, store_vmem, half_ref, total_ref, store_sems = refs[sent:]

    def before(step):
        start_store(store_ref, store_vmem, store_sems, step)

    precondition(rows_ref.at[0], both_ref[...], mixer_ref[...], half_ref, pre_ref, before)
    dots(pre_ref, store_ref, store_vmem, store_sems, total_ref, out_ref)


VMEM = pl.BlockSpec(memory_space=pltpu.VMEM)
HBM = pl.BlockSpec(memory_space=pltpu.HBM)


def in_hbm(array):
    return pltpu.with_memory_space_constraint(array, pltpu.HBM)


def call(kernel, queries, store, outs, in_specs, scratch, operands):
    count, depth = queries.shape[1:]
    examples = store.shape[1]
    return pl.pallas_call(
        kernel,
        out_shape=(jax.ShapeDtypeStruct((count, examples), jnp.float32),) + outs,
        in_specs=in_specs,
        out_specs=(VMEM,) * (1 + len(outs)),
        scratch_shapes=scratch,
        compiler_params=pltpu.CompilerParams(vmem_limit_bytes=VMEM_LIMIT),
        cost_estimate=pl.CostEstimate(
            flops=2 * count * depth * (examples + 1024),
            bytes_accessed=2 * depth * (count + examples),
            transcendentals=0,
        ),
    )(*operands)


def buffers(queries, store):
    count, depth = queries.shape[1:]
    examples = store.shape[1]
    return [
        pltpu.VMEM((count, depth), jnp.bfloat16),
        pltpu.VMEM((examples, depth), jnp.bfloat16),
        pltpu.VMEM((count // ROWS, WIDE, KOUT), jnp.bfloat16),
        pltpu.VMEM((min(COLUMNS, examples), count), jnp.float32),
    ]


def first_scores(queries, left_inv, right_inv, store):
    small = [pltpu.VMEM((KIN, KIN), jnp.bfloat16), pltpu.VMEM((KOUT, KOUT), jnp.bfloat16)]
    sems = [pltpu.SemaphoreType.DMA((n,)) for n in (1, 1, PIECES, STORE_COPIES)]
    outs = (
        jax.ShapeDtypeStruct((PAIR, PAIR), jnp.bfloat16),
        jax.ShapeDtypeStruct((WIDE, WIDE), jnp.bfloat16),
    )
    operands = [in_hbm(a) for a in (queries, left_inv, right_inv, store)]
    return call(
        first_kernel, queries, store, outs, [HBM] * 4,
        small + buffers(queries, store) + sems, operands,
    )


def later_scores(queries, both, mixer, store, sent):
    sems = [pltpu.SemaphoreType.DMA((STORE_COPIES,))]
    return call(
        functools.partial(later_kernel, len(sent)), queries, store, (),
        [VMEM] * 3 + [HBM] + [VMEM] * len(sent), buffers(queries, store) + sems,
        [queries, both, mixer, in_hbm(store), *sent],
    )[0]


def swap(block, bit):
    route = [(i, i ^ bit) for i in range(lax.axis_size("layer"))]
    return lax.ppermute(block, "layer", route)


HALVE, EXCHANGE, DOUBLE = range(3)


class LayerSum:
    def __init__(self, block, bits, index):
        self.block, self.index = block, index
        self.moves = [(bit, HALVE) for bit in bits[:-1]]
        self.moves += [(bit, EXCHANGE) for bit in bits[-1:]]
        self.moves += [(bit, DOUBLE) for bit in reversed(bits[:-1])]
        if len(bits) < 2:
            self.block = block.astype(jnp.bfloat16)

    def send(self, order):
        bit, kind = self.moves[0]
        sent = self.block
        if kind == HALVE:
            rows = self.block.shape[0] // 2
            upper = (self.index & bit) // bit
            sent = lax.dynamic_slice_in_dim(self.block, (1 - upper) * rows, rows, 0)
            sent = sent.astype(jnp.bfloat16)
            self.block = lax.dynamic_slice_in_dim(self.block, upper * rows, rows, 0)
        self.sent = order.mark(sent)
        self.received = swap(self.sent, bit)

    def bytes_of_move(self):
        size = self.block.size
        return size if self.moves[0][1] == HALVE else 2 * size

    def take(self, order):
        bit, kind = self.moves.pop(0)
        received = order.mark(self.received)
        mine = self.block
        if kind == DOUBLE:
            low = (self.index & bit) == 0
            self.block = jnp.concatenate(
                [jnp.where(low, mine, received), jnp.where(low, received, mine)], 0
            )
            return
        self.block = mine.astype(jnp.float32) + received.astype(jnp.float32)
        if not (self.moves and self.moves[0][1] == HALVE):
            self.block = self.block.astype(jnp.bfloat16)


class Order:
    def __init__(self):
        self.last = jnp.zeros((), jnp.float32)

    def after(self, value):
        value, _ = lax.optimization_barrier((value, self.last))
        return value

    def mark(self, value):
        value, self.last = lax.optimization_barrier((value, self.last))
        return value


class Clock:
    def __init__(self):
        self.now = 0.0
        self.links = {}
        self.arrivals = {}

    def send(self, chunk):
        bit, _ = chunk.moves[0]
        far = bit > 2
        self.now += FAR_START_US if far else NEAR_START_US
        begin = max(self.now, self.links.get(bit, 0.0))
        end = begin + chunk.bytes_of_move() / (FAR_BYTES_PER_US if far else NEAR_BYTES_PER_US)
        self.links[bit] = end
        self.arrivals[chunk] = end + (2 * LATENCY_US if far else LATENCY_US)

    def next(self):
        there = [chunk for chunk, at in self.arrivals.items() if at <= self.now]
        return there[-1] if there else min(self.arrivals, key=self.arrivals.get)

    def take(self, chunk):
        self.now = max(self.now, self.arrivals.pop(chunk))


def send(chunk, order, clock):
    if chunk.moves:
        clock.send(chunk)
        chunk.send(order)


def shards(store, queries, left_inv, right_inv, query_prompt, winner):
    rows = queries.shape[1]
    columns = store.shape[1]
    ex_count = lax.axis_size("ex")
    position = lax.axis_index("ex")
    count = lax.axis_size("layer")
    index = lax.axis_index("layer")
    bits = [1 << k for k in range(count.bit_length() - 1)]
    orders = [bits, bits[1:2] + bits[:1] + bits[2:]]
    order, clock = Order(), Clock()
    weights = lax.optimization_barrier(prompt_weights(query_prompt, winner))
    chunks, places = [], []
    current = queries
    for step in range(ex_count):
        if step == 0:
            part, both, mixer = first_scores(queries, left_inv, right_inv, store)
        else:
            route = [((i - 1) % ex_count, i) for i in range(ex_count)]
            current = lax.ppermute(current, "ex", route)
            sent = [chunk.sent for chunk in chunks if chunk.moves]
            part = order.mark(later_scores(order.after(current), both, mixer, store, sent))
            clock.now += KERNEL_US
            for chunk in chunks:
                clock.take(chunk)
                chunk.take(order)
                send(chunk, order, clock)
        choices = ORDERS[min(step, len(ORDERS) - 1)]
        width = columns // len(choices)
        for number, choice in enumerate(choices):
            first = number * width
            chunk = LayerSum(part[:, first : first + width], orders[choice], index)
            send(chunk, order, clock)
            chunks.append(chunk)
            places.append((step, first))
    while clock.arrivals:
        chunk = clock.next()
        clock.take(chunk)
        chunk.take(order)
        send(chunk, order, clock)
    done = [chunk.block for chunk in chunks]
    blocks = [
        jnp.concatenate([block for block, (at, _) in zip(done, places) if at == step], 1)
        for step in range(ex_count)
    ]
    scores = jnp.concatenate(
        [pick(blocks, (position - core) % ex_count) for core in range(ex_count)], 0
    )
    advantage = jnp.dot(weights, scores, preferred_element_type=jnp.float32)
    return (scores, advantage.astype(jnp.bfloat16))


def pick(blocks, step):
    out = blocks[0]
    for k, block in enumerate(blocks[1:], 1):
        out = jnp.where(step == k, block, out)
    return out


def prompt_weights(query_prompt, winner):
    ids = jnp.arange(query_prompt.shape[0], dtype=jnp.int32)
    prompts = jnp.arange(winner.shape[0], dtype=jnp.int32)
    picks = (winner[:, None] == ids[None, :]).astype(jnp.float32)
    member = (query_prompt[None, :] == prompts[:, None]).astype(jnp.float32)
    return (picks - member / BEST).astype(jnp.bfloat16)


def solution(mesh):
    return jax.shard_map(
        shards,
        mesh=mesh,
        in_specs=(
            P("layer", ("grp", "ex"), None),
            P("layer", ("grp", "ex"), None),
            P("layer", None, None),
            P("layer", None, None),
            P("grp"),
            P("grp"),
        ),
        out_specs=(P(None, ("grp", "ex")), P(None, ("grp", "ex"))),
        check_vma=False,
    )
```

```python
import functools

import jax
import jax.numpy as jnp
from jax import lax
from jax.experimental import pallas as pl
from jax.experimental.pallas import tpu as pltpu
from jax.sharding import PartitionSpec as P

KIN = 32
KOUT = 128
BEST = 4
ROWS = 8
WIDE = KIN * ROWS
PAIR = 2 * KOUT
DEPTH_BLOCK = 2048
COLUMNS = 512
ORDERS = ((1, 0), (1, 0))
NEAR_START_US = 1.1
FAR_START_US = 1.5
LATENCY_US = 0.5
NEAR_BYTES_PER_US = 50000
FAR_BYTES_PER_US = 25000
KERNEL_US = 5.3
PIECES = 4
STORE_COPIES = 8
VMEM_LIMIT = 32 * 1024 * 1024
NT = (((1,), (1,)), ((), ()))


def left_matrix(left):
    row = lax.broadcasted_iota(jnp.int32, (WIDE, KIN), 0)
    column = lax.broadcasted_iota(jnp.int32, (WIDE, KIN), 1)
    spread = jnp.where((row >> 3) == column, 1.0, 0.0).astype(jnp.bfloat16)
    tall = jnp.dot(spread, left, preferred_element_type=jnp.float32).astype(jnp.bfloat16)
    full = lax.dot_general(tall, spread, NT, preferred_element_type=jnp.float32)
    row = lax.broadcasted_iota(jnp.int32, (WIDE, WIDE), 0)
    column = lax.broadcasted_iota(jnp.int32, (WIDE, WIDE), 1)
    return jnp.where((row & (ROWS - 1)) == (column & (ROWS - 1)), full, 0.0).astype(jnp.bfloat16)


def right_matrix(right):
    zero = jnp.zeros_like(right)
    return jnp.concatenate(
        [jnp.concatenate([right, zero], 1), jnp.concatenate([zero, right], 1)], 0
    )


def side_by_side_to_stacked(block):
    tiles = block.reshape(block.shape[0] // ROWS, ROWS, PAIR)
    return jnp.concatenate([tiles[:, :, :KOUT], tiles[:, :, KOUT:]], 1)


def precondition(rows_ref, both, mixer, half_ref, pre_ref, before):
    rows = rows_ref.shape[0] // PIECES

    def piece(step, carry):
        before(step)
        at = pl.ds(pl.multiple_of(step * rows, rows), rows)
        block = jnp.concatenate(
            [rows_ref[at, p * PAIR : (p + 1) * PAIR] for p in range(KIN // 2)], 0
        )
        half = jnp.dot(block, both, preferred_element_type=jnp.float32)
        groups = pl.ds(step * (rows // ROWS), rows // ROWS)
        for p in range(KIN // 2):
            half_ref[groups, 2 * ROWS * p : 2 * ROWS * (p + 1), :] = side_by_side_to_stacked(
                half[p * rows : (p + 1) * rows]
            ).astype(jnp.bfloat16)
        return carry

    lax.fori_loop(0, PIECES, piece, 0)

    def groups(index, carry):
        stacked = jnp.concatenate([half_ref[2 * index], half_ref[2 * index + 1]], 1)
        mixed = side_by_side_to_stacked(
            jnp.dot(mixer, stacked, preferred_element_type=jnp.float32)
        ).astype(jnp.bfloat16)
        at = pl.ds(pl.multiple_of(index * 2 * ROWS, 2 * ROWS), 2 * ROWS)
        for i in range(KIN):
            pre_ref[at, i * KOUT : (i + 1) * KOUT] = mixed[i]
        return carry

    lax.fori_loop(0, rows_ref.shape[0] // (2 * ROWS), groups, 0, unroll=8)


def copy_of(source_ref, target_ref, sems, step):
    rows = target_ref.shape[0] // sems.shape[0]
    at = pl.ds(pl.multiple_of(step * rows, rows), rows)
    return pltpu.make_async_copy(source_ref.at[at], target_ref.at[at], sems.at[step])


def start_store(store_ref, store_vmem, sems, step):
    share = sems.shape[0] // PIECES
    for k in range(share):
        copy_of(store_ref.at[0], store_vmem, sems, step * share + k).start()


def dots(pre_ref, store_ref, store_vmem, sems, total_ref, out_ref):
    columns = total_ref.shape[0]
    depth = pre_ref.shape[1]
    blocks = store_vmem.shape[0] // columns
    share = sems.shape[0] // blocks

    def block(step, carry):
        for k in range(share):
            copy_of(store_ref.at[0], store_vmem, sems, step * share + k).wait()
        rows = pl.ds(pl.multiple_of(step * columns, columns), columns)
        for at in range(0, depth, DEPTH_BLOCK):
            term = lax.dot_general(
                store_vmem[rows, at : at + DEPTH_BLOCK],
                pre_ref[:, at : at + DEPTH_BLOCK],
                NT,
                preferred_element_type=jnp.float32,
            )
            if at == 0:
                total_ref[...] = term
            elif at + DEPTH_BLOCK < depth:
                total_ref[...] += term
            else:
                out_ref[:, rows] = (total_ref[...] + term).T
        return carry

    lax.fori_loop(0, blocks, block, 0)


def first_kernel(
    rows_ref, left_ref, right_ref, store_ref, out_ref, both_ref, mixer_ref,
    left_vmem, right_vmem, rows_vmem, store_vmem, half_ref, total_ref,
    left_sems, right_sems, rows_sems, store_sems,
):
    right = copy_of(right_ref.at[0], right_vmem, right_sems, 0)
    left = copy_of(left_ref.at[0], left_vmem, left_sems, 0)
    right.start()
    left.start()
    for step in range(PIECES):
        copy_of(rows_ref.at[0], rows_vmem, rows_sems, step).start()
    right.wait()
    both_ref[...] = right_matrix(right_vmem[...])
    left.wait()
    mixer_ref[...] = left_matrix(left_vmem[...])

    def before(step):
        copy_of(rows_ref.at[0], rows_vmem, rows_sems, step).wait()
        start_store(store_ref, store_vmem, store_sems, step)

    precondition(rows_vmem, both_ref[...], mixer_ref[...], half_ref, rows_vmem, before)
    dots(rows_vmem, store_ref, store_vmem, store_sems, total_ref, out_ref)


def later_kernel(
    sent, rows_ref, both_ref, mixer_ref, store_ref, *refs,
):
    out_ref, pre_ref, store_vmem, half_ref, total_ref, store_sems = refs[sent:]

    def before(step):
        start_store(store_ref, store_vmem, store_sems, step)

    precondition(rows_ref.at[0], both_ref[...], mixer_ref[...], half_ref, pre_ref, before)
    dots(pre_ref, store_ref, store_vmem, store_sems, total_ref, out_ref)


VMEM = pl.BlockSpec(memory_space=pltpu.VMEM)
HBM = pl.BlockSpec(memory_space=pltpu.HBM)


def in_hbm(array):
    return pltpu.with_memory_space_constraint(array, pltpu.HBM)


def call(kernel, queries, store, outs, in_specs, scratch, operands):
    count, depth = queries.shape[1:]
    examples = store.shape[1]
    return pl.pallas_call(
        kernel,
        out_shape=(jax.ShapeDtypeStruct((count, examples), jnp.float32),) + outs,
        in_specs=in_specs,
        out_specs=(VMEM,) * (1 + len(outs)),
        scratch_shapes=scratch,
        compiler_params=pltpu.CompilerParams(vmem_limit_bytes=VMEM_LIMIT),
        cost_estimate=pl.CostEstimate(
            flops=2 * count * depth * (examples + 1024),
            bytes_accessed=2 * depth * (count + examples),
            transcendentals=0,
        ),
    )(*operands)


def buffers(queries, store):
    count, depth = queries.shape[1:]
    examples = store.shape[1]
    return [
        pltpu.VMEM((count, depth), jnp.bfloat16),
        pltpu.VMEM((examples, depth), jnp.bfloat16),
        pltpu.VMEM((count // ROWS, WIDE, KOUT), jnp.bfloat16),
        pltpu.VMEM((min(COLUMNS, examples), count), jnp.float32),
    ]


def first_scores(queries, left_inv, right_inv, store):
    small = [pltpu.VMEM((KIN, KIN), jnp.bfloat16), pltpu.VMEM((KOUT, KOUT), jnp.bfloat16)]
    sems = [pltpu.SemaphoreType.DMA((n,)) for n in (1, 1, PIECES, STORE_COPIES)]
    outs = (
        jax.ShapeDtypeStruct((PAIR, PAIR), jnp.bfloat16),
        jax.ShapeDtypeStruct((WIDE, WIDE), jnp.bfloat16),
    )
    operands = [in_hbm(a) for a in (queries, left_inv, right_inv, store)]
    return call(
        first_kernel, queries, store, outs, [HBM] * 4,
        small + buffers(queries, store) + sems, operands,
    )


def later_scores(queries, both, mixer, store, sent):
    sems = [pltpu.SemaphoreType.DMA((STORE_COPIES,))]
    return call(
        functools.partial(later_kernel, len(sent)), queries, store, (),
        [VMEM] * 3 + [HBM] + [VMEM] * len(sent), buffers(queries, store) + sems,
        [queries, both, mixer, in_hbm(store), *sent],
    )[0]


def swap(block, bit, cores):
    ex_count = lax.axis_size("ex")
    route = [
        (i * ex_count + core, (i ^ bit) * ex_count + core)
        for i in range(lax.axis_size("layer"))
        for core in cores
    ]
    return lax.ppermute(block, ("layer", "ex"), route)


def hand_over(block, source, target):
    return lax.ppermute(block, "ex", [(source, target)])


HALVE, EXCHANGE, DOUBLE = range(3)


class LayerSum:
    def __init__(self, block, bits, index, cores):
        self.block, self.index, self.cores = block, index, cores
        self.moves = [(bit, HALVE) for bit in bits[:-1]]
        self.moves += [(bit, EXCHANGE) for bit in bits[-1:]]
        self.moves += [(bit, DOUBLE) for bit in reversed(bits[:-1])]
        if len(bits) < 2:
            self.block = block.astype(jnp.bfloat16)

    def send(self, order):
        bit, kind = self.moves[0]
        sent = self.block
        if kind == HALVE:
            rows = self.block.shape[0] // 2
            upper = (self.index & bit) // bit
            sent = lax.dynamic_slice_in_dim(self.block, (1 - upper) * rows, rows, 0)
            sent = sent.astype(jnp.bfloat16)
            self.block = lax.dynamic_slice_in_dim(self.block, upper * rows, rows, 0)
        self.sent = order.mark(sent)
        self.received = swap(self.sent, bit, self.cores)

    def bytes_of_move(self):
        size = self.block.size
        size = size if self.moves[0][1] == HALVE else 2 * size
        return size * len(self.cores) // lax.axis_size("ex")

    def take(self, order):
        bit, kind = self.moves.pop(0)
        received = order.mark(self.received)
        mine = self.block
        if kind == DOUBLE:
            low = (self.index & bit) == 0
            self.block = jnp.concatenate(
                [jnp.where(low, mine, received), jnp.where(low, received, mine)], 0
            )
            return
        self.block = mine.astype(jnp.float32) + received.astype(jnp.float32)
        if not (self.moves and self.moves[0][1] == HALVE):
            self.block = self.block.astype(jnp.bfloat16)


class Order:
    def __init__(self):
        self.last = jnp.zeros((), jnp.float32)

    def after(self, value):
        value, _ = lax.optimization_barrier((value, self.last))
        return value

    def mark(self, value):
        value, self.last = lax.optimization_barrier((value, self.last))
        return value


class Clock:
    def __init__(self):
        self.now = 0.0
        self.links = {}
        self.arrivals = {}

    def send(self, chunk):
        bit, _ = chunk.moves[0]
        far = bit > 2
        self.now += FAR_START_US if far else NEAR_START_US
        begin = max(self.now, self.links.get(bit, 0.0))
        end = begin + chunk.bytes_of_move() / (FAR_BYTES_PER_US if far else NEAR_BYTES_PER_US)
        self.links[bit] = end
        self.arrivals[chunk] = end + (2 * LATENCY_US if far else LATENCY_US)

    def next(self):
        there = [chunk for chunk, at in self.arrivals.items() if at <= self.now]
        return there[-1] if there else min(self.arrivals, key=self.arrivals.get)

    def take(self, chunk):
        self.now = max(self.now, self.arrivals.pop(chunk))


def send(chunk, order, clock):
    if chunk.moves:
        clock.send(chunk)
        chunk.send(order)


def shards(store, queries, left_inv, right_inv, query_prompt, winner):
    rows = queries.shape[1]
    columns = store.shape[1]
    ex_count = lax.axis_size("ex")
    position = lax.axis_index("ex")
    count = lax.axis_size("layer")
    index = lax.axis_index("layer")
    bits = [1 << k for k in range(count.bit_length() - 1)]
    orders = [bits, bits[1:2] + bits[:1] + bits[2:]]
    order, clock = Order(), Clock()
    shared = None
    chunks, places = [], []
    current = queries
    for step in range(ex_count):
        if step == 0:
            part, both, mixer = first_scores(queries, left_inv, right_inv, store)
        else:
            route = [((i - 1) % ex_count, i) for i in range(ex_count)]
            current = lax.ppermute(current, "ex", route)
            sent = [chunk.sent for chunk in chunks if chunk.moves]
            part = order.mark(later_scores(order.after(current), both, mixer, store, sent))
            clock.now += KERNEL_US
            for chunk in chunks:
                clock.take(chunk)
                chunk.take(order)
                send(chunk, order, clock)
        choices = ORDERS[min(step, len(ORDERS) - 1)]
        width = columns // len(choices)
        for number, choice in enumerate(choices):
            first = number * width
            block, cores = part[:, first : first + width], range(ex_count)
            if step == 0 and number == 1 and ex_count == 2:
                given = hand_over(order.mark(block.astype(jnp.bfloat16)), 0, 1)
                shared, given_block = len(chunks), block
                places.append(((position - step) % ex_count * rows, jnp.int32(first)))
                chunks.append(None)
                continue
            chunk = LayerSum(block, orders[choice], index, cores)
            send(chunk, order, clock)
            chunks.append(chunk)
            places.append(((position - step) % ex_count * rows, jnp.int32(first)))
        if step == 0 and shared is not None:
            block = jnp.concatenate([given_block, order.mark(given).astype(jnp.float32)], 1)
            chunks[shared] = LayerSum(block, orders[choices[1]], index, (1,))
            send(chunks[shared], order, clock)
    while clock.arrivals:
        chunk = clock.next()
        clock.take(chunk)
        chunk.take(order)
        send(chunk, order, clock)
    done = [chunk.block for chunk in chunks]
    if shared is not None:
        mine, theirs = jnp.split(done[shared], 2, 1)
        done[shared] = jnp.where(position == 1, mine, hand_over(theirs, 1, 0))
    scores = jnp.zeros((rows * ex_count, columns), jnp.bfloat16)
    for place, block in zip(places, done):
        scores = lax.dynamic_update_slice(scores, block, place)
    ids = jnp.arange(scores.shape[0], dtype=jnp.int32)
    prompts = jnp.arange(winner.shape[0], dtype=jnp.int32)
    picks = (winner[:, None] == ids[None, :]).astype(jnp.float32)
    member = (query_prompt[None, :] == prompts[:, None]).astype(jnp.float32)
    weights = (picks - member / BEST).astype(jnp.bfloat16)
    advantage = jnp.dot(weights, scores, preferred_element_type=jnp.float32)
    return (scores, advantage.astype(jnp.bfloat16))


def solution(mesh):
    return jax.shard_map(
        shards,
        mesh=mesh,
        in_specs=(
            P("layer", ("grp", "ex"), None),
            P("layer", ("grp", "ex"), None),
            P("layer", None, None),
            P("layer", None, None),
            P("grp"),
            P("grp"),
        ),
        out_specs=(P(None, ("grp", "ex")), P(None, ("grp", "ex"))),
        check_vma=False,
    )
```

```python
import functools

import jax
import jax.numpy as jnp
from jax import lax
from jax.experimental import pallas as pl
from jax.experimental.pallas import tpu as pltpu
from jax.sharding import PartitionSpec as P

KIN = 32
KOUT = 128
BEST = 4
ROWS = 8
WIDE = KIN * ROWS
PAIR = 2 * KOUT
DEPTH_BLOCK = 2048
COLUMNS = 512
ORDERS = (((1, 1), (0, 1)), ((1, 1), (0, 1)))
NEAR_START_US = 1.1
FAR_START_US = 1.5
LATENCY_US = 0.5
NEAR_BYTES_PER_US = 50000
FAR_BYTES_PER_US = 25000
KERNEL_US = 5.3
PIECES = 4
STORE_COPIES = 8
VMEM_LIMIT = 20 * 1024 * 1024
NT = (((1,), (1,)), ((), ()))


def left_matrix(left):
    row = lax.broadcasted_iota(jnp.int32, (WIDE, KIN), 0)
    column = lax.broadcasted_iota(jnp.int32, (WIDE, KIN), 1)
    spread = jnp.where((row >> 3) == column, 1.0, 0.0).astype(jnp.bfloat16)
    tall = jnp.dot(spread, left, preferred_element_type=jnp.float32).astype(jnp.bfloat16)
    full = lax.dot_general(tall, spread, NT, preferred_element_type=jnp.float32)
    row = lax.broadcasted_iota(jnp.int32, (WIDE, WIDE), 0)
    column = lax.broadcasted_iota(jnp.int32, (WIDE, WIDE), 1)
    return jnp.where((row & (ROWS - 1)) == (column & (ROWS - 1)), full, 0.0).astype(jnp.bfloat16)


def right_matrix(right):
    zero = jnp.zeros_like(right)
    return jnp.concatenate(
        [jnp.concatenate([right, zero], 1), jnp.concatenate([zero, right], 1)], 0
    )


def side_by_side_to_stacked(block):
    tiles = block.reshape(block.shape[0] // ROWS, ROWS, PAIR)
    return jnp.concatenate([tiles[:, :, :KOUT], tiles[:, :, KOUT:]], 1)


def precondition(rows_ref, both, mixer, half_ref, pre_ref, before):
    rows = rows_ref.shape[0] // PIECES

    def piece(step, carry):
        before(step)
        at = pl.ds(pl.multiple_of(step * rows, rows), rows)
        block = jnp.concatenate(
            [rows_ref[at, p * PAIR : (p + 1) * PAIR] for p in range(KIN // 2)], 0
        )
        half = jnp.dot(block, both, preferred_element_type=jnp.float32)
        groups = pl.ds(step * (rows // ROWS), rows // ROWS)
        for p in range(KIN // 2):
            half_ref[groups, 2 * ROWS * p : 2 * ROWS * (p + 1), :] = side_by_side_to_stacked(
                half[p * rows : (p + 1) * rows]
            ).astype(jnp.bfloat16)
        return carry

    lax.fori_loop(0, PIECES, piece, 0)

    def groups(index, carry):
        stacked = jnp.concatenate([half_ref[2 * index], half_ref[2 * index + 1]], 1)
        mixed = side_by_side_to_stacked(
            jnp.dot(mixer, stacked, preferred_element_type=jnp.float32)
        ).astype(jnp.bfloat16)
        at = pl.ds(pl.multiple_of(index * 2 * ROWS, 2 * ROWS), 2 * ROWS)
        for i in range(KIN):
            pre_ref[at, i * KOUT : (i + 1) * KOUT] = mixed[i]
        return carry

    lax.fori_loop(0, rows_ref.shape[0] // (2 * ROWS), groups, 0, unroll=8)


def copy_of(source_ref, target_ref, sems, step):
    rows = target_ref.shape[0] // sems.shape[0]
    at = pl.ds(pl.multiple_of(step * rows, rows), rows)
    return pltpu.make_async_copy(source_ref.at[at], target_ref.at[at], sems.at[step])


def start_store(store_ref, store_vmem, sems, step):
    share = sems.shape[0] // PIECES
    for k in range(share):
        copy_of(store_ref.at[0], store_vmem, sems, step * share + k).start()


def dots(pre_ref, store_ref, store_vmem, sems, total_ref, out_ref):
    columns = total_ref.shape[0]
    depth = pre_ref.shape[1]
    blocks = store_vmem.shape[0] // columns
    share = sems.shape[0] // blocks

    def block(step, carry):
        for k in range(share):
            copy_of(store_ref.at[0], store_vmem, sems, step * share + k).wait()
        rows = pl.ds(pl.multiple_of(step * columns, columns), columns)
        for at in range(0, depth, DEPTH_BLOCK):
            term = lax.dot_general(
                store_vmem[rows, at : at + DEPTH_BLOCK],
                pre_ref[:, at : at + DEPTH_BLOCK],
                NT,
                preferred_element_type=jnp.float32,
            )
            if at == 0:
                total_ref[...] = term
            elif at + DEPTH_BLOCK < depth:
                total_ref[...] += term
            else:
                out_ref[:, rows] = (total_ref[...] + term).T
        return carry

    lax.fori_loop(0, blocks, block, 0)


def first_kernel(
    rows_ref, left_ref, right_ref, store_ref, out_ref, both_ref, mixer_ref,
    left_vmem, right_vmem, rows_vmem, store_vmem, half_ref, total_ref,
    left_sems, right_sems, rows_sems, store_sems,
):
    right = copy_of(right_ref.at[0], right_vmem, right_sems, 0)
    left = copy_of(left_ref.at[0], left_vmem, left_sems, 0)
    right.start()
    left.start()
    for step in range(PIECES):
        copy_of(rows_ref.at[0], rows_vmem, rows_sems, step).start()
    right.wait()
    both_ref[...] = right_matrix(right_vmem[...])
    left.wait()
    mixer_ref[...] = left_matrix(left_vmem[...])

    def before(step):
        copy_of(rows_ref.at[0], rows_vmem, rows_sems, step).wait()
        start_store(store_ref, store_vmem, store_sems, step)

    precondition(rows_vmem, both_ref[...], mixer_ref[...], half_ref, rows_vmem, before)
    dots(rows_vmem, store_ref, store_vmem, store_sems, total_ref, out_ref)


def later_kernel(
    sent, rows_ref, both_ref, mixer_ref, store_ref, *refs,
):
    out_ref, pre_ref, store_vmem, half_ref, total_ref, store_sems = refs[sent:]

    def before(step):
        start_store(store_ref, store_vmem, store_sems, step)

    precondition(rows_ref.at[0], both_ref[...], mixer_ref[...], half_ref, pre_ref, before)
    dots(pre_ref, store_ref, store_vmem, store_sems, total_ref, out_ref)


VMEM = pl.BlockSpec(memory_space=pltpu.VMEM)
HBM = pl.BlockSpec(memory_space=pltpu.HBM)


def in_hbm(array):
    return pltpu.with_memory_space_constraint(array, pltpu.HBM)


def call(kernel, queries, store, outs, in_specs, scratch, operands):
    count, depth = queries.shape[1:]
    examples = store.shape[1]
    return pl.pallas_call(
        kernel,
        out_shape=(jax.ShapeDtypeStruct((count, examples), jnp.float32),) + outs,
        in_specs=in_specs,
        out_specs=(VMEM,) * (1 + len(outs)),
        scratch_shapes=scratch,
        compiler_params=pltpu.CompilerParams(vmem_limit_bytes=VMEM_LIMIT),
        cost_estimate=pl.CostEstimate(
            flops=2 * count * depth * (examples + 1024),
            bytes_accessed=2 * depth * (count + examples),
            transcendentals=0,
        ),
    )(*operands)


def buffers(queries, store):
    count, depth = queries.shape[1:]
    examples = store.shape[1]
    return [
        pltpu.VMEM((count, depth), jnp.bfloat16),
        pltpu.VMEM((examples, depth), jnp.bfloat16),
        pltpu.VMEM((count // ROWS, WIDE, KOUT), jnp.bfloat16),
        pltpu.VMEM((min(COLUMNS, examples), count), jnp.float32),
    ]


def first_scores(queries, left_inv, right_inv, store):
    small = [pltpu.VMEM((KIN, KIN), jnp.bfloat16), pltpu.VMEM((KOUT, KOUT), jnp.bfloat16)]
    sems = [pltpu.SemaphoreType.DMA((n,)) for n in (1, 1, PIECES, STORE_COPIES)]
    outs = (
        jax.ShapeDtypeStruct((PAIR, PAIR), jnp.bfloat16),
        jax.ShapeDtypeStruct((WIDE, WIDE), jnp.bfloat16),
    )
    operands = [in_hbm(a) for a in (queries, left_inv, right_inv, store)]
    return call(
        first_kernel, queries, store, outs, [HBM] * 4,
        small + buffers(queries, store) + sems, operands,
    )


def later_scores(queries, both, mixer, store, sent):
    sems = [pltpu.SemaphoreType.DMA((STORE_COPIES,))]
    return call(
        functools.partial(later_kernel, len(sent)), queries, store, (),
        [VMEM] * 3 + [HBM] + [VMEM] * len(sent), buffers(queries, store) + sems,
        [queries, both, mixer, in_hbm(store), *sent],
    )[0]


def swap(block, bit):
    route = [(i, i ^ bit) for i in range(lax.axis_size("layer"))]
    return lax.ppermute(block, "layer", route)


HALVE, EXCHANGE, DOUBLE = range(3)


class LayerSum:
    def __init__(self, block, bits, index, exchanges):
        self.block, self.index = block, index
        halved, exchanged = bits[:-exchanges], bits[-exchanges:]
        self.moves = [(bit, HALVE) for bit in halved]
        self.moves += [(bit, EXCHANGE) for bit in exchanged]
        self.moves += [(bit, DOUBLE) for bit in reversed(halved)]
        if not halved:
            self.block = block.astype(jnp.bfloat16)

    def send(self, order):
        bit, kind = self.moves[0]
        sent = self.block
        if kind == HALVE:
            rows = self.block.shape[0] // 2
            upper = (self.index & bit) // bit
            sent = lax.dynamic_slice_in_dim(self.block, (1 - upper) * rows, rows, 0)
            sent = sent.astype(jnp.bfloat16)
            self.block = lax.dynamic_slice_in_dim(self.block, upper * rows, rows, 0)
        self.sent = order.mark(sent)
        self.received = swap(self.sent, bit)

    def bytes_of_move(self):
        size = self.block.size
        return size if self.moves[0][1] == HALVE else 2 * size

    def take(self, order):
        bit, kind = self.moves.pop(0)
        received = order.mark(self.received)
        mine = self.block
        if kind == DOUBLE:
            low = (self.index & bit) == 0
            self.block = jnp.concatenate(
                [jnp.where(low, mine, received), jnp.where(low, received, mine)], 0
            )
            return
        self.block = mine.astype(jnp.float32) + received.astype(jnp.float32)
        if not (self.moves and self.moves[0][1] == HALVE):
            self.block = self.block.astype(jnp.bfloat16)


class Order:
    def __init__(self):
        self.last = jnp.zeros((), jnp.float32)

    def after(self, value):
        value, _ = lax.optimization_barrier((value, self.last))
        return value

    def mark(self, value):
        value, self.last = lax.optimization_barrier((value, self.last))
        return value


class Clock:
    def __init__(self):
        self.now = 0.0
        self.links = {}
        self.arrivals = {}

    def send(self, chunk):
        bit, _ = chunk.moves[0]
        far = bit > 2
        self.now += FAR_START_US if far else NEAR_START_US
        begin = max(self.now, self.links.get(bit, 0.0))
        end = begin + chunk.bytes_of_move() / (FAR_BYTES_PER_US if far else NEAR_BYTES_PER_US)
        self.links[bit] = end
        self.arrivals[chunk] = end + (2 * LATENCY_US if far else LATENCY_US)

    def next(self):
        there = [chunk for chunk, at in self.arrivals.items() if at <= self.now]
        return there[-1] if there else min(self.arrivals, key=self.arrivals.get)

    def take(self, chunk):
        self.now = max(self.now, self.arrivals.pop(chunk))


def send(chunk, order, clock):
    if chunk.moves:
        clock.send(chunk)
        chunk.send(order)


def shards(store, queries, left_inv, right_inv, query_prompt, winner):
    rows = queries.shape[1]
    columns = store.shape[1]
    ex_count = lax.axis_size("ex")
    position = lax.axis_index("ex")
    count = lax.axis_size("layer")
    index = lax.axis_index("layer")
    bits = [1 << k for k in range(count.bit_length() - 1)]
    orders = [bits, bits[1:2] + bits[:1] + bits[2:]]
    order, clock = Order(), Clock()
    chunks, places = [], []
    current = queries
    for step in range(ex_count):
        if step == 0:
            part, both, mixer = first_scores(queries, left_inv, right_inv, store)
        else:
            route = [((i - 1) % ex_count, i) for i in range(ex_count)]
            current = lax.ppermute(current, "ex", route)
            sent = [chunk.sent for chunk in chunks if chunk.moves]
            part = order.mark(later_scores(order.after(current), both, mixer, store, sent))
            clock.now += KERNEL_US
            for chunk in chunks:
                clock.take(chunk)
                chunk.take(order)
                send(chunk, order, clock)
        choices = ORDERS[min(step, len(ORDERS) - 1)]
        width = columns // len(choices)
        for number, (choice, exchanges) in enumerate(choices):
            first = number * width
            chunk = LayerSum(part[:, first : first + width], orders[choice], index, exchanges)
            send(chunk, order, clock)
            chunks.append(chunk)
            places.append(((position - step) % ex_count * rows, jnp.int32(first)))
    while clock.arrivals:
        chunk = clock.next()
        clock.take(chunk)
        chunk.take(order)
        send(chunk, order, clock)
    done = [chunk.block for chunk in chunks]
    scores = jnp.zeros((rows * ex_count, columns), jnp.bfloat16)
    for place, block in zip(places, done):
        scores = lax.dynamic_update_slice(scores, block, place)
    ids = jnp.arange(scores.shape[0], dtype=jnp.int32)
    prompts = jnp.arange(winner.shape[0], dtype=jnp.int32)
    picks = (winner[:, None] == ids[None, :]).astype(jnp.float32)
    member = (query_prompt[None, :] == prompts[:, None]).astype(jnp.float32)
    weights = (picks - member / BEST).astype(jnp.bfloat16)
    advantage = jnp.dot(weights, scores, preferred_element_type=jnp.float32)
    return (scores, advantage.astype(jnp.bfloat16))


def solution(mesh):
    return jax.shard_map(
        shards,
        mesh=mesh,
        in_specs=(
            P("layer", ("grp", "ex"), None),
            P("layer", ("grp", "ex"), None),
            P("layer", None, None),
            P("layer", None, None),
            P("grp"),
            P("grp"),
        ),
        out_specs=(P(None, ("grp", "ex")), P(None, ("grp", "ex"))),
        check_vma=False,
    )
```

```python
import functools

import jax
import jax.numpy as jnp
from jax import lax
from jax.experimental import pallas as pl
from jax.experimental.pallas import tpu as pltpu
from jax.sharding import PartitionSpec as P

KIN = 32
KOUT = 128
BEST = 4
ROWS = 8
WIDE = KIN * ROWS
PAIR = 2 * KOUT
COLUMNS = 512
ORDERS = (((1, 1), (0, 1)), ((1, 1), (0, 1)))
NEAR_START_US = 1.1
FAR_START_US = 1.5
LATENCY_US = 0.5
NEAR_BYTES_PER_US = 50000
FAR_BYTES_PER_US = 25000
KERNEL_US = 5.3
PIECES = 4
STORE_COPIES = 8
VMEM_LIMIT = 20 * 1024 * 1024
NT = (((1,), (1,)), ((), ()))


def left_matrix(left):
    row = lax.broadcasted_iota(jnp.int32, (WIDE, KIN), 0)
    column = lax.broadcasted_iota(jnp.int32, (WIDE, KIN), 1)
    spread = jnp.where((row >> 3) == column, 1.0, 0.0).astype(jnp.bfloat16)
    tall = jnp.dot(spread, left, preferred_element_type=jnp.float32).astype(jnp.bfloat16)
    full = lax.dot_general(tall, spread, NT, preferred_element_type=jnp.float32)
    row = lax.broadcasted_iota(jnp.int32, (WIDE, WIDE), 0)
    column = lax.broadcasted_iota(jnp.int32, (WIDE, WIDE), 1)
    return jnp.where((row & (ROWS - 1)) == (column & (ROWS - 1)), full, 0.0).astype(jnp.bfloat16)


def right_matrix(right):
    zero = jnp.zeros_like(right)
    return jnp.concatenate(
        [jnp.concatenate([right, zero], 1), jnp.concatenate([zero, right], 1)], 0
    )


def side_by_side_to_stacked(block):
    tiles = block.reshape(block.shape[0] // ROWS, ROWS, PAIR)
    return jnp.concatenate([tiles[:, :, :KOUT], tiles[:, :, KOUT:]], 1)


def precondition(rows_ref, both, mixer, half_ref, pre_ref, before):
    rows = rows_ref.shape[0] // PIECES

    def piece(step, carry):
        before(step)
        at = pl.ds(pl.multiple_of(step * rows, rows), rows)
        block = jnp.concatenate(
            [rows_ref[at, p * PAIR : (p + 1) * PAIR] for p in range(KIN // 2)], 0
        )
        half = jnp.dot(block, both, preferred_element_type=jnp.float32)
        groups = pl.ds(step * (rows // ROWS), rows // ROWS)
        for p in range(KIN // 2):
            half_ref[groups, 2 * ROWS * p : 2 * ROWS * (p + 1), :] = side_by_side_to_stacked(
                half[p * rows : (p + 1) * rows]
            ).astype(jnp.bfloat16)
        return carry

    lax.fori_loop(0, PIECES, piece, 0, unroll=2)

    def groups(index, carry):
        stacked = jnp.concatenate([half_ref[2 * index], half_ref[2 * index + 1]], 1)
        mixed = side_by_side_to_stacked(
            jnp.dot(mixer, stacked, preferred_element_type=jnp.float32)
        ).astype(jnp.bfloat16)
        at = pl.ds(pl.multiple_of(index * 2 * ROWS, 2 * ROWS), 2 * ROWS)
        for i in range(KIN):
            pre_ref[at, i * KOUT : (i + 1) * KOUT] = mixed[i]
        return carry

    lax.fori_loop(0, rows_ref.shape[0] // (2 * ROWS), groups, 0, unroll=8)


def copy_of(source_ref, target_ref, sems, step):
    rows = target_ref.shape[0] // sems.shape[0]
    at = pl.ds(pl.multiple_of(step * rows, rows), rows)
    return pltpu.make_async_copy(source_ref.at[at], target_ref.at[at], sems.at[step])


def start_store(store_ref, store_vmem, sems, step):
    share = sems.shape[0] // PIECES
    for k in range(share):
        copy_of(store_ref.at[0], store_vmem, sems, step * share + k).start()


def dots(pre_ref, store_ref, store_vmem, sems, out_ref):
    columns = min(COLUMNS, store_vmem.shape[0])
    blocks = store_vmem.shape[0] // columns
    share = sems.shape[0] // blocks

    def block(step, carry):
        for k in range(share):
            copy_of(store_ref.at[0], store_vmem, sems, step * share + k).wait()
        rows = pl.ds(pl.multiple_of(step * columns, columns), columns)
        out_ref[:, rows] = lax.dot_general(
            store_vmem[rows, :], pre_ref[...], NT, preferred_element_type=jnp.float32
        ).T
        return carry

    lax.fori_loop(0, blocks, block, 0)


def first_kernel(
    rows_ref, left_ref, right_ref, store_ref, out_ref, both_ref, mixer_ref,
    left_vmem, right_vmem, rows_vmem, store_vmem, half_ref,
    left_sems, right_sems, rows_sems, store_sems,
):
    right = copy_of(right_ref.at[0], right_vmem, right_sems, 0)
    left = copy_of(left_ref.at[0], left_vmem, left_sems, 0)
    right.start()
    left.start()
    for step in range(PIECES):
        copy_of(rows_ref.at[0], rows_vmem, rows_sems, step).start()
    right.wait()
    both_ref[...] = right_matrix(right_vmem[...])
    left.wait()
    mixer_ref[...] = left_matrix(left_vmem[...])

    def before(step):
        copy_of(rows_ref.at[0], rows_vmem, rows_sems, step).wait()
        start_store(store_ref, store_vmem, store_sems, step)

    precondition(rows_vmem, both_ref[...], mixer_ref[...], half_ref, rows_vmem, before)
    dots(rows_vmem, store_ref, store_vmem, store_sems, out_ref)


def later_kernel(
    sent, rows_ref, both_ref, mixer_ref, store_ref, *refs,
):
    out_ref, pre_ref, store_vmem, half_ref, store_sems = refs[sent:]

    def before(step):
        start_store(store_ref, store_vmem, store_sems, step)

    precondition(rows_ref.at[0], both_ref[...], mixer_ref[...], half_ref, pre_ref, before)
    dots(pre_ref, store_ref, store_vmem, store_sems, out_ref)


VMEM = pl.BlockSpec(memory_space=pltpu.VMEM)
HBM = pl.BlockSpec(memory_space=pltpu.HBM)


def in_hbm(array):
    return pltpu.with_memory_space_constraint(array, pltpu.HBM)


def call(kernel, queries, store, outs, in_specs, scratch, operands):
    count, depth = queries.shape[1:]
    examples = store.shape[1]
    return pl.pallas_call(
        kernel,
        out_shape=(jax.ShapeDtypeStruct((count, examples), jnp.float32),) + outs,
        in_specs=in_specs,
        out_specs=(VMEM,) * (1 + len(outs)),
        scratch_shapes=scratch,
        compiler_params=pltpu.CompilerParams(vmem_limit_bytes=VMEM_LIMIT),
        cost_estimate=pl.CostEstimate(
            flops=2 * count * depth * (examples + 1024),
            bytes_accessed=2 * depth * (count + examples),
            transcendentals=0,
        ),
    )(*operands)


def buffers(queries, store):
    count, depth = queries.shape[1:]
    examples = store.shape[1]
    return [
        pltpu.VMEM((count, depth), jnp.bfloat16),
        pltpu.VMEM((examples, depth), jnp.bfloat16),
        pltpu.VMEM((count // ROWS, WIDE, KOUT), jnp.bfloat16),
    ]


def first_scores(queries, left_inv, right_inv, store):
    small = [pltpu.VMEM((KIN, KIN), jnp.bfloat16), pltpu.VMEM((KOUT, KOUT), jnp.bfloat16)]
    sems = [pltpu.SemaphoreType.DMA((n,)) for n in (1, 1, PIECES, STORE_COPIES)]
    outs = (
        jax.ShapeDtypeStruct((PAIR, PAIR), jnp.bfloat16),
        jax.ShapeDtypeStruct((WIDE, WIDE), jnp.bfloat16),
    )
    operands = [in_hbm(a) for a in (queries, left_inv, right_inv, store)]
    return call(
        first_kernel, queries, store, outs, [HBM] * 4,
        small + buffers(queries, store) + sems, operands,
    )


def later_scores(queries, both, mixer, store, sent):
    sems = [pltpu.SemaphoreType.DMA((STORE_COPIES,))]
    return call(
        functools.partial(later_kernel, len(sent)), queries, store, (),
        [VMEM] * 3 + [HBM] + [VMEM] * len(sent), buffers(queries, store) + sems,
        [queries, both, mixer, in_hbm(store), *sent],
    )[0]


def swap(block, bit):
    route = [(i, i ^ bit) for i in range(lax.axis_size("layer"))]
    return lax.ppermute(block, "layer", route)


HALVE, EXCHANGE, DOUBLE = range(3)


class LayerSum:
    def __init__(self, block, bits, index, exchanges):
        self.block, self.index = block, index
        halved, exchanged = bits[:-exchanges], bits[-exchanges:]
        self.moves = [(bit, HALVE) for bit in halved]
        self.moves += [(bit, EXCHANGE) for bit in exchanged]
        self.moves += [(bit, DOUBLE) for bit in reversed(halved)]
        if not halved:
            self.block = block.astype(jnp.bfloat16)

    def send(self, order):
        bit, kind = self.moves[0]
        sent = self.block
        if kind == HALVE:
            rows = self.block.shape[0] // 2
            upper = (self.index & bit) // bit
            sent = lax.dynamic_slice_in_dim(self.block, (1 - upper) * rows, rows, 0)
            sent = sent.astype(jnp.bfloat16)
            self.block = lax.dynamic_slice_in_dim(self.block, upper * rows, rows, 0)
        self.sent = order.mark(sent)
        self.received = swap(self.sent, bit)

    def bytes_of_move(self):
        size = self.block.size
        return size if self.moves[0][1] == HALVE else 2 * size

    def take(self, order):
        bit, kind = self.moves.pop(0)
        received = order.mark(self.received)
        mine = self.block
        if kind == DOUBLE:
            low = (self.index & bit) == 0
            self.block = jnp.concatenate(
                [jnp.where(low, mine, received), jnp.where(low, received, mine)], 0
            )
            return
        self.block = mine.astype(jnp.float32) + received.astype(jnp.float32)
        if not (self.moves and self.moves[0][1] == HALVE):
            self.block = self.block.astype(jnp.bfloat16)


class Order:
    def __init__(self):
        self.last = jnp.zeros((), jnp.float32)

    def after(self, value):
        value, _ = lax.optimization_barrier((value, self.last))
        return value

    def mark(self, value):
        value, self.last = lax.optimization_barrier((value, self.last))
        return value


class Clock:
    def __init__(self):
        self.now = 0.0
        self.links = {}
        self.arrivals = {}

    def send(self, chunk):
        bit, _ = chunk.moves[0]
        far = bit > 2
        self.now += FAR_START_US if far else NEAR_START_US
        begin = max(self.now, self.links.get(bit, 0.0))
        end = begin + chunk.bytes_of_move() / (FAR_BYTES_PER_US if far else NEAR_BYTES_PER_US)
        self.links[bit] = end
        self.arrivals[chunk] = end + (2 * LATENCY_US if far else LATENCY_US)

    def next(self):
        there = [chunk for chunk, at in self.arrivals.items() if at <= self.now]
        return there[-1] if there else min(self.arrivals, key=self.arrivals.get)

    def take(self, chunk):
        self.now = max(self.now, self.arrivals.pop(chunk))


def send(chunk, order, clock):
    if chunk.moves:
        clock.send(chunk)
        chunk.send(order)


def shards(store, queries, left_inv, right_inv, query_prompt, winner):
    rows = queries.shape[1]
    columns = store.shape[1]
    ex_count = lax.axis_size("ex")
    position = lax.axis_index("ex")
    count = lax.axis_size("layer")
    index = lax.axis_index("layer")
    bits = [1 << k for k in range(count.bit_length() - 1)]
    orders = [bits, bits[1:2] + bits[:1] + bits[2:]]
    order, clock = Order(), Clock()
    chunks, places = [], []
    current = queries
    for step in range(ex_count):
        if step == 0:
            part, both, mixer = first_scores(queries, left_inv, right_inv, store)
        else:
            route = [((i - 1) % ex_count, i) for i in range(ex_count)]
            current = lax.ppermute(current, "ex", route)
            sent = [chunk.sent for chunk in chunks if chunk.moves]
            part = order.mark(later_scores(order.after(current), both, mixer, store, sent))
            clock.now += KERNEL_US
            for chunk in chunks:
                clock.take(chunk)
                chunk.take(order)
                send(chunk, order, clock)
        choices = ORDERS[min(step, len(ORDERS) - 1)]
        width = columns // len(choices)
        for number, (choice, exchanges) in enumerate(choices):
            first = number * width
            chunk = LayerSum(part[:, first : first + width], orders[choice], index, exchanges)
            send(chunk, order, clock)
            chunks.append(chunk)
            places.append(((position - step) % ex_count * rows, jnp.int32(first)))
    while clock.arrivals:
        chunk = clock.next()
        clock.take(chunk)
        chunk.take(order)
        send(chunk, order, clock)
    done = [chunk.block for chunk in chunks]
    scores = jnp.zeros((rows * ex_count, columns), jnp.bfloat16)
    for place, block in zip(places, done):
        scores = lax.dynamic_update_slice(scores, block, place)
    ids = jnp.arange(scores.shape[0], dtype=jnp.int32)
    prompts = jnp.arange(winner.shape[0], dtype=jnp.int32)
    picks = (winner[:, None] == ids[None, :]).astype(jnp.float32)
    member = (query_prompt[None, :] == prompts[:, None]).astype(jnp.float32)
    weights = (picks - member / BEST).astype(jnp.bfloat16)
    advantage = jnp.dot(weights, scores, preferred_element_type=jnp.float32)
    return (scores, advantage.astype(jnp.bfloat16))


def solution(mesh):
    return jax.shard_map(
        shards,
        mesh=mesh,
        in_specs=(
            P("layer", ("grp", "ex"), None),
            P("layer", ("grp", "ex"), None),
            P("layer", None, None),
            P("layer", None, None),
            P("grp"),
            P("grp"),
        ),
        out_specs=(P(None, ("grp", "ex")), P(None, ("grp", "ex"))),
        check_vma=False,
    )
```

```python
import functools

import jax
import jax.numpy as jnp
from jax import lax
from jax.experimental import pallas as pl
from jax.experimental.pallas import tpu as pltpu
from jax.sharding import PartitionSpec as P

KIN = 32
KOUT = 128
BEST = 4
ROWS = 8
WIDE = KIN * ROWS
PAIR = 2 * KOUT
DEPTH_BLOCK = 2048
COLUMNS = 512
ORDERS = (((1, 1), (0, 1)), ((1, 1), (0, 1)))
NEAR_START_US = 1.1
FAR_START_US = 1.5
LATENCY_US = 0.5
NEAR_BYTES_PER_US = 50000
FAR_BYTES_PER_US = 25000
KERNEL_US = 5.3
PIECES = 4
STORE_COPIES = 8
VMEM_LIMIT = 20 * 1024 * 1024
NT = (((1,), (1,)), ((), ()))


def left_matrix(left):
    row = lax.broadcasted_iota(jnp.int32, (WIDE, KIN), 0)
    column = lax.broadcasted_iota(jnp.int32, (WIDE, KIN), 1)
    spread = jnp.where((row >> 3) == column, 1.0, 0.0).astype(jnp.bfloat16)
    tall = jnp.dot(spread, left, preferred_element_type=jnp.float32).astype(jnp.bfloat16)
    full = lax.dot_general(tall, spread, NT, preferred_element_type=jnp.float32)
    row = lax.broadcasted_iota(jnp.int32, (WIDE, WIDE), 0)
    column = lax.broadcasted_iota(jnp.int32, (WIDE, WIDE), 1)
    return jnp.where((row & (ROWS - 1)) == (column & (ROWS - 1)), full, 0.0).astype(jnp.bfloat16)


def right_matrix(right):
    zero = jnp.zeros_like(right)
    return jnp.concatenate(
        [jnp.concatenate([right, zero], 1), jnp.concatenate([zero, right], 1)], 0
    )


def side_by_side_to_stacked(block):
    tiles = block.reshape(block.shape[0] // ROWS, ROWS, PAIR)
    return jnp.concatenate([tiles[:, :, :KOUT], tiles[:, :, KOUT:]], 1)


def precondition(rows_ref, both, mixer, half_ref, pre_ref, before):
    rows = rows_ref.shape[0] // PIECES

    def piece(step, carry):
        before(step)
        at = pl.ds(pl.multiple_of(step * rows, rows), rows)
        block = jnp.concatenate(
            [rows_ref[at, p * PAIR : (p + 1) * PAIR] for p in range(KIN // 2)], 0
        )
        half = jnp.dot(block, both, preferred_element_type=jnp.float32)
        groups = pl.ds(step * (rows // ROWS), rows // ROWS)
        for p in range(KIN // 2):
            half_ref[groups, 2 * ROWS * p : 2 * ROWS * (p + 1), :] = side_by_side_to_stacked(
                half[p * rows : (p + 1) * rows]
            ).astype(jnp.bfloat16)
        return carry

    lax.fori_loop(0, PIECES, piece, 0)

    def groups(index, carry):
        stacked = jnp.concatenate([half_ref[2 * index], half_ref[2 * index + 1]], 1)
        mixed = side_by_side_to_stacked(
            jnp.dot(mixer, stacked, preferred_element_type=jnp.float32)
        ).astype(jnp.bfloat16)
        at = pl.ds(pl.multiple_of(index * 2 * ROWS, 2 * ROWS), 2 * ROWS)
        for i in range(KIN):
            pre_ref[at, i * KOUT : (i + 1) * KOUT] = mixed[i]
        return carry

    lax.fori_loop(0, rows_ref.shape[0] // (2 * ROWS), groups, 0, unroll=8)


def copy_of(source_ref, target_ref, sems, step):
    rows = target_ref.shape[0] // sems.shape[0]
    at = pl.ds(pl.multiple_of(step * rows, rows), rows)
    return pltpu.make_async_copy(source_ref.at[at], target_ref.at[at], sems.at[step])


def start_store(store_ref, store_vmem, sems, step):
    share = sems.shape[0] // PIECES
    for k in range(share):
        copy_of(store_ref.at[0], store_vmem, sems, step * share + k).start()


def dots(pre_ref, store_ref, store_vmem, sems, total_ref, out_ref):
    columns = total_ref.shape[0]
    depth = pre_ref.shape[1]
    blocks = store_vmem.shape[0] // columns
    share = sems.shape[0] // blocks

    def block(step, carry):
        for k in range(share):
            copy_of(store_ref.at[0], store_vmem, sems, step * share + k).wait()
        rows = pl.ds(pl.multiple_of(step * columns, columns), columns)
        for at in range(0, depth, DEPTH_BLOCK):
            term = lax.dot_general(
                store_vmem[rows, at : at + DEPTH_BLOCK],
                pre_ref[:, at : at + DEPTH_BLOCK],
                NT,
                preferred_element_type=jnp.float32,
            )
            if at == 0:
                total_ref[...] = term
            elif at + DEPTH_BLOCK < depth:
                total_ref[...] += term
            else:
                out_ref[:, rows] = (total_ref[...] + term).T
        return carry

    lax.fori_loop(0, blocks, block, 0)


def first_kernel(
    rows_ref, left_ref, right_ref, store_ref, out_ref, both_ref, mixer_ref,
    left_vmem, right_vmem, rows_vmem, store_vmem, half_ref, total_ref,
    left_sems, right_sems, rows_sems, store_sems,
):
    right = copy_of(right_ref.at[0], right_vmem, right_sems, 0)
    left = copy_of(left_ref.at[0], left_vmem, left_sems, 0)
    right.start()
    left.start()
    for step in range(PIECES):
        copy_of(rows_ref.at[0], rows_vmem, rows_sems, step).start()
    right.wait()
    both_ref[...] = right_matrix(right_vmem[...])
    left.wait()
    mixer_ref[...] = left_matrix(left_vmem[...])

    def before(step):
        copy_of(rows_ref.at[0], rows_vmem, rows_sems, step).wait()
        start_store(store_ref, store_vmem, store_sems, step)

    precondition(rows_vmem, both_ref[...], mixer_ref[...], half_ref, rows_vmem, before)
    dots(rows_vmem, store_ref, store_vmem, store_sems, total_ref, out_ref)


def later_kernel(
    sent, rows_ref, both_ref, mixer_ref, store_ref, *refs,
):
    out_ref, pre_ref, store_vmem, half_ref, total_ref, store_sems = refs[sent:]

    def before(step):
        start_store(store_ref, store_vmem, store_sems, step)

    precondition(rows_ref.at[0], both_ref[...], mixer_ref[...], half_ref, pre_ref, before)
    dots(pre_ref, store_ref, store_vmem, store_sems, total_ref, out_ref)


VMEM = pl.BlockSpec(memory_space=pltpu.VMEM)
HBM = pl.BlockSpec(memory_space=pltpu.HBM)


def in_hbm(array):
    return pltpu.with_memory_space_constraint(array, pltpu.HBM)


def call(kernel, queries, store, outs, in_specs, scratch, operands):
    count, depth = queries.shape[1:]
    examples = store.shape[1]
    return pl.pallas_call(
        kernel,
        out_shape=(jax.ShapeDtypeStruct((count, examples), jnp.float32),) + outs,
        in_specs=in_specs,
        out_specs=(VMEM,) * (1 + len(outs)),
        scratch_shapes=scratch,
        compiler_params=pltpu.CompilerParams(vmem_limit_bytes=VMEM_LIMIT),
        cost_estimate=pl.CostEstimate(
            flops=2 * count * depth * (examples + 1024),
            bytes_accessed=2 * depth * (count + examples),
            transcendentals=0,
        ),
    )(*operands)


def buffers(queries, store):
    count, depth = queries.shape[1:]
    examples = store.shape[1]
    return [
        pltpu.VMEM((count, depth), jnp.bfloat16),
        pltpu.VMEM((examples, depth), jnp.bfloat16),
        pltpu.VMEM((count // ROWS, WIDE, KOUT), jnp.bfloat16),
        pltpu.VMEM((min(COLUMNS, examples), count), jnp.float32),
    ]


def first_scores(queries, left_inv, right_inv, store):
    small = [pltpu.VMEM((KIN, KIN), jnp.bfloat16), pltpu.VMEM((KOUT, KOUT), jnp.bfloat16)]
    sems = [pltpu.SemaphoreType.DMA((n,)) for n in (1, 1, PIECES, STORE_COPIES)]
    outs = (
        jax.ShapeDtypeStruct((PAIR, PAIR), jnp.bfloat16),
        jax.ShapeDtypeStruct((WIDE, WIDE), jnp.bfloat16),
    )
    operands = [in_hbm(a) for a in (queries, left_inv, right_inv, store)]
    return call(
        first_kernel, queries, store, outs, [HBM] * 4,
        small + buffers(queries, store) + sems, operands,
    )


def later_scores(queries, both, mixer, store, sent):
    sems = [pltpu.SemaphoreType.DMA((STORE_COPIES,))]
    return call(
        functools.partial(later_kernel, len(sent)), queries, store, (),
        [VMEM] * 3 + [HBM] + [VMEM] * len(sent), buffers(queries, store) + sems,
        [queries, both, mixer, in_hbm(store), *sent],
    )[0]


def swap(block, bit):
    route = [(i, i ^ bit) for i in range(lax.axis_size("layer"))]
    return lax.ppermute(block, "layer", route)


HALVE, EXCHANGE, DOUBLE = range(3)


class LayerSum:
    def __init__(self, block, bits, index, exchanges):
        self.block, self.index = block, index
        halved, exchanged = bits[:-exchanges], bits[-exchanges:]
        self.moves = [(bit, HALVE) for bit in halved]
        self.moves += [(bit, EXCHANGE) for bit in exchanged]
        self.moves += [(bit, DOUBLE) for bit in reversed(halved)]
        if not halved:
            self.block = block.astype(jnp.bfloat16)

    def piece(self):
        bit, kind = self.moves[0]
        sent = self.block
        if kind == HALVE:
            rows = self.block.shape[0] // 2
            upper = (self.index & bit) // bit
            sent = lax.dynamic_slice_in_dim(self.block, (1 - upper) * rows, rows, 0)
            sent = sent.astype(jnp.bfloat16)
            self.block = lax.dynamic_slice_in_dim(self.block, upper * rows, rows, 0)
        return sent

    def bytes_of_move(self):
        size = self.block.size
        return size if self.moves[0][1] == HALVE else 2 * size

    def take(self, order):
        bit, kind = self.moves.pop(0)
        received = order.mark(self.received)
        mine = self.block
        if kind == DOUBLE:
            low = (self.index & bit) == 0
            self.block = jnp.concatenate(
                [jnp.where(low, mine, received), jnp.where(low, received, mine)], 0
            )
            return
        self.block = mine.astype(jnp.float32) + received.astype(jnp.float32)
        if not (self.moves and self.moves[0][1] == HALVE):
            self.block = self.block.astype(jnp.bfloat16)


class Order:
    def __init__(self):
        self.last = jnp.zeros((), jnp.float32)

    def after(self, value):
        value, _ = lax.optimization_barrier((value, self.last))
        return value

    def mark(self, value):
        value, self.last = lax.optimization_barrier((value, self.last))
        return value


class Clock:
    def __init__(self):
        self.now = 0.0
        self.links = {}
        self.arrivals = {}

    def send(self, chunks):
        bit, _ = chunks[0].moves[0]
        far = bit > 2
        self.now += FAR_START_US if far else NEAR_START_US
        begin = max(self.now, self.links.get(bit, 0.0))
        end = begin + sum(c.bytes_of_move() for c in chunks) / (FAR_BYTES_PER_US if far else NEAR_BYTES_PER_US)
        self.links[bit] = end
        for chunk in chunks:
            self.arrivals[chunk] = end + (2 * LATENCY_US if far else LATENCY_US)

    def next(self):
        there = [chunk for chunk, at in self.arrivals.items() if at <= self.now]
        return there[-1] if there else min(self.arrivals, key=self.arrivals.get)

    def take(self, chunk):
        self.now = max(self.now, self.arrivals.pop(chunk))


def send(chunks, order, clock):
    if not chunks[0].moves:
        return
    clock.send(chunks)
    pieces = [chunk.piece() for chunk in chunks]
    sent = order.mark(jnp.concatenate(pieces, 0) if len(pieces) > 1 else pieces[0])
    received, first = swap(sent, chunks[0].moves[0][0]), 0
    for chunk, piece in zip(chunks, pieces):
        chunk.sent = sent
        chunk.received = received[first : first + piece.shape[0]]
        first += piece.shape[0]


def shards(store, queries, left_inv, right_inv, query_prompt, winner):
    rows = queries.shape[1]
    columns = store.shape[1]
    ex_count = lax.axis_size("ex")
    position = lax.axis_index("ex")
    count = lax.axis_size("layer")
    index = lax.axis_index("layer")
    bits = [1 << k for k in range(count.bit_length() - 1)]
    orders = [bits, bits[1:2] + bits[:1] + bits[2:]]
    order, clock = Order(), Clock()
    chunks, places = [], []
    current = queries
    for step in range(ex_count):
        if step == 0:
            part, both, mixer = first_scores(queries, left_inv, right_inv, store)
        else:
            route = [((i - 1) % ex_count, i) for i in range(ex_count)]
            current = lax.ppermute(current, "ex", route)
            sent = [chunk.sent for chunk in chunks if chunk.moves]
            part = order.mark(later_scores(order.after(current), both, mixer, store, sent))
            clock.now += KERNEL_US
            for chunk in chunks:
                clock.take(chunk)
                chunk.take(order)
        waiting = list(chunks)
        choices = ORDERS[min(step, len(ORDERS) - 1)]
        width = columns // len(choices)
        for number, (choice, exchanges) in enumerate(choices):
            first = number * width
            chunk = LayerSum(part[:, first : first + width], orders[choice], index, exchanges)
            partners = [
                early
                for early in waiting
                if early.moves and early.moves[0] == chunk.moves[0]
                and early.block.shape[1] == chunk.block.shape[1]
            ][:1]
            send([chunk] + partners, order, clock)
            waiting = [early for early in waiting if early not in partners]
            chunks.append(chunk)
            places.append(((position - step) % ex_count * rows, jnp.int32(first)))
        for early in waiting:
            send([early], order, clock)
    while clock.arrivals:
        chunk = clock.next()
        clock.take(chunk)
        chunk.take(order)
        send([chunk], order, clock)
    done = [chunk.block for chunk in chunks]
    scores = jnp.zeros((rows * ex_count, columns), jnp.bfloat16)
    for place, block in zip(places, done):
        scores = lax.dynamic_update_slice(scores, block, place)
    ids = jnp.arange(scores.shape[0], dtype=jnp.int32)
    prompts = jnp.arange(winner.shape[0], dtype=jnp.int32)
    picks = (winner[:, None] == ids[None, :]).astype(jnp.float32)
    member = (query_prompt[None, :] == prompts[:, None]).astype(jnp.float32)
    weights = (picks - member / BEST).astype(jnp.bfloat16)
    advantage = jnp.dot(weights, scores, preferred_element_type=jnp.float32)
    return (scores, advantage.astype(jnp.bfloat16))


def solution(mesh):
    return jax.shard_map(
        shards,
        mesh=mesh,
        in_specs=(
            P("layer", ("grp", "ex"), None),
            P("layer", ("grp", "ex"), None),
            P("layer", None, None),
            P("layer", None, None),
            P("grp"),
            P("grp"),
        ),
        out_specs=(P(None, ("grp", "ex")), P(None, ("grp", "ex"))),
        check_vma=False,
    )
```

```python
import functools

import jax
import jax.numpy as jnp
from jax import lax
from jax.experimental import pallas as pl
from jax.experimental.pallas import tpu as pltpu
from jax.sharding import PartitionSpec as P

KIN = 32
KOUT = 128
BEST = 4
ROWS = 8
WIDE = KIN * ROWS
PAIR = 2 * KOUT
DEPTH_BLOCK = 2048
COLUMNS = 512
ORDERS = (((1, 1), (0, 1)), ((1, 1), (0, 1)))
NEAR_START_US = 1.1
FAR_START_US = 1.5
LATENCY_US = 0.5
NEAR_BYTES_PER_US = 50000
FAR_BYTES_PER_US = 25000
KERNEL_US = 5.3
PIECES = 4
STORE_COPIES = 8
VMEM_LIMIT = 20 * 1024 * 1024
NT = (((1,), (1,)), ((), ()))


def left_matrix(left):
    row = lax.broadcasted_iota(jnp.int32, (WIDE, KIN), 0)
    column = lax.broadcasted_iota(jnp.int32, (WIDE, KIN), 1)
    spread = jnp.where((row >> 3) == column, 1.0, 0.0).astype(jnp.bfloat16)
    tall = jnp.dot(spread, left, preferred_element_type=jnp.float32).astype(jnp.bfloat16)
    full = lax.dot_general(tall, spread, NT, preferred_element_type=jnp.float32)
    row = lax.broadcasted_iota(jnp.int32, (WIDE, WIDE), 0)
    column = lax.broadcasted_iota(jnp.int32, (WIDE, WIDE), 1)
    return jnp.where((row & (ROWS - 1)) == (column & (ROWS - 1)), full, 0.0).astype(jnp.bfloat16)


def right_matrix(right):
    zero = jnp.zeros_like(right)
    return jnp.concatenate(
        [jnp.concatenate([right, zero], 1), jnp.concatenate([zero, right], 1)], 0
    )


def side_by_side_to_stacked(block):
    tiles = block.reshape(block.shape[0] // ROWS, ROWS, PAIR)
    return jnp.concatenate([tiles[:, :, :KOUT], tiles[:, :, KOUT:]], 1)


def precondition(rows_ref, both, mixer, half_ref, pre_ref, before):
    rows = rows_ref.shape[0] // PIECES

    def piece(step, carry):
        before(step)
        at = pl.ds(pl.multiple_of(step * rows, rows), rows)
        block = jnp.concatenate(
            [rows_ref[at, p * PAIR : (p + 1) * PAIR] for p in range(KIN // 2)], 0
        )
        half = jnp.dot(block, both, preferred_element_type=jnp.float32)
        groups = pl.ds(step * (rows // ROWS), rows // ROWS)
        for p in range(KIN // 2):
            half_ref[groups, 2 * ROWS * p : 2 * ROWS * (p + 1), :] = side_by_side_to_stacked(
                half[p * rows : (p + 1) * rows]
            ).astype(jnp.bfloat16)
        return carry

    lax.fori_loop(0, PIECES, piece, 0)

    def groups(index, carry):
        stacked = jnp.concatenate([half_ref[2 * index], half_ref[2 * index + 1]], 1)
        mixed = side_by_side_to_stacked(
            jnp.dot(mixer, stacked, preferred_element_type=jnp.float32)
        ).astype(jnp.bfloat16)
        at = pl.ds(pl.multiple_of(index * 2 * ROWS, 2 * ROWS), 2 * ROWS)
        for i in range(KIN):
            pre_ref[at, i * KOUT : (i + 1) * KOUT] = mixed[i]
        return carry

    lax.fori_loop(0, rows_ref.shape[0] // (2 * ROWS), groups, 0, unroll=8)


def copy_of(source_ref, target_ref, sems, step):
    rows = target_ref.shape[0] // sems.shape[0]
    at = pl.ds(pl.multiple_of(step * rows, rows), rows)
    return pltpu.make_async_copy(source_ref.at[at], target_ref.at[at], sems.at[step])


def start_store(store_ref, store_vmem, sems, step):
    share = sems.shape[0] // PIECES
    for k in range(share):
        copy_of(store_ref.at[0], store_vmem, sems, step * share + k).start()


def dots(pre_ref, store_ref, store_vmem, sems, total_ref, out_ref):
    columns = total_ref.shape[0]
    depth = pre_ref.shape[1]
    blocks = store_vmem.shape[0] // columns
    share = sems.shape[0] // blocks

    def block(step, carry):
        for k in range(share):
            copy_of(store_ref.at[0], store_vmem, sems, step * share + k).wait()
        rows = pl.ds(pl.multiple_of(step * columns, columns), columns)
        for at in range(0, depth, DEPTH_BLOCK):
            term = lax.dot_general(
                store_vmem[rows, at : at + DEPTH_BLOCK],
                pre_ref[:, at : at + DEPTH_BLOCK],
                NT,
                preferred_element_type=jnp.float32,
            )
            if at == 0:
                total_ref[...] = term
            elif at + DEPTH_BLOCK < depth:
                total_ref[...] += term
            else:
                out_ref[step] = (total_ref[...] + term).T
        return carry

    lax.fori_loop(0, blocks, block, 0)


def first_kernel(
    rows_ref, left_ref, right_ref, store_ref, out_ref, both_ref, mixer_ref,
    left_vmem, right_vmem, rows_vmem, store_vmem, half_ref, total_ref,
    left_sems, right_sems, rows_sems, store_sems,
):
    right = copy_of(right_ref.at[0], right_vmem, right_sems, 0)
    left = copy_of(left_ref.at[0], left_vmem, left_sems, 0)
    right.start()
    left.start()
    for step in range(PIECES):
        copy_of(rows_ref.at[0], rows_vmem, rows_sems, step).start()
    right.wait()
    both_ref[...] = right_matrix(right_vmem[...])
    left.wait()
    mixer_ref[...] = left_matrix(left_vmem[...])

    def before(step):
        copy_of(rows_ref.at[0], rows_vmem, rows_sems, step).wait()
        start_store(store_ref, store_vmem, store_sems, step)

    precondition(rows_vmem, both_ref[...], mixer_ref[...], half_ref, rows_vmem, before)
    dots(rows_vmem, store_ref, store_vmem, store_sems, total_ref, out_ref)


def later_kernel(
    sent, rows_ref, both_ref, mixer_ref, store_ref, *refs,
):
    out_ref, pre_ref, store_vmem, half_ref, total_ref, store_sems = refs[sent:]

    def before(step):
        start_store(store_ref, store_vmem, store_sems, step)

    precondition(rows_ref.at[0], both_ref[...], mixer_ref[...], half_ref, pre_ref, before)
    dots(pre_ref, store_ref, store_vmem, store_sems, total_ref, out_ref)


VMEM = pl.BlockSpec(memory_space=pltpu.VMEM)
HBM = pl.BlockSpec(memory_space=pltpu.HBM)


def in_hbm(array):
    return pltpu.with_memory_space_constraint(array, pltpu.HBM)


def call(kernel, queries, store, outs, in_specs, scratch, operands):
    count, depth = queries.shape[1:]
    examples = store.shape[1]
    columns = min(COLUMNS, examples)
    scores = jax.ShapeDtypeStruct((examples // columns, count, columns), jnp.float32)
    return pl.pallas_call(
        kernel,
        out_shape=(scores,) + outs,
        in_specs=in_specs,
        out_specs=(VMEM,) * (1 + len(outs)),
        scratch_shapes=scratch,
        compiler_params=pltpu.CompilerParams(vmem_limit_bytes=VMEM_LIMIT),
        cost_estimate=pl.CostEstimate(
            flops=2 * count * depth * (examples + 1024),
            bytes_accessed=2 * depth * (count + examples),
            transcendentals=0,
        ),
    )(*operands)


def buffers(queries, store):
    count, depth = queries.shape[1:]
    examples = store.shape[1]
    return [
        pltpu.VMEM((count, depth), jnp.bfloat16),
        pltpu.VMEM((examples, depth), jnp.bfloat16),
        pltpu.VMEM((count // ROWS, WIDE, KOUT), jnp.bfloat16),
        pltpu.VMEM((min(COLUMNS, examples), count), jnp.float32),
    ]


def first_scores(queries, left_inv, right_inv, store):
    small = [pltpu.VMEM((KIN, KIN), jnp.bfloat16), pltpu.VMEM((KOUT, KOUT), jnp.bfloat16)]
    sems = [pltpu.SemaphoreType.DMA((n,)) for n in (1, 1, PIECES, STORE_COPIES)]
    outs = (
        jax.ShapeDtypeStruct((PAIR, PAIR), jnp.bfloat16),
        jax.ShapeDtypeStruct((WIDE, WIDE), jnp.bfloat16),
    )
    operands = [in_hbm(a) for a in (queries, left_inv, right_inv, store)]
    return call(
        first_kernel, queries, store, outs, [HBM] * 4,
        small + buffers(queries, store) + sems, operands,
    )


def later_scores(queries, both, mixer, store, sent):
    sems = [pltpu.SemaphoreType.DMA((STORE_COPIES,))]
    return call(
        functools.partial(later_kernel, len(sent)), queries, store, (),
        [VMEM] * 3 + [HBM] + [VMEM] * len(sent), buffers(queries, store) + sems,
        [queries, both, mixer, in_hbm(store), *sent],
    )[0]


def swap(block, bit):
    route = [(i, i ^ bit) for i in range(lax.axis_size("layer"))]
    return lax.ppermute(block, "layer", route)


HALVE, EXCHANGE, DOUBLE = range(3)


class LayerSum:
    def __init__(self, block, bits, index, exchanges):
        self.block, self.index = block, index
        halved, exchanged = bits[:-exchanges], bits[-exchanges:]
        self.moves = [(bit, HALVE) for bit in halved]
        self.moves += [(bit, EXCHANGE) for bit in exchanged]
        self.moves += [(bit, DOUBLE) for bit in reversed(halved)]
        if not halved:
            self.block = block.astype(jnp.bfloat16)

    def send(self, order):
        bit, kind = self.moves[0]
        sent = self.block
        if kind == HALVE:
            rows = self.block.shape[0] // 2
            upper = (self.index & bit) // bit
            sent = lax.dynamic_slice_in_dim(self.block, (1 - upper) * rows, rows, 0)
            sent = sent.astype(jnp.bfloat16)
            self.block = lax.dynamic_slice_in_dim(self.block, upper * rows, rows, 0)
        self.sent = order.mark(sent)
        self.received = swap(self.sent, bit)

    def bytes_of_move(self):
        size = self.block.size
        return size if self.moves[0][1] == HALVE else 2 * size

    def take(self, order):
        bit, kind = self.moves.pop(0)
        received = order.mark(self.received)
        mine = self.block
        if kind == DOUBLE:
            low = (self.index & bit) == 0
            self.block = jnp.concatenate(
                [jnp.where(low, mine, received), jnp.where(low, received, mine)], 0
            )
            return
        self.block = mine.astype(jnp.float32) + received.astype(jnp.float32)
        if not (self.moves and self.moves[0][1] == HALVE):
            self.block = self.block.astype(jnp.bfloat16)


class Order:
    def __init__(self):
        self.last = jnp.zeros((), jnp.float32)

    def after(self, value):
        value, _ = lax.optimization_barrier((value, self.last))
        return value

    def mark(self, value):
        value, self.last = lax.optimization_barrier((value, self.last))
        return value


class Clock:
    def __init__(self):
        self.now = 0.0
        self.links = {}
        self.arrivals = {}

    def send(self, chunk):
        bit, _ = chunk.moves[0]
        far = bit > 2
        self.now += FAR_START_US if far else NEAR_START_US
        begin = max(self.now, self.links.get(bit, 0.0))
        end = begin + chunk.bytes_of_move() / (FAR_BYTES_PER_US if far else NEAR_BYTES_PER_US)
        self.links[bit] = end
        self.arrivals[chunk] = end + (2 * LATENCY_US if far else LATENCY_US)

    def next(self):
        there = [chunk for chunk, at in self.arrivals.items() if at <= self.now]
        return there[-1] if there else min(self.arrivals, key=self.arrivals.get)

    def take(self, chunk):
        self.now = max(self.now, self.arrivals.pop(chunk))


def send(chunk, order, clock):
    if chunk.moves:
        clock.send(chunk)
        chunk.send(order)


def shards(store, queries, left_inv, right_inv, query_prompt, winner):
    rows = queries.shape[1]
    columns = store.shape[1]
    ex_count = lax.axis_size("ex")
    position = lax.axis_index("ex")
    count = lax.axis_size("layer")
    index = lax.axis_index("layer")
    bits = [1 << k for k in range(count.bit_length() - 1)]
    orders = [bits, bits[1:2] + bits[:1] + bits[2:]]
    order, clock = Order(), Clock()
    chunks, places = [], []
    current = queries
    for step in range(ex_count):
        if step == 0:
            part, both, mixer = first_scores(queries, left_inv, right_inv, store)
        else:
            route = [((i - 1) % ex_count, i) for i in range(ex_count)]
            current = lax.ppermute(current, "ex", route)
            sent = [chunk.sent for chunk in chunks if chunk.moves]
            part = order.mark(later_scores(order.after(current), both, mixer, store, sent))
            clock.now += KERNEL_US
            for chunk in chunks:
                clock.take(chunk)
                chunk.take(order)
                send(chunk, order, clock)
        choices = ORDERS[min(step, len(ORDERS) - 1)]
        width = part.shape[2]
        for number, (choice, exchanges) in enumerate(choices):
            first = number * width
            chunk = LayerSum(part[number], orders[choice], index, exchanges)
            send(chunk, order, clock)
            chunks.append(chunk)
            places.append(((position - step) % ex_count * rows, jnp.int32(first)))
    while clock.arrivals:
        chunk = clock.next()
        clock.take(chunk)
        chunk.take(order)
        send(chunk, order, clock)
    done = [chunk.block for chunk in chunks]
    scores = jnp.zeros((rows * ex_count, columns), jnp.bfloat16)
    for place, block in zip(places, done):
        scores = lax.dynamic_update_slice(scores, block, place)
    ids = jnp.arange(scores.shape[0], dtype=jnp.int32)
    prompts = jnp.arange(winner.shape[0], dtype=jnp.int32)
    picks = (winner[:, None] == ids[None, :]).astype(jnp.float32)
    member = (query_prompt[None, :] == prompts[:, None]).astype(jnp.float32)
    weights = (picks - member / BEST).astype(jnp.bfloat16)
    advantage = jnp.dot(weights, scores, preferred_element_type=jnp.float32)
    return (scores, advantage.astype(jnp.bfloat16))


def solution(mesh):
    return jax.shard_map(
        shards,
        mesh=mesh,
        in_specs=(
            P("layer", ("grp", "ex"), None),
            P("layer", ("grp", "ex"), None),
            P("layer", None, None),
            P("layer", None, None),
            P("grp"),
            P("grp"),
        ),
        out_specs=(P(None, ("grp", "ex")), P(None, ("grp", "ex"))),
        check_vma=False,
    )
```

```python
import functools

import jax
import jax.numpy as jnp
from jax import lax
from jax.experimental import pallas as pl
from jax.experimental.pallas import tpu as pltpu
from jax.sharding import PartitionSpec as P

KIN = 32
KOUT = 128
BEST = 4
ROWS = 8
WIDE = KIN * ROWS
PAIR = 2 * KOUT
DEPTH_BLOCK = 2048
COLUMNS = 512
ORDERS = (((1, 1), (0, 1)), ((1, 1), (0, 1)))
NEAR_START_US = 1.1
FAR_START_US = 1.5
LATENCY_US = 0.5
NEAR_BYTES_PER_US = 50000
FAR_BYTES_PER_US = 25000
KERNEL_US = 5.3
PIECES = 4
STORE_COPIES = 8
VMEM_LIMIT = 20 * 1024 * 1024
NT = (((1,), (1,)), ((), ()))


def left_matrix(left):
    row = lax.broadcasted_iota(jnp.int32, (WIDE, KIN), 0)
    column = lax.broadcasted_iota(jnp.int32, (WIDE, KIN), 1)
    spread = jnp.where((row >> 3) == column, 1.0, 0.0).astype(jnp.bfloat16)
    tall = jnp.dot(spread, left, preferred_element_type=jnp.float32).astype(jnp.bfloat16)
    full = lax.dot_general(tall, spread, NT, preferred_element_type=jnp.float32)
    row = lax.broadcasted_iota(jnp.int32, (WIDE, WIDE), 0)
    column = lax.broadcasted_iota(jnp.int32, (WIDE, WIDE), 1)
    return jnp.where((row & (ROWS - 1)) == (column & (ROWS - 1)), full, 0.0).astype(jnp.bfloat16)


def right_matrix(right):
    zero = jnp.zeros_like(right)
    return jnp.concatenate(
        [jnp.concatenate([right, zero], 1), jnp.concatenate([zero, right], 1)], 0
    )


def side_by_side_to_stacked(block):
    tiles = block.reshape(block.shape[0] // ROWS, ROWS, PAIR)
    return jnp.concatenate([tiles[:, :, :KOUT], tiles[:, :, KOUT:]], 1)


def precondition(rows_ref, both, mixer, half_ref, pre_ref, before):
    rows = rows_ref.shape[0] // PIECES

    def piece(step, carry):
        before(step)
        at = pl.ds(pl.multiple_of(step * rows, rows), rows)
        block = jnp.concatenate(
            [rows_ref[at, p * PAIR : (p + 1) * PAIR] for p in range(KIN // 2)], 0
        )
        half = jnp.dot(block, both, preferred_element_type=jnp.float32)
        groups = pl.ds(step * (rows // ROWS), rows // ROWS)
        for p in range(KIN // 2):
            half_ref[groups, 2 * ROWS * p : 2 * ROWS * (p + 1), :] = side_by_side_to_stacked(
                half[p * rows : (p + 1) * rows]
            ).astype(jnp.bfloat16)
        return carry

    lax.fori_loop(0, PIECES, piece, 0)

    def groups(index, carry):
        stacked = jnp.concatenate([half_ref[2 * index], half_ref[2 * index + 1]], 1)
        mixed = side_by_side_to_stacked(
            jnp.dot(mixer, stacked, preferred_element_type=jnp.float32)
        ).astype(jnp.bfloat16)
        at = pl.ds(pl.multiple_of(index * 2 * ROWS, 2 * ROWS), 2 * ROWS)
        for i in range(KIN):
            pre_ref[at, i * KOUT : (i + 1) * KOUT] = mixed[i]
        return carry

    lax.fori_loop(0, rows_ref.shape[0] // (2 * ROWS), groups, 0, unroll=8)


def copy_of(source_ref, target_ref, sems, step):
    rows = target_ref.shape[0] // sems.shape[0]
    at = pl.ds(pl.multiple_of(step * rows, rows), rows)
    return pltpu.make_async_copy(source_ref.at[at], target_ref.at[at], sems.at[step])


def start_store(store_ref, store_vmem, sems, step):
    share = sems.shape[0] // PIECES
    for k in range(share):
        copy_of(store_ref.at[0], store_vmem, sems, step * share + k).start()


def dots(pre_ref, store_ref, store_vmem, sems, total_ref, out_ref):
    columns = total_ref.shape[0]
    depth = pre_ref.shape[1]
    blocks = store_vmem.shape[0] // columns
    share = sems.shape[0] // blocks

    def block(step, carry):
        for k in range(share):
            copy_of(store_ref.at[0], store_vmem, sems, step * share + k).wait()
        rows = pl.ds(pl.multiple_of(step * columns, columns), columns)
        for at in range(0, depth, DEPTH_BLOCK):
            term = lax.dot_general(
                store_vmem[rows, at : at + DEPTH_BLOCK],
                pre_ref[:, at : at + DEPTH_BLOCK],
                NT,
                preferred_element_type=jnp.float32,
            )
            if at == 0:
                total_ref[...] = term
            elif at + DEPTH_BLOCK < depth:
                total_ref[...] += term
            else:
                out_ref[step] = (total_ref[...] + term).T
        return carry

    lax.fori_loop(0, blocks, block, 0)


def first_kernel(
    rows_ref, left_ref, right_ref, store_ref, out_ref, both_ref, mixer_ref,
    left_vmem, right_vmem, rows_vmem, store_vmem, half_ref, total_ref,
    left_sems, right_sems, rows_sems, store_sems,
):
    right = copy_of(right_ref.at[0], right_vmem, right_sems, 0)
    left = copy_of(left_ref.at[0], left_vmem, left_sems, 0)
    right.start()
    left.start()
    for step in range(PIECES):
        copy_of(rows_ref.at[0], rows_vmem, rows_sems, step).start()
    right.wait()
    both_ref[...] = right_matrix(right_vmem[...])
    left.wait()
    mixer_ref[...] = left_matrix(left_vmem[...])

    def before(step):
        copy_of(rows_ref.at[0], rows_vmem, rows_sems, step).wait()
        start_store(store_ref, store_vmem, store_sems, step)

    precondition(rows_vmem, both_ref[...], mixer_ref[...], half_ref, rows_vmem, before)
    dots(rows_vmem, store_ref, store_vmem, store_sems, total_ref, out_ref)


def later_kernel(
    sent, rows_ref, both_ref, mixer_ref, store_ref, *refs,
):
    out_ref, pre_ref, store_vmem, half_ref, total_ref, store_sems = refs[sent:]

    def before(step):
        start_store(store_ref, store_vmem, store_sems, step)

    precondition(rows_ref.at[0], both_ref[...], mixer_ref[...], half_ref, pre_ref, before)
    dots(pre_ref, store_ref, store_vmem, store_sems, total_ref, out_ref)


VMEM = pl.BlockSpec(memory_space=pltpu.VMEM)
HBM = pl.BlockSpec(memory_space=pltpu.HBM)


def in_hbm(array):
    return pltpu.with_memory_space_constraint(array, pltpu.HBM)


def call(kernel, queries, store, outs, in_specs, scratch, operands):
    count, depth = queries.shape[1:]
    examples = store.shape[1]
    columns = min(COLUMNS, examples)
    scores = jax.ShapeDtypeStruct((examples // columns, count, columns), jnp.float32)
    return pl.pallas_call(
        kernel,
        out_shape=(scores,) + outs,
        in_specs=in_specs,
        out_specs=(VMEM,) * (1 + len(outs)),
        scratch_shapes=scratch,
        compiler_params=pltpu.CompilerParams(vmem_limit_bytes=VMEM_LIMIT),
        cost_estimate=pl.CostEstimate(
            flops=2 * count * depth * (examples + 1024),
            bytes_accessed=2 * depth * (count + examples),
            transcendentals=0,
        ),
    )(*operands)


def buffers(queries, store):
    count, depth = queries.shape[1:]
    examples = store.shape[1]
    return [
        pltpu.VMEM((count, depth), jnp.bfloat16),
        pltpu.VMEM((examples, depth), jnp.bfloat16),
        pltpu.VMEM((count // ROWS, WIDE, KOUT), jnp.bfloat16),
        pltpu.VMEM((min(COLUMNS, examples), count), jnp.float32),
    ]


def first_scores(queries, left_inv, right_inv, store):
    small = [pltpu.VMEM((KIN, KIN), jnp.bfloat16), pltpu.VMEM((KOUT, KOUT), jnp.bfloat16)]
    sems = [pltpu.SemaphoreType.DMA((n,)) for n in (1, 1, PIECES, STORE_COPIES)]
    outs = (
        jax.ShapeDtypeStruct((PAIR, PAIR), jnp.bfloat16),
        jax.ShapeDtypeStruct((WIDE, WIDE), jnp.bfloat16),
    )
    operands = [in_hbm(a) for a in (queries, left_inv, right_inv, store)]
    return call(
        first_kernel, queries, store, outs, [HBM] * 4,
        small + buffers(queries, store) + sems, operands,
    )


def later_scores(queries, both, mixer, store, sent):
    sems = [pltpu.SemaphoreType.DMA((STORE_COPIES,))]
    return call(
        functools.partial(later_kernel, len(sent)), queries, store, (),
        [VMEM] * 3 + [HBM] + [VMEM] * len(sent), buffers(queries, store) + sems,
        [queries, both, mixer, in_hbm(store), *sent],
    )[0]


def swap(block, bit):
    route = [(i, i ^ bit) for i in range(lax.axis_size("layer"))]
    return lax.ppermute(block, "layer", route)


HALVE, EXCHANGE, DOUBLE = range(3)


class LayerSum:
    def __init__(self, block, bits, index, exchanges):
        self.block, self.index, self.sent = block, index, None
        halved, exchanged = bits[:-exchanges], bits[-exchanges:]
        self.moves = [(bit, HALVE) for bit in halved]
        self.moves += [(bit, EXCHANGE) for bit in exchanged]
        self.moves += [(bit, DOUBLE) for bit in reversed(halved)]
        if not halved:
            self.block = block.astype(jnp.bfloat16)

    def send(self, order):
        bit, kind = self.moves[0]
        sent = self.block
        if kind == HALVE:
            rows = self.block.shape[0] // 2
            upper = (self.index & bit) // bit
            sent = lax.dynamic_slice_in_dim(self.block, (1 - upper) * rows, rows, 0)
            sent = sent.astype(jnp.bfloat16)
            self.block = lax.dynamic_slice_in_dim(self.block, upper * rows, rows, 0)
            if self.sent is None:
                self.block, sent = lax.optimization_barrier((self.block, sent))
        self.sent = order.mark(sent)
        self.received = swap(self.sent, bit)

    def bytes_of_move(self):
        size = self.block.size
        return size if self.moves[0][1] == HALVE else 2 * size

    def take(self, order):
        bit, kind = self.moves.pop(0)
        received = order.mark(self.received)
        mine = self.block
        if kind == DOUBLE:
            low = (self.index & bit) == 0
            self.block = jnp.concatenate(
                [jnp.where(low, mine, received), jnp.where(low, received, mine)], 0
            )
            return
        self.block = mine.astype(jnp.float32) + received.astype(jnp.float32)
        if not (self.moves and self.moves[0][1] == HALVE):
            self.block = self.block.astype(jnp.bfloat16)


class Order:
    def __init__(self):
        self.last = jnp.zeros((), jnp.float32)

    def after(self, value):
        value, _ = lax.optimization_barrier((value, self.last))
        return value

    def mark(self, value):
        value, self.last = lax.optimization_barrier((value, self.last))
        return value


class Clock:
    def __init__(self):
        self.now = 0.0
        self.links = {}
        self.arrivals = {}

    def send(self, chunk):
        bit, _ = chunk.moves[0]
        far = bit > 2
        self.now += FAR_START_US if far else NEAR_START_US
        begin = max(self.now, self.links.get(bit, 0.0))
        end = begin + chunk.bytes_of_move() / (FAR_BYTES_PER_US if far else NEAR_BYTES_PER_US)
        self.links[bit] = end
        self.arrivals[chunk] = end + (2 * LATENCY_US if far else LATENCY_US)

    def next(self):
        there = [chunk for chunk, at in self.arrivals.items() if at <= self.now]
        return there[-1] if there else min(self.arrivals, key=self.arrivals.get)

    def take(self, chunk):
        self.now = max(self.now, self.arrivals.pop(chunk))


def send(chunk, order, clock):
    if chunk.moves:
        clock.send(chunk)
        chunk.send(order)


def shards(store, queries, left_inv, right_inv, query_prompt, winner):
    rows = queries.shape[1]
    columns = store.shape[1]
    ex_count = lax.axis_size("ex")
    position = lax.axis_index("ex")
    count = lax.axis_size("layer")
    index = lax.axis_index("layer")
    bits = [1 << k for k in range(count.bit_length() - 1)]
    orders = [bits, bits[1:2] + bits[:1] + bits[2:]]
    order, clock = Order(), Clock()
    chunks, places = [], []
    current = queries
    for step in range(ex_count):
        if step == 0:
            part, both, mixer = first_scores(queries, left_inv, right_inv, store)
        else:
            route = [((i - 1) % ex_count, i) for i in range(ex_count)]
            current = lax.ppermute(current, "ex", route)
            sent = [chunk.sent for chunk in chunks if chunk.moves]
            part = order.mark(later_scores(order.after(current), both, mixer, store, sent))
            clock.now += KERNEL_US
            for chunk in chunks:
                clock.take(chunk)
                chunk.take(order)
                send(chunk, order, clock)
        choices = ORDERS[min(step, len(ORDERS) - 1)]
        width = part.shape[2]
        for number, (choice, exchanges) in enumerate(choices):
            first = number * width
            chunk = LayerSum(part[number], orders[choice], index, exchanges)
            send(chunk, order, clock)
            chunks.append(chunk)
            places.append(((position - step) % ex_count * rows, jnp.int32(first)))
    while clock.arrivals:
        chunk = clock.next()
        clock.take(chunk)
        chunk.take(order)
        send(chunk, order, clock)
    done = [chunk.block for chunk in chunks]
    scores = jnp.zeros((rows * ex_count, columns), jnp.bfloat16)
    for place, block in zip(places, done):
        scores = lax.dynamic_update_slice(scores, block, place)
    ids = jnp.arange(scores.shape[0], dtype=jnp.int32)
    prompts = jnp.arange(winner.shape[0], dtype=jnp.int32)
    picks = (winner[:, None] == ids[None, :]).astype(jnp.float32)
    member = (query_prompt[None, :] == prompts[:, None]).astype(jnp.float32)
    weights = (picks - member / BEST).astype(jnp.bfloat16)
    advantage = jnp.dot(weights, scores, preferred_element_type=jnp.float32)
    return (scores, advantage.astype(jnp.bfloat16))


def solution(mesh):
    return jax.shard_map(
        shards,
        mesh=mesh,
        in_specs=(
            P("layer", ("grp", "ex"), None),
            P("layer", ("grp", "ex"), None),
            P("layer", None, None),
            P("layer", None, None),
            P("grp"),
            P("grp"),
        ),
        out_specs=(P(None, ("grp", "ex")), P(None, ("grp", "ex"))),
        check_vma=False,
    )
```

```python
import functools

import jax
import jax.numpy as jnp
from jax import lax
from jax.experimental import pallas as pl
from jax.experimental.pallas import tpu as pltpu
from jax.sharding import PartitionSpec as P

KIN = 32
KOUT = 128
BEST = 4
ROWS = 8
WIDE = KIN * ROWS
PAIR = 2 * KOUT
DEPTH_BLOCK = 2048
COLUMNS = 512
ORDERS = (((1, 1), (0, 1)), ((1, 1), (0, 1)))
NEAR_START_US = 1.1
FAR_START_US = 1.5
LATENCY_US = 0.5
NEAR_BYTES_PER_US = 50000
FAR_BYTES_PER_US = 25000
KERNEL_US = 5.3
PIECES = 4
STORE_COPIES = 8
VMEM_LIMIT = 20 * 1024 * 1024
NT = (((1,), (1,)), ((), ()))


def left_matrix(left):
    row = lax.broadcasted_iota(jnp.int32, (WIDE, KIN), 0)
    column = lax.broadcasted_iota(jnp.int32, (WIDE, KIN), 1)
    spread = jnp.where((row >> 3) == column, 1.0, 0.0).astype(jnp.bfloat16)
    tall = jnp.dot(spread, left, preferred_element_type=jnp.float32).astype(jnp.bfloat16)
    full = lax.dot_general(tall, spread, NT, preferred_element_type=jnp.float32)
    row = lax.broadcasted_iota(jnp.int32, (WIDE, WIDE), 0)
    column = lax.broadcasted_iota(jnp.int32, (WIDE, WIDE), 1)
    return jnp.where((row & (ROWS - 1)) == (column & (ROWS - 1)), full, 0.0).astype(jnp.bfloat16)


def right_matrix(right):
    zero = jnp.zeros_like(right)
    return jnp.concatenate(
        [jnp.concatenate([right, zero], 1), jnp.concatenate([zero, right], 1)], 0
    )


def side_by_side_to_stacked(block):
    tiles = block.reshape(block.shape[0] // ROWS, ROWS, PAIR)
    return jnp.concatenate([tiles[:, :, :KOUT], tiles[:, :, KOUT:]], 1)


def precondition(rows_ref, both, mixer, half_ref, pre_ref, before):
    rows = rows_ref.shape[0] // PIECES

    def piece(step, carry):
        before(step)
        at = pl.ds(pl.multiple_of(step * rows, rows), rows)
        block = jnp.concatenate(
            [rows_ref[at, p * PAIR : (p + 1) * PAIR] for p in range(KIN // 2)], 0
        )
        half = jnp.dot(block, both, preferred_element_type=jnp.float32)
        groups = pl.ds(step * (rows // ROWS), rows // ROWS)
        for p in range(KIN // 2):
            half_ref[groups, 2 * ROWS * p : 2 * ROWS * (p + 1), :] = side_by_side_to_stacked(
                half[p * rows : (p + 1) * rows]
            ).astype(jnp.bfloat16)
        return carry

    lax.fori_loop(0, PIECES, piece, 0)

    def groups(index, carry):
        stacked = jnp.concatenate([half_ref[2 * index], half_ref[2 * index + 1]], 1)
        mixed = side_by_side_to_stacked(
            jnp.dot(mixer, stacked, preferred_element_type=jnp.float32)
        ).astype(jnp.bfloat16)
        at = pl.ds(pl.multiple_of(index * 2 * ROWS, 2 * ROWS), 2 * ROWS)
        for i in range(KIN):
            pre_ref[at, i * KOUT : (i + 1) * KOUT] = mixed[i]
        return carry

    lax.fori_loop(0, rows_ref.shape[0] // (2 * ROWS), groups, 0, unroll=8)


def copy_of(source_ref, target_ref, sems, step):
    rows = target_ref.shape[0] // sems.shape[0]
    at = pl.ds(pl.multiple_of(step * rows, rows), rows)
    return pltpu.make_async_copy(source_ref.at[at], target_ref.at[at], sems.at[step])


def start_store(store_ref, store_vmem, sems, step):
    share = sems.shape[0] // PIECES
    for k in range(share):
        copy_of(store_ref.at[0], store_vmem, sems, step * share + k).start()


def dots(pre_ref, store_ref, store_vmem, sems, total_ref, out_ref):
    columns = total_ref.shape[0]
    depth = pre_ref.shape[1]
    blocks = store_vmem.shape[0] // columns
    share = sems.shape[0] // blocks

    def block(step, carry):
        for k in range(share):
            copy_of(store_ref.at[0], store_vmem, sems, step * share + k).wait()
        rows = pl.ds(pl.multiple_of(step * columns, columns), columns)
        for at in range(0, depth, DEPTH_BLOCK):
            term = lax.dot_general(
                store_vmem[rows, at : at + DEPTH_BLOCK],
                pre_ref[:, at : at + DEPTH_BLOCK],
                NT,
                preferred_element_type=jnp.float32,
            )
            if at == 0:
                total_ref[...] = term
            elif at + DEPTH_BLOCK < depth:
                total_ref[...] += term
            else:
                out_ref[step] = (total_ref[...] + term).T
        return carry

    lax.fori_loop(0, blocks, block, 0)


def first_kernel(
    rows_ref, left_ref, right_ref, store_ref, out_ref, both_ref, mixer_ref,
    left_vmem, right_vmem, rows_vmem, store_vmem, half_ref, total_ref,
    left_sems, right_sems, rows_sems, store_sems,
):
    right = copy_of(right_ref.at[0], right_vmem, right_sems, 0)
    left = copy_of(left_ref.at[0], left_vmem, left_sems, 0)
    right.start()
    left.start()
    for step in range(PIECES):
        copy_of(rows_ref.at[0], rows_vmem, rows_sems, step).start()
    right.wait()
    both_ref[...] = right_matrix(right_vmem[...])
    left.wait()
    mixer_ref[...] = left_matrix(left_vmem[...])

    def before(step):
        copy_of(rows_ref.at[0], rows_vmem, rows_sems, step).wait()
        start_store(store_ref, store_vmem, store_sems, step)

    precondition(rows_vmem, both_ref[...], mixer_ref[...], half_ref, rows_vmem, before)
    dots(rows_vmem, store_ref, store_vmem, store_sems, total_ref, out_ref)


def later_kernel(
    sent, rows_ref, both_ref, mixer_ref, store_ref, *refs,
):
    out_ref, pre_ref, store_vmem, half_ref, total_ref, store_sems = refs[sent:]

    def before(step):
        start_store(store_ref, store_vmem, store_sems, step)

    precondition(rows_ref.at[0], both_ref[...], mixer_ref[...], half_ref, pre_ref, before)
    dots(pre_ref, store_ref, store_vmem, store_sems, total_ref, out_ref)


VMEM = pl.BlockSpec(memory_space=pltpu.VMEM)
HBM = pl.BlockSpec(memory_space=pltpu.HBM)


def in_hbm(array):
    return pltpu.with_memory_space_constraint(array, pltpu.HBM)


def call(kernel, queries, store, outs, in_specs, scratch, operands):
    count, depth = queries.shape[1:]
    examples = store.shape[1]
    columns = min(COLUMNS, examples)
    scores = jax.ShapeDtypeStruct((examples // columns, count, columns), jnp.float32)
    return pl.pallas_call(
        kernel,
        out_shape=(scores,) + outs,
        in_specs=in_specs,
        out_specs=(VMEM,) * (1 + len(outs)),
        scratch_shapes=scratch,
        compiler_params=pltpu.CompilerParams(vmem_limit_bytes=VMEM_LIMIT),
        cost_estimate=pl.CostEstimate(
            flops=2 * count * depth * (examples + 1024),
            bytes_accessed=2 * depth * (count + examples),
            transcendentals=0,
        ),
    )(*operands)


def buffers(queries, store):
    count, depth = queries.shape[1:]
    examples = store.shape[1]
    return [
        pltpu.VMEM((count, depth), jnp.bfloat16),
        pltpu.VMEM((examples, depth), jnp.bfloat16),
        pltpu.VMEM((count // ROWS, WIDE, KOUT), jnp.bfloat16),
        pltpu.VMEM((min(COLUMNS, examples), count), jnp.float32),
    ]


def first_scores(queries, left_inv, right_inv, store):
    small = [pltpu.VMEM((KIN, KIN), jnp.bfloat16), pltpu.VMEM((KOUT, KOUT), jnp.bfloat16)]
    sems = [pltpu.SemaphoreType.DMA((n,)) for n in (1, 1, PIECES, STORE_COPIES)]
    outs = (
        jax.ShapeDtypeStruct((PAIR, PAIR), jnp.bfloat16),
        jax.ShapeDtypeStruct((WIDE, WIDE), jnp.bfloat16),
    )
    operands = [in_hbm(a) for a in (queries, left_inv, right_inv, store)]
    return call(
        first_kernel, queries, store, outs, [HBM] * 4,
        small + buffers(queries, store) + sems, operands,
    )


def later_scores(queries, both, mixer, store, sent):
    sems = [pltpu.SemaphoreType.DMA((STORE_COPIES,))]
    return call(
        functools.partial(later_kernel, len(sent)), queries, store, (),
        [VMEM] * 3 + [HBM] + [VMEM] * len(sent), buffers(queries, store) + sems,
        [queries, both, mixer, in_hbm(store), *sent],
    )[0]


def swap(block, bit):
    route = [(i, i ^ bit) for i in range(lax.axis_size("layer"))]
    return lax.ppermute(block, "layer", route)


HALVE, EXCHANGE, DOUBLE = range(3)


class LayerSum:
    def __init__(self, block, bits, index, exchanges):
        self.block, self.index, self.sent = block, index, None
        halved, exchanged = bits[:-exchanges], bits[-exchanges:]
        self.moves = [(bit, HALVE) for bit in halved]
        self.moves += [(bit, EXCHANGE) for bit in exchanged]
        self.moves += [(bit, DOUBLE) for bit in reversed(halved)]
        if not halved:
            self.block = block.astype(jnp.bfloat16)

    def send(self, order):
        bit, kind = self.moves[0]
        sent = self.block
        if kind == HALVE:
            rows = self.block.shape[0] // 2
            upper = (self.index & bit) // bit
            sent = lax.dynamic_slice_in_dim(self.block, (1 - upper) * rows, rows, 0)
            sent = sent.astype(jnp.bfloat16)
            self.block = lax.dynamic_slice_in_dim(self.block, upper * rows, rows, 0)
            self.block, sent = lax.optimization_barrier((self.block, sent))
        self.sent = order.mark(sent)
        self.received = swap(self.sent, bit)

    def bytes_of_move(self):
        size = self.block.size
        return size if self.moves[0][1] == HALVE else 2 * size

    def take(self, order):
        bit, kind = self.moves.pop(0)
        received = order.mark(self.received)
        mine = self.block
        if kind == DOUBLE:
            low = (self.index & bit) == 0
            self.block = jnp.concatenate(
                [jnp.where(low, mine, received), jnp.where(low, received, mine)], 0
            )
            return
        self.block = mine.astype(jnp.float32) + received.astype(jnp.float32)
        if not (self.moves and self.moves[0][1] == HALVE):
            self.block = self.block.astype(jnp.bfloat16)


class Order:
    def __init__(self):
        self.last = jnp.zeros((), jnp.float32)

    def after(self, value):
        value, _ = lax.optimization_barrier((value, self.last))
        return value

    def mark(self, value):
        value, self.last = lax.optimization_barrier((value, self.last))
        return value


class Clock:
    def __init__(self):
        self.now = 0.0
        self.links = {}
        self.arrivals = {}

    def send(self, chunk):
        bit, _ = chunk.moves[0]
        far = bit > 2
        self.now += FAR_START_US if far else NEAR_START_US
        begin = max(self.now, self.links.get(bit, 0.0))
        end = begin + chunk.bytes_of_move() / (FAR_BYTES_PER_US if far else NEAR_BYTES_PER_US)
        self.links[bit] = end
        self.arrivals[chunk] = end + (2 * LATENCY_US if far else LATENCY_US)

    def next(self):
        there = [chunk for chunk, at in self.arrivals.items() if at <= self.now]
        return there[-1] if there else min(self.arrivals, key=self.arrivals.get)

    def take(self, chunk):
        self.now = max(self.now, self.arrivals.pop(chunk))


def send(chunk, order, clock):
    if chunk.moves:
        clock.send(chunk)
        chunk.send(order)


def shards(store, queries, left_inv, right_inv, query_prompt, winner):
    rows = queries.shape[1]
    columns = store.shape[1]
    ex_count = lax.axis_size("ex")
    position = lax.axis_index("ex")
    count = lax.axis_size("layer")
    index = lax.axis_index("layer")
    bits = [1 << k for k in range(count.bit_length() - 1)]
    orders = [bits, bits[1:2] + bits[:1] + bits[2:]]
    order, clock = Order(), Clock()
    chunks, places = [], []
    current = queries
    for step in range(ex_count):
        if step == 0:
            part, both, mixer = first_scores(queries, left_inv, right_inv, store)
        else:
            route = [((i - 1) % ex_count, i) for i in range(ex_count)]
            current = lax.ppermute(current, "ex", route)
            sent = [chunk.sent for chunk in chunks if chunk.moves]
            part = order.mark(later_scores(order.after(current), both, mixer, store, sent))
            clock.now += KERNEL_US
            for chunk in chunks:
                clock.take(chunk)
                chunk.take(order)
                send(chunk, order, clock)
        choices = ORDERS[min(step, len(ORDERS) - 1)]
        width = part.shape[2]
        for number, (choice, exchanges) in enumerate(choices):
            first = number * width
            chunk = LayerSum(part[number], orders[choice], index, exchanges)
            send(chunk, order, clock)
            chunks.append(chunk)
            places.append(((position - step) % ex_count * rows, jnp.int32(first)))
    while clock.arrivals:
        chunk = clock.next()
        clock.take(chunk)
        chunk.take(order)
        send(chunk, order, clock)
    done = [chunk.block for chunk in chunks]
    scores = jnp.zeros((rows * ex_count, columns), jnp.bfloat16)
    for place, block in zip(places, done):
        scores = lax.dynamic_update_slice(scores, block, place)
    ids = jnp.arange(scores.shape[0], dtype=jnp.int32)
    prompts = jnp.arange(winner.shape[0], dtype=jnp.int32)
    picks = (winner[:, None] == ids[None, :]).astype(jnp.float32)
    member = (query_prompt[None, :] == prompts[:, None]).astype(jnp.float32)
    weights = (picks - member / BEST).astype(jnp.bfloat16)
    advantage = jnp.dot(weights, scores, preferred_element_type=jnp.float32)
    return (scores, advantage.astype(jnp.bfloat16))


def solution(mesh):
    return jax.shard_map(
        shards,
        mesh=mesh,
        in_specs=(
            P("layer", ("grp", "ex"), None),
            P("layer", ("grp", "ex"), None),
            P("layer", None, None),
            P("layer", None, None),
            P("grp"),
            P("grp"),
        ),
        out_specs=(P(None, ("grp", "ex")), P(None, ("grp", "ex"))),
        check_vma=False,
    )
```
